32 devices in a mesh: narrow: 4 (over x, core), wide: 8 (over z, y).
Axes of the slice: x: 2, y: 2, z: 4, core: 2. Of those that a mesh axis runs over, the one named last changes fastest.
Arguments:
- tokens: bfloat16 [32768, 512], P(('narrow', 'wide')), may hold values from -6 to 6
- memory: bfloat16 [32768, 512], P(('narrow', 'wide')), may hold values from -6 to 6
- target_segments: int32 [32768], P(('narrow', 'wide')), may hold values from 0 to 31, as said below
- memory_segments: int32 [32768], P(('narrow', 'wide')), may hold values from 0 to 31, as said below
- self_qkv: bfloat16 [512, 1536], P('wide'), may hold values from -0.25 to 0.25
- self_out: bfloat16 [512, 512], P('wide'), may hold values from -0.75 to 0.75
- cross_q: bfloat16 [512, 512], P('wide'), may hold values from -0.25 to 0.25
- cross_kv: bfloat16 [512, 1024], P('wide'), may hold values from -0.25 to 0.25
- cross_out: bfloat16 [512, 512], P('wide'), may hold values from -0.75 to 0.75
- ffn_in: bfloat16 [512, 2048], P('wide'), may hold values from -0.25 to 0.25
- ffn_out: bfloat16 [2048, 512], P('wide'), may hold values from -0.125 to 0.125
- norm_gain: bfloat16 [512, 3], P('wide'), may hold values from 0.5 to 1.5
- norm_bias: bfloat16 [512, 3], P('wide'), may hold values from -3 to 3
- omega: bfloat16 [512, 3], P('wide'), may hold values from 0.5 to 2
- cotangent: bfloat16 [32768, 512], P(('narrow', 'wide')), may hold values from -6 to 6
Outputs:
- out: bfloat16 [32768, 512], P(('narrow', 'wide'))
- grad_tokens: float32 [32768, 512], P(('narrow', 'wide'))
- grad_memory: float32 [32768, 512], P(('narrow', 'wide'))
- grad_self_qkv: float32 [512, 1536], P('wide')
- grad_self_out: float32 [512, 512], P('wide')
- grad_cross_q: float32 [512, 512], P('wide')
- grad_cross_kv: float32 [512, 1024], P('wide')
- grad_cross_out: float32 [512, 512], P('wide')
- grad_ffn_in: float32 [512, 2048], P('wide')
- grad_ffn_out: float32 [2048, 512], P('wide')
- grad_norm_gain: float32 [512, 3], P('wide')
- grad_norm_bias: float32 [512, 3], P('wide')
- grad_omega: float32 [512, 3], P('wide')
The draws below stay inside these ranges and needn't reach their ends.
Inputs may be any that keep to these rules, and one draw needn't show every extreme that they name: `target_segments`: within each row of 1024 target tokens the numbers never fall, start at 0 and take every value 0 to 31. `memory_segments`: within each row of 1024 memory tokens the numbers never fall, start at 0 and take every value 0 to 31, so every target sentence has memory of its own number in the matching row.
All inputs are finite; a program needn't handle non-finite values.
Results may differ from the reference program's by a relative error of at most 0.02.
Values may be sent and summed in bfloat16 or wider, within the bound.
A program may use at most 320 MiB of HBM per device.

```python
import math
import jax
import jax.numpy as jnp
from jax import lax

D = 512
HEADS = 8
HD = 64
FF = 2048
SEQ = 1024
MEM = 1024
SEGS = 32
TOKENS = 32768
MEMS = 32768


def segment_numbers(key, length, count, rows):

    def one_row(row_key):
        cuts = jax.random.permutation(row_key, length - 1)[:count - 1] + 1
        places = jnp.arange(length)
        return jnp.sum((cuts[None, :] <= places[:, None]).astype(jnp.int32), axis=1).astype(jnp.int32)
    row_keys = jax.random.split(key, rows)
    return jax.vmap(one_row)(row_keys).reshape(rows * length)


def draw_target_segments(key, part):
    key = jax.random.fold_in(key, 11)
    return segment_numbers(key, SEQ, SEGS, TOKENS // SEQ)


def draw_memory_segments(key, part):
    key = jax.random.fold_in(key, 23)
    return segment_numbers(key, MEM, SEGS, MEMS // MEM)


def spiked(entries, own_key, source, target, shards_of, factor):
    def block_of(dim):
        return (jnp.arange(entries.shape[dim]) // (entries.shape[dim] // shards_of)).reshape((-1,) + (1,) * (entries.ndim - 1 - dim))

    one_side = jax.random.permutation(own_key, shards_of)[block_of(target)]
    second = (block_of(target) + shards_of // 2) % shards_of
    return jnp.where((block_of(source) == one_side) | (block_of(source) == second), factor * entries, entries)


def levels(stream_key, extent, pieces, least, top_value):
    def one(axis_at, shards_of):
        draws = jax.random.uniform(jax.random.fold_in(jax.random.fold_in(stream_key, 6), axis_at), (shards_of,), jnp.float32, least / len(pieces), top_value / len(pieces))
        return jnp.repeat(jnp.exp(draws), extent[axis_at] // shards_of).reshape((-1,) + (1,) * (len(extent) - axis_at - 1))

    level = one(*pieces[0])
    for cut in pieces[1:]:
        level = level * one(*cut)
    return level


def bell_draw(stream_key, dims, scale, most, pieces=(), dtype=jnp.bfloat16):
    values = jax.random.normal(stream_key, dims, jnp.float32) * scale
    if len(pieces) > 0:
        values = levels(stream_key, dims, pieces, -0.22, 0.18) * values
    return jnp.clip(values, min=-most, max=most).astype(dtype)


def heavy_noise(key, dims, scale, reach, cuts, heavy, held_as=jnp.bfloat16):
    array = scale * jax.random.normal(key, dims, jnp.float32)
    if cuts:
        array = array * levels(key, dims, cuts, -0.22, 0.18)
    return jnp.clip(spiked(array, jax.random.fold_in(key, 3), *heavy), -reach, reach).astype(held_as)


def setup_inputs(seed: int = 0) -> dict:
    key_of = jax.random.split(jax.random.key(seed), 16)
    tokens = heavy_noise(key_of[0], (TOKENS, D), 1.0, 6.0, ((0, 32),), (0, 1, 32, 2.75))
    memory = bell_draw(key_of[1], (MEMS, D), 1.0, 6.0, ((0, 32),))
    target_segments = draw_target_segments(jax.random.fold_in(key_of[15], 71), 0)
    memory_segments = draw_memory_segments(jax.random.fold_in(key_of[15], 71), 0)
    self_qkv = bell_draw(key_of[4], (D, 3 * D), D ** -0.5, 0.25, ((0, 8),))
    self_out = bell_draw(key_of[5], (D, D), (D // 8) ** -0.5, 0.75, ((0, 8),))
    cross_q = bell_draw(key_of[6], (D, D), D ** -0.5, 0.25, ((0, 8),))
    cross_kv = bell_draw(key_of[7], (D, 2 * D), D ** -0.5, 0.25, ((0, 8),))
    cross_out = bell_draw(key_of[8], (D, D), (D // 8) ** -0.5, 0.75, ((0, 8),))
    ffn_in = bell_draw(key_of[9], (D, FF), D ** -0.5, 0.25, ((0, 8),))
    ffn_out = bell_draw(key_of[10], (FF, D), FF ** -0.5, 0.125, ((0, 8),))
    norm_gain = jnp.clip(1.0 + 0.1 * jax.random.normal(key_of[11], (D, 3), jnp.float32), 0.5, 1.5).astype(jnp.bfloat16)
    norm_bias = bell_draw(key_of[12], (D, 3), 0.5, 3.0, ((0, 8),))
    omega = jnp.clip(jnp.exp(math.log(2.0) - 1.3862944 * jax.random.uniform(key_of[13], (D, 3), jnp.float32) ** levels(key_of[13], (D, 3), ((0, 8),), -0.2, 0.2)), 0.5, 2.0).astype(jnp.bfloat16)
    cotangent = bell_draw(key_of[14], (TOKENS, D), 1.0, 6.0, ((0, 32),))
    return dict(tokens=tokens, memory=memory, target_segments=target_segments, memory_segments=memory_segments, self_qkv=self_qkv, self_out=self_out, cross_q=cross_q, cross_kv=cross_kv, cross_out=cross_out, ffn_in=ffn_in, ffn_out=ffn_out, norm_gain=norm_gain, norm_bias=norm_bias, omega=omega, cotangent=cotangent)


@jax.custom_vjp
def low(v):
    return lax.optimization_barrier(v.astype(jnp.bfloat16)).astype(jnp.float32)

@jax.custom_vjp
def low_back(v):
    return v

def low_keep(v):
    return (low(v), None)

def low_pass(kept, grad):
    return (grad,)

def back_keep(v):
    return (v, None)

def back_low(kept, grad):
    return (low(grad),)
low.defvjp(low_keep, low_pass)
low_back.defvjp(back_keep, back_low)
EPSILON = 1e-05
NEGATIVE = -1000000000.0
HIGH = lax.Precision.HIGHEST

def norm_apply(resid, gain, shift):
    middle = lax.optimization_barrier(jnp.mean(resid, axis=-1, keepdims=True))
    centred = resid - middle
    spread = lax.optimization_barrier(jnp.mean(centred * centred, axis=-1, keepdims=True))
    return centred * lax.rsqrt(spread + EPSILON) * gain + shift

def attend(query, keys, values, allowed):
    rows, length = (query.shape[0], query.shape[1])
    width = keys.shape[1]
    query_heads = query.reshape(rows, length, HEADS, HD)
    key_heads = keys.reshape(rows, width, HEADS, HD)
    value_heads = values.reshape(rows, width, HEADS, HD)
    scores = jnp.einsum('rqhd,rkhd->rhqk', query_heads, key_heads, precision=HIGH) * HD ** (-0.5)
    scores = low_back(jnp.where(allowed[:, None], scores, NEGATIVE))
    probs = low(jax.nn.softmax(scores, axis=-1))
    mixed = jnp.einsum('rhqk,rkhd->rqhd', probs, value_heads, precision=HIGH)
    return low(low_back(mixed.reshape(rows * length, HEADS * HD)))

def layer_group(weights, item):
    w_qkv, w_out, w_cq, w_ckv, w_co, w_in, w_down, gains, shifts, omegas = weights
    inputs, context, target_ids, memory_ids = item
    rows = inputs.shape[0] // SEQ
    target_rows = target_ids.reshape(rows, SEQ)
    memory_rows = memory_ids.reshape(rows, MEM)
    places = jnp.arange(SEQ)
    own_ok = (target_rows[:, :, None] == target_rows[:, None, :]) & (places[None, None, :] <= places[None, :, None])
    far_ok = target_rows[:, :, None] == memory_rows[:, None, :]
    qkv = low(low_back(jnp.dot(inputs, w_qkv, precision=HIGH)))
    query = qkv[:, :D].reshape(rows, SEQ, D)
    keys = qkv[:, D:2 * D].reshape(rows, SEQ, D)
    values = qkv[:, 2 * D:].reshape(rows, SEQ, D)
    mixed_one = attend(query, keys, values, own_ok)
    branch_one = low_back(jnp.dot(mixed_one, w_out, precision=HIGH))
    hidden_one = norm_apply(inputs * omegas[:, 0] + branch_one, gains[:, 0], shifts[:, 0])
    hidden_one_low = low(hidden_one)
    cross_query = low(low_back(jnp.dot(hidden_one_low, w_cq, precision=HIGH)))
    cross_pairs = low(low_back(jnp.dot(context, w_ckv, precision=HIGH)))
    mixed_two = attend(cross_query.reshape(rows, SEQ, D), cross_pairs[:, :D].reshape(rows, MEM, D), cross_pairs[:, D:].reshape(rows, MEM, D), far_ok)
    branch_two = low_back(jnp.dot(mixed_two, w_co, precision=HIGH))
    hidden_two = norm_apply(hidden_one * omegas[:, 1] + branch_two, gains[:, 1], shifts[:, 1])
    hidden_two_low = low(hidden_two)
    inner = low_back(jnp.dot(hidden_two_low, w_in, precision=HIGH))
    active = low(jax.nn.gelu(inner, approximate=False))
    branch_three = low_back(jnp.dot(active, w_down, precision=HIGH))
    return norm_apply(hidden_two * omegas[:, 2] + branch_three, gains[:, 2], shifts[:, 2])

def reference(tokens, memory, target_segments, memory_segments, self_qkv, self_out, cross_q, cross_kv, cross_out, ffn_in, ffn_out, norm_gain, norm_bias, omega, cotangent):
    params = tuple((entry.astype(jnp.float32) for entry in (self_qkv, self_out, cross_q, cross_kv, cross_out, ffn_in, ffn_out, norm_gain, norm_bias, omega)))
    groups = tokens.shape[0] // (4 * SEQ)
    target_parts = target_segments.reshape(groups, 4 * SEQ)
    memory_parts = memory_segments.reshape(groups, 4 * MEM)
    stepper = jax.checkpoint(layer_group)

    def whole(inputs, context, weights):
        items = (inputs.reshape(groups, 4 * SEQ, D), context.reshape(groups, 4 * MEM, D), target_parts, memory_parts)
        results = lax.map(lambda entry: stepper(weights, entry), items)
        return results.reshape(groups * 4 * SEQ, D)
    result, pullback = jax.vjp(whole, tokens.astype(jnp.float32), memory.astype(jnp.float32), params)
    grad_tokens, grad_memory, grads = pullback(cotangent.astype(jnp.float32))
    return (result.astype(jnp.bfloat16), grad_tokens, grad_memory, grads[0], grads[1], grads[2], grads[3], grads[4], grads[5], grads[6], grads[7], grads[8], grads[9])
```

```python
import functools
import math

import jax
import jax.numpy as jnp
from jax import lax
from jax.experimental import pallas as pl
from jax.experimental.pallas import tpu as pltpu
from jax.sharding import PartitionSpec as P

HD = 64

EPSILON = 1e-05
NEGATIVE = -1000000000.0


def flip_pairs(mesh, axis, step):
    narrow, wide = mesh.shape["narrow"], mesh.shape["wide"]
    pairs = []
    for n in range(narrow):
        for w in range(wide):
            there = (n ^ step, w) if axis == "narrow" else (n, w ^ step)
            pairs.append((n * wide + w, there[0] * wide + there[1]))
    return pairs


def swap(mesh, value, axis, step):
    return lax.ppermute(value, ("narrow", "wide"), flip_pairs(mesh, axis, step))


def wide_groups(mesh):
    bits = mesh.shape["wide"].bit_length() - 1
    first = [(0, 1)] if bits % 2 else []
    return first + [(low, 2) for low in range(bits % 2, bits, 2)]


def part_of(value, index, count, dim):
    size = value.shape[dim] // count
    return lax.dynamic_slice_in_dim(value, index * size, size, dim)


def gather_group(mesh, group, order):
    n = lax.axis_index("narrow")
    w = lax.axis_index("wide")
    wide = mesh.shape["wide"]
    core, x = n % 2, n // 2
    held = part_of(group, core * 2 + x, 4, 1)[None]
    places = [w]

    def widen(held, places, low, count):
        arrived = [held]
        spots = list(places)
        for d in range(1, 2**count):
            arrived.append(swap(mesh, held, "wide", d << low))
            spots += [p ^ (d << low) for p in places]
        return jnp.concatenate(arrived, 0), spots

    def join_x(held):
        other = swap(mesh, held, "narrow", 2)
        pair = jnp.stack([jnp.where(x == 0, held, other), jnp.where(x == 0, other, held)], 2)
        return pair

    groups = wide_groups(mesh)[::-1]
    for at, (low, count) in enumerate(groups):
        if order == "zxy" and at == len(groups) - 1:
            held = join_x(held)
        held, places = widen(held, places, low, count)
    if order != "zxy":
        held = join_x(held)
    other = swap(mesh, held, "narrow", 1)
    both = jnp.stack([jnp.where(core == 0, held, other), jnp.where(core == 0, other, held)], 2)
    both = both.reshape(wide, group.shape[0], group.shape[1])
    out = jnp.zeros_like(both)
    for k, place in enumerate(places):
        out = lax.dynamic_update_slice_in_dim(out, both[k : k + 1], place, 0)
    return out


def reduce_grad(mesh, grad, order):
    n = lax.axis_index("narrow")
    w = lax.axis_index("wide")
    wide = mesh.shape["wide"]
    core, x = n % 2, n // 2
    columns = grad.shape[1]
    held = grad.astype(jnp.bfloat16).reshape(wide, grad.shape[0] // wide, columns)

    def halve(held, index, step):
        sent = swap(mesh, part_of(held, 1 - index, 2, 2), "narrow", step)
        total = part_of(held, index, 2, 2).astype(jnp.float32) + sent.astype(jnp.float32)
        return total.astype(jnp.bfloat16)

    def scatter(held, low, count):
        members = 2**count
        step = (w >> low) % members
        rest = held.shape[0] // members
        shape = held.shape
        view = held.reshape((rest, members) + shape[1:])
        total = part_of(view, step, members, 1).astype(jnp.float32)
        for d in range(1, members):
            got = swap(mesh, part_of(view, step ^ d, members, 1), "wide", d << low)
            total = total + got.astype(jnp.float32)
        return total.astype(jnp.bfloat16).reshape((rest,) + shape[1:])

    held = halve(held, core, 1)
    groups = wide_groups(mesh)
    if order == "xyz":
        held = halve(held, x, 2)
        for low, count in groups:
            held = scatter(held, low, count)
    else:
        for at, (low, count) in enumerate(groups):
            held = scatter(held, low, count)
            if at == 0:
                held = halve(held, x, 2)
    held = held[0]
    other = swap(mesh, held, "narrow", 2)
    held = jnp.concatenate([jnp.where(x == 0, held, other), jnp.where(x == 0, other, held)], 1)
    other = swap(mesh, held, "narrow", 1)
    held = jnp.concatenate([jnp.where(core == 0, held, other), jnp.where(core == 0, other, held)], 1)
    return held.astype(jnp.float32)


BF = jnp.bfloat16
F32 = jnp.float32
QB = 64
WIN = 256
GROUP = 256
SIDE = GROUP // HD
VMEM_BYTES = 56 * 2**20


def dot(left, right):
    return lax.dot_general(left, right, (((1,), (0,)), ((), ())), preferred_element_type=F32)


def dot_nt(left, right):
    return lax.dot_general(left, right, (((1,), (1,)), ((), ())), preferred_element_type=F32)


def dot_tn(left, right):
    return lax.dot_general(left, right, (((0,), (0,)), ((), ())), preferred_element_type=F32)


def norm_parts(resid):
    middle = jnp.mean(resid, axis=-1, keepdims=True)
    centred = resid - middle
    spread = jnp.mean(centred * centred, axis=-1, keepdims=True)
    scale = lax.rsqrt(spread + EPSILON)
    return centred * scale, scale


def norm_back(grad, normal, scale, gain):
    scaled = grad * gain
    middle = jnp.mean(scaled, axis=-1, keepdims=True)
    along = jnp.mean(scaled * normal, axis=-1, keepdims=True)
    return (scaled - middle - normal * along) * scale


def down_sum(value):
    return jnp.sum(value, axis=0, keepdims=True)


def head_masks(scale):
    rows = lax.broadcasted_iota(jnp.int32, (SIDE * QB, GROUP), 0) // QB
    lanes = lax.broadcasted_iota(jnp.int32, (SIDE * QB, GROUP), 1) // HD
    return jnp.where(rows == lanes, scale, 0.0).astype(BF)


def pick_heads(stacked):
    lanes = lax.broadcasted_iota(jnp.int32, (QB, GROUP), 1) // HD
    out = stacked[:QB]
    for h in range(1, SIDE):
        out = jnp.where(lanes == h, stacked[h * QB : (h + 1) * QB], out)
    return out


def stack_heads(block, mask):
    return jnp.concatenate([block] * SIDE, axis=0) * mask


def window(first, step, length):
    begin = first + step * WIN
    start = pl.multiple_of(jnp.minimum(begin, length - WIN), 16)
    return begin, start


def attend_fwd(q_ref, q_at, k_ref, k_at, v_at, lo_s, hi_s, lohi_ref, o_ref):
    length = k_ref.shape[0]
    mask = head_masks(HD**-0.5)

    def one(b, carry):
        q0 = pl.multiple_of(b * QB, QB)
        first = (lo_s[q0] // 16) * 16
        last = hi_s[q0 + QB - 1]
        low = lohi_ref[pl.ds(q0, QB), 0:1]
        high = lohi_ref[pl.ds(q0, QB), 1:2]

        def scores(g, begin, start):
            places = start + lax.broadcasted_iota(jnp.int32, (QB, WIN), 1)
            ok = (places >= jnp.maximum(low, begin)) & (places <= high)
            ok = jnp.concatenate([ok] * SIDE, axis=0)
            query = stack_heads(q_ref[pl.ds(q0, QB), pl.ds(q_at + g * GROUP, GROUP)], mask)
            keys = k_ref[pl.ds(start, WIN), pl.ds(k_at + g * GROUP, GROUP)]
            return jnp.where(ok, dot_nt(query, keys), NEGATIVE)

        def values(g, start):
            return k_ref[pl.ds(start, WIN), pl.ds(v_at + g * GROUP, GROUP)]

        def store(g, stacked):
            o_ref[pl.ds(q0, QB), pl.ds(g * GROUP, GROUP)] = pick_heads(stacked).astype(BF)

        @pl.when(last - first < WIN)
        def _():
            begin, start = window(first, 0, length)
            for g in range(2):
                score = scores(g, begin, start)
                top = jnp.max(score, axis=-1, keepdims=True)
                raised = jnp.exp(score - top)
                total = jnp.sum(raised, axis=-1, keepdims=True)
                weights = (raised * (1.0 / total)).astype(BF)
                store(g, dot(weights, values(g, start)))

        @pl.when(last - first >= WIN)
        def _():
            count = (last - first) // WIN + 1
            for g in range(2):

                def stats(k, state):
                    top, total = state
                    begin, start = window(first, k, length)
                    score = scores(g, begin, start)
                    higher = jnp.maximum(top, jnp.max(score, axis=-1, keepdims=True))
                    raised = jnp.sum(jnp.exp(score - higher), axis=-1, keepdims=True)
                    return higher, total * jnp.exp(top - higher) + raised

                start_top = jnp.full((SIDE * QB, 1), 2 * NEGATIVE, F32)
                top, total = lax.fori_loop(0, count, stats, (start_top, jnp.zeros((SIDE * QB, 1), F32)))

                def mix(k, out):
                    begin, start = window(first, k, length)
                    weights = jnp.exp(scores(g, begin, start) - top) * (1.0 / total)
                    return out + dot(weights.astype(BF), values(g, start))

                store(g, lax.fori_loop(0, count, mix, jnp.zeros((SIDE * QB, GROUP), F32)))

        return carry

    lax.fori_loop(0, q_ref.shape[0] // QB, one, 0)


def attend_bwd(q_ref, q_at, k_ref, k_at, v_at, do_ref, lo_s, hi_s, lo_rows, hi_rows, dq_ref, dq_at, dk_acc, dv_acc):
    length = k_ref.shape[0]
    factor = HD**-0.5
    q_mask = head_masks(factor)
    do_mask = head_masks(1.0)
    dk_acc[...] = jnp.zeros_like(dk_acc)
    dv_acc[...] = jnp.zeros_like(dv_acc)

    def one(b, carry):
        q0 = pl.multiple_of(b * QB, QB)
        first = (lo_s[q0] // 16) * 16
        last = hi_s[q0 + QB - 1]
        low = lo_rows[pl.ds(b, 1), :]
        high = hi_rows[pl.ds(b, 1), :]

        def keys(g, start):
            return k_ref[pl.ds(start, WIN), pl.ds(k_at + g * GROUP, GROUP)]

        def values(g, start):
            return k_ref[pl.ds(start, WIN), pl.ds(v_at + g * GROUP, GROUP)]

        def query(g):
            return stack_heads(q_ref[pl.ds(q0, QB), pl.ds(q_at + g * GROUP, GROUP)], q_mask)

        def grad(g):
            return stack_heads(do_ref[pl.ds(q0, QB), pl.ds(g * GROUP, GROUP)], do_mask)

        def scores(g, begin, start):
            places = start + lax.broadcasted_iota(jnp.int32, (WIN, SIDE * QB), 0)
            ok = (places >= jnp.maximum(low, begin)) & (places <= high)
            return jnp.where(ok, dot_nt(keys(g, start), query(g)), NEGATIVE)

        def spread(g, start, probs, slopes, middle):
            delta = (probs * (slopes - middle)).astype(BF)
            rows = pl.ds(start, WIN)
            lanes = pl.ds(g * GROUP, GROUP)
            dv_acc[rows, lanes] += dot(probs.astype(BF), grad(g))
            dk_acc[rows, lanes] += dot(delta, query(g))
            return dot_tn(delta, keys(g, start))

        def store(g, stacked):
            dq = pick_heads(stacked) * factor
            dq_ref[pl.ds(q0, QB), pl.ds(dq_at + g * GROUP, GROUP)] = dq.astype(BF)

        @pl.when(last - first < WIN)
        def _():
            begin, start = window(first, 0, length)
            for g in range(2):
                score = scores(g, begin, start)
                slopes = dot_nt(values(g, start), grad(g))
                raised = jnp.exp(score - jnp.max(score, axis=0, keepdims=True))
                probs = raised * (1.0 / down_sum(raised))
                store(g, spread(g, start, probs, slopes, down_sum(probs * slopes)))

        @pl.when(last - first >= WIN)
        def _():
            count = (last - first) // WIN + 1
            for g in range(2):

                def stats(k, state):
                    top, total = state
                    begin, start = window(first, k, length)
                    score = scores(g, begin, start)
                    higher = jnp.maximum(top, jnp.max(score, axis=0, keepdims=True))
                    return higher, total * jnp.exp(top - higher) + down_sum(jnp.exp(score - higher))

                start_top = jnp.full((1, SIDE * QB), 2 * NEGATIVE, F32)
                top, total = lax.fori_loop(0, count, stats, (start_top, jnp.zeros((1, SIDE * QB), F32)))

                def probs_of(k):
                    begin, start = window(first, k, length)
                    probs = jnp.exp(scores(g, begin, start) - top) * (1.0 / total)
                    return start, probs, dot_nt(values(g, start), grad(g))

                def centre(k, middle):
                    _, probs, slopes = probs_of(k)
                    return middle + down_sum(probs * slopes)

                middle = lax.fori_loop(0, count, centre, jnp.zeros((1, SIDE * QB), F32))

                def last_pass(k, out):
                    start, probs, slopes = probs_of(k)
                    return out + spread(g, start, probs, slopes, middle)

                store(g, lax.fori_loop(0, count, last_pass, jnp.zeros((SIDE * QB, GROUP), F32)))

        return carry

    lax.fori_loop(0, q_ref.shape[0] // QB, one, 0)


def over_tiles(count, size, step):
    def one(t, carry):
        step(pl.multiple_of(t * size, size))
        return carry

    lax.fori_loop(0, count, one, 0)


def self_forward(lo_s, hi_s, tok_ref, w_ref, lohi_ref, qkv_ref, o_ref):
    def project(at):
        qkv_ref[:, pl.ds(at, 256)] = dot(tok_ref[...], w_ref[:, pl.ds(at, 256)]).astype(BF)

    over_tiles(w_ref.shape[1] // 256, 256, project)
    width = o_ref.shape[1]
    attend_fwd(qkv_ref, 0, qkv_ref, width, 2 * width, lo_s, hi_s, lohi_ref, o_ref)


def cross_forward(
    lo_s, hi_s, tok_ref, mem_ref, o1_ref, w_out, w_cq, w_ckv, par, lohi_ref, r1_ref, cq_ref, ckv_ref, o2_ref
):
    tokens = tok_ref.shape[0]

    def pairs(at):
        ckv_ref[:, pl.ds(at, 256)] = dot(mem_ref[...], w_ckv[:, pl.ds(at, 256)]).astype(BF)

    over_tiles(w_ckv.shape[1] // 256, 256, pairs)
    for t in range(tokens // 256):
        rows = pl.ds(t * 256, 256)
        resid = tok_ref[rows, :].astype(F32) * par[6:7, :] + dot(o1_ref[rows, :], w_out[...])
        r1_ref[rows, :] = resid
        normal, _ = norm_parts(resid)
        hidden = (normal * par[0:1, :] + par[3:4, :]).astype(BF)
        cq_ref[rows, :] = dot(hidden, w_cq[...]).astype(BF)
    attend_fwd(cq_ref, 0, ckv_ref, 0, cq_ref.shape[1], lo_s, hi_s, lohi_ref, o2_ref)


def gelu_parts(value):
    area = 0.5 * (1.0 + lax.erf(value * (0.5**0.5)))
    bell = jnp.exp(-0.5 * value * value) * 0.3989422804014327
    return value * area, area + value * bell


def ffn_both(
    r1_ref, o2_ref, cot_ref, w_co, w_in, w_down, par,
    out_ref, dr2_ref, do2_ref, g_in, g_down, g_co, vec_ref,
    r2_ref, h2_ref, z_ref, gp_ref, du_ref, dr3_ref, df_ref, da_ref,
):
    tokens, width = r1_ref.shape
    wide = w_in.shape[1]

    def resid_two(t):
        rows = pl.ds(t * 256, 256)
        hidden = norm_parts(r1_ref[rows, :])[0] * par[0:1, :] + par[3:4, :]
        resid = hidden * par[7:8, :] + dot(o2_ref[rows, :], w_co[...])
        r2_ref[rows, :] = resid
        h2_ref[rows, :] = (norm_parts(resid)[0] * par[1:2, :] + par[4:5, :]).astype(BF)

    for t in range(tokens // 256):
        resid_two(t)

    def up(at):
        lanes = pl.ds(at, 256)
        active, slope = gelu_parts(dot(h2_ref[...], w_in[:, lanes]))
        z_ref[:, lanes] = active.astype(BF)
        gp_ref[:, lanes] = slope

    over_tiles(wide // 256, 256, up)
    vec = [jnp.zeros((1, width), F32) for _ in range(6)]
    for t in range(tokens // 256):
        rows = pl.ds(t * 256, 256)
        hidden = norm_parts(r2_ref[rows, :])[0] * par[1:2, :] + par[4:5, :]
        resid = hidden * par[8:9, :] + dot(z_ref[rows, :], w_down[...])
        normal, scale = norm_parts(resid)
        out_ref[rows, :] = (normal * par[2:3, :] + par[5:6, :]).astype(BF)
        grad = cot_ref[rows, :].astype(F32)
        vec[0] += down_sum(grad * normal)
        vec[1] += down_sum(grad)
        back = norm_back(grad, normal, scale, par[2:3, :])
        vec[2] += down_sum(hidden * back)
        dr3_ref[rows, :] = back
        df_ref[rows, :] = back.astype(BF)

    def down(at):
        lanes = pl.ds(at, 256)
        grad = dot_nt(df_ref[...], w_down[pl.ds(at, 256), :])
        du_ref[:, lanes] = (grad * gp_ref[:, lanes]).astype(BF)

    over_tiles(wide // 256, 256, down)
    for t in range(tokens // 256):
        rows = pl.ds(t * 256, 256)
        grad = dr3_ref[rows, :] * par[8:9, :] + dot_nt(du_ref[rows, :], w_in[...])
        normal, scale = norm_parts(r2_ref[rows, :])
        vec[3] += down_sum(grad * normal)
        vec[4] += down_sum(grad)
        back = norm_back(grad, normal, scale, par[1:2, :])
        hidden = norm_parts(r1_ref[rows, :])[0] * par[0:1, :] + par[3:4, :]
        vec[5] += down_sum(hidden * back)
        dr2_ref[rows, :] = back
        low = back.astype(BF)
        da_ref[rows, :] = low
        do2_ref[rows, :] = dot_nt(low, w_co[...]).astype(BF)
    for k in range(6):
        vec_ref[k : k + 1, :] = vec[k]

    def grad_up(at):
        lanes = pl.ds(at, 256)
        g_in[:, lanes] = dot_tn(h2_ref[...], du_ref[:, lanes]).astype(BF)
        g_down[pl.ds(at, 256), :] = dot_tn(z_ref[:, lanes], df_ref[...]).astype(BF)

    over_tiles(wide // 256, 256, grad_up)

    def grad_co(at):
        lanes = pl.ds(at, 256)
        g_co[:, lanes] = dot_tn(o2_ref[...], da_ref[:, lanes]).astype(BF)

    over_tiles(width // 256, 256, grad_co)


def cross_backward(
    lo_s, hi_s, cq_ref, ckv_ref, do2_ref, lo_rows, hi_rows, mem_ref, tok_ref, r1_ref, dr2_ref, o1_ref, w_cq, w_out, par,
    dckv_ref, dr1_ref, do1_ref, g_cross, g_out, vec_ref,
    dq_ref, dk_acc, dv_acc, h1_ref, da_ref,
):
    tokens, width = r1_ref.shape
    attend_bwd(
        cq_ref, 0, ckv_ref, 0, width, do2_ref, lo_s, hi_s, lo_rows, hi_rows, dq_ref, 0, dk_acc, dv_acc
    )
    dckv_ref[:, :width] = dk_acc[...].astype(BF)
    dckv_ref[:, width:] = dv_acc[...].astype(BF)
    vec = [jnp.zeros((1, width), F32) for _ in range(3)]
    for t in range(tokens // 256):
        rows = pl.ds(t * 256, 256)
        grad = dr2_ref[rows, :] * par[7:8, :] + dot_nt(dq_ref[rows, :], w_cq[...])
        normal, scale = norm_parts(r1_ref[rows, :])
        h1_ref[rows, :] = (normal * par[0:1, :] + par[3:4, :]).astype(BF)
        vec[0] += down_sum(grad * normal)
        vec[1] += down_sum(grad)
        back = norm_back(grad, normal, scale, par[0:1, :])
        vec[2] += down_sum(tok_ref[rows, :].astype(F32) * back)
        dr1_ref[rows, :] = back
        low = back.astype(BF)
        da_ref[rows, :] = low
        do1_ref[rows, :] = dot_nt(low, w_out[...]).astype(BF)
    for k in range(3):
        vec_ref[k : k + 1, :] = vec[k]

    def grads(at):
        lanes = pl.ds(at, 256)
        g_out[:, lanes] = dot_tn(o1_ref[...], da_ref[:, lanes]).astype(BF)
        g_cross[:, lanes] = dot_tn(h1_ref[...], dq_ref[:, lanes]).astype(BF)

    over_tiles(width // 256, 256, grads)

    def pairs(at):
        g_cross[:, pl.ds(width + at, 256)] = dot_tn(mem_ref[...], dckv_ref[:, pl.ds(at, 256)]).astype(BF)

    over_tiles(2 * width // 256, 256, pairs)


def self_backward(
    lo_s, hi_s, qkv_ref, do1_ref, lo_rows, hi_rows, tok_ref, dqkv_ref, g_qkv, dk_acc, dv_acc
):
    width = tok_ref.shape[1]
    attend_bwd(
        qkv_ref, 0, qkv_ref, width, 2 * width, do1_ref, lo_s, hi_s, lo_rows, hi_rows, dqkv_ref, 0, dk_acc, dv_acc
    )
    dqkv_ref[:, width : 2 * width] = dk_acc[...].astype(BF)
    dqkv_ref[:, 2 * width :] = dv_acc[...].astype(BF)

    def grads(at):
        lanes = pl.ds(at, 256)
        g_qkv[:, lanes] = dot_tn(tok_ref[...], dqkv_ref[:, lanes]).astype(BF)

    over_tiles(3 * width // 256, 256, grads)


def last_grads(dqkv_ref, w_qkv, dr1_ref, dckv_ref, w_ckv, par, gt_ref, gm_ref):
    for t in range(gt_ref.shape[0] // 256):
        rows = pl.ds(t * 256, 256)
        gt_ref[rows, :] = dr1_ref[rows, :] * par[6:7, :] + dot_nt(dqkv_ref[rows, :], w_qkv[...])
        gm_ref[rows, :] = dot_nt(dckv_ref[rows, :], w_ckv[...])


def shaped(*dims, dtype=BF):
    return jax.ShapeDtypeStruct(dims, dtype)


def call(kernel, name, scalars, arrays, outs, scratch=(), flops=0):
    smem = [pl.BlockSpec(memory_space=pltpu.SMEM)] * len(scalars)
    vmem = [pl.BlockSpec(memory_space=pltpu.VMEM)] * len(arrays)
    moved = sum(a.size * a.dtype.itemsize for a in arrays) + sum(
        math.prod(o.shape) * jnp.dtype(o.dtype).itemsize for o in outs
    )
    return pl.pallas_call(
        kernel,
        out_shape=tuple(outs),
        in_specs=smem + vmem,
        out_specs=tuple(pl.BlockSpec(memory_space=pltpu.VMEM) for _ in outs),
        scratch_shapes=list(scratch),
        compiler_params=pltpu.CompilerParams(vmem_limit_bytes=VMEM_BYTES),
        cost_estimate=pl.CostEstimate(flops=flops, bytes_accessed=moved, transcendentals=0),
        name=name,
    )(*scalars, *arrays)


def count_below(values, bounds, strict):
    hit = values[None, :] < bounds[:, None] if strict else values[None, :] <= bounds[:, None]
    return jnp.sum(hit.astype(jnp.int32), axis=1)


def head_rows(values):
    return jnp.tile(values.reshape(-1, QB), (1, SIDE))


def layer(tokens, memory, target_segments, memory_segments, cotangent, w_qkv, w_out, w_cq, w_ckv, w_co, w_in, w_down, par):
    length, width = tokens.shape
    ff = w_in.shape[1]
    own_lo = count_below(target_segments, target_segments, True)
    own_hi = jnp.arange(length, dtype=jnp.int32)
    far_lo = count_below(memory_segments, target_segments, True)
    far_hi = count_below(memory_segments, target_segments, False) - 1
    own = jnp.stack([own_lo, own_hi], axis=1)
    far = jnp.stack([far_lo, far_hi], axis=1)
    vm = pltpu.VMEM
    g = 10**9
    qkv, o1 = call(
        self_forward, "self_forward", (own_lo, own_hi), (tokens, w_qkv, own),
        (shaped(length, 3 * width), shaped(length, width)), flops=8 * g,
    )
    r1, cq, ckv, o2 = call(
        cross_forward, "cross_forward", (far_lo, far_hi), (tokens, memory, o1, w_out, w_cq, w_ckv, par, far),
        (shaped(length, width, dtype=F32), shaped(length, width), shaped(length, 2 * width), shaped(length, width)),
        flops=10 * g,
    )
    out, dr2, do2, g_in, g_down, g_co, vec_two = call(
        ffn_both, "ffn_both", (), (r1, o2, cotangent, w_co, w_in, w_down, par),
        (
            shaped(length, width), shaped(length, width, dtype=F32), shaped(length, width),
            shaped(width, ff), shaped(ff, width), shaped(width, width), shaped(8, width, dtype=F32),
        ),
        (
            vm((length, width), F32), vm((length, width), BF), vm((length, ff), BF), vm((length, ff), F32),
            vm((length, ff), BF), vm((length, width), F32), vm((length, width), BF), vm((length, width), BF),
        ),
        flops=20 * g,
    )
    dckv, dr1, do1, g_cross, g_out, vec_one = call(
        cross_backward, "cross_backward", (far_lo, far_hi),
        (cq, ckv, do2, head_rows(far_lo), head_rows(far_hi), memory, tokens, r1, dr2, o1, w_cq, w_out, par),
        (
            shaped(length, 2 * width), shaped(length, width, dtype=F32), shaped(length, width),
            shaped(width, 3 * width), shaped(width, width), shaped(8, width, dtype=F32),
        ),
        (
            vm((length, width), BF), vm((length, width), F32), vm((length, width), F32),
            vm((length, width), BF), vm((length, width), BF),
        ),
        flops=20 * g,
    )
    dqkv, g_qkv = call(
        self_backward, "self_backward", (own_lo, own_hi),
        (qkv, do1, head_rows(own_lo), head_rows(own_hi), tokens),
        (shaped(length, 3 * width), shaped(width, 3 * width)),
        (vm((length, width), F32), vm((length, width), F32)),
        flops=15 * g,
    )
    grad_tokens, grad_memory = call(
        last_grads, "last_grads", (), (dqkv, w_qkv, dr1, dckv, w_ckv, par),
        (shaped(length, width, dtype=F32), shaped(length, width, dtype=F32)), flops=3 * g,
    )
    vec = jnp.concatenate([vec_one[:3], vec_two[3:6], vec_two[:3]], axis=0)
    return out, grad_tokens, grad_memory, g_in, g_down, g_co, g_cross, g_out, g_qkv, vec


def body(
    mesh,
    tokens,
    memory,
    target_segments,
    memory_segments,
    self_qkv,
    self_out,
    cross_q,
    cross_kv,
    cross_out,
    ffn_in,
    ffn_out,
    norm_gain,
    norm_bias,
    omega,
    cotangent,
):
    wide = mesh.shape["wide"]
    rows = self_qkv.shape[0]
    width = rows * wide
    small = jnp.concatenate([norm_gain, norm_bias, omega, jnp.zeros((rows, 503), jnp.bfloat16)], axis=1)
    down_view = ffn_out.reshape(4, rows, width).transpose(1, 0, 2).reshape(rows, 4 * width)
    first = gather_group(mesh, jnp.concatenate([self_qkv, small], axis=1), "zyx").reshape(width, -1)
    second = gather_group(mesh, jnp.concatenate([self_out, cross_q, cross_kv], axis=1), "zxy").reshape(width, -1)
    third = gather_group(mesh, jnp.concatenate([cross_out, ffn_in], axis=1), "zyx").reshape(width, -1)
    fourth = gather_group(mesh, down_view, "zxy")
    w_qkv = first[:, :1536]
    par = first[:, 1536:1545].astype(jnp.float32).T
    par = jnp.concatenate([par[0:9], jnp.zeros((7, width), jnp.float32)], axis=0)
    w_out, w_cq, w_ckv = second[:, :512], second[:, 512:1024], second[:, 1024:]
    w_co, w_in = third[:, :512], third[:, 512:]
    w_down = fourth.reshape(wide, rows, 4, width).transpose(0, 2, 1, 3).reshape(4 * width, width)
    output, grad_tokens, grad_memory, g_in, g_down, g_co, g_cross, g_out, g_qkv, vec = layer(
        tokens, memory, target_segments, memory_segments, cotangent, w_qkv, w_out, w_cq, w_ckv, w_co, w_in, w_down, par
    )
    vectors = jnp.concatenate([vec.T.astype(jnp.bfloat16), jnp.zeros((width, 503), jnp.bfloat16)], axis=1)
    sum_down = reduce_grad(mesh, g_down, "yxz")
    sum_up = reduce_grad(mesh, g_in, "xyz")
    sum_co = reduce_grad(mesh, g_co, "yxz")
    sum_cross = reduce_grad(mesh, g_cross, "xyz")
    sum_out = reduce_grad(mesh, jnp.concatenate([g_out, vectors], axis=1), "yxz")
    sum_qkv = reduce_grad(mesh, g_qkv, "xyz")
    summed = (
        sum_qkv,
        sum_out[:, :512],
        sum_cross[:, :512],
        sum_cross[:, 512:],
        sum_co,
        sum_up,
        sum_down,
        jnp.stack([sum_out[:, 512], sum_out[:, 515], sum_out[:, 518]], axis=1),
        jnp.stack([sum_out[:, 513], sum_out[:, 516], sum_out[:, 519]], axis=1),
        jnp.stack([sum_out[:, 514], sum_out[:, 517], sum_out[:, 520]], axis=1),
    )
    return (output, grad_tokens, grad_memory) + summed


def solution(mesh):
    in_specs = (
        P(("narrow", "wide"), None),
        P(("narrow", "wide"), None),
        P(("narrow", "wide")),
        P(("narrow", "wide")),
        P("wide", None),
        P("wide", None),
        P("wide", None),
        P("wide", None),
        P("wide", None),
        P("wide", None),
        P("wide", None),
        P("wide", None),
        P("wide", None),
        P("wide", None),
        P(("narrow", "wide"), None),
    )
    out_specs = (
        P(("narrow", "wide"), None),
        P(("narrow", "wide"), None),
        P(("narrow", "wide"), None),
        P("wide", None),
        P("wide", None),
        P("wide", None),
        P("wide", None),
        P("wide", None),
        P("wide", None),
        P("wide", None),
        P("wide", None),
        P("wide", None),
        P("wide", None),
    )
    return jax.shard_map(functools.partial(body, mesh), mesh=mesh, in_specs=in_specs, out_specs=out_specs, check_vma=False)
```

```python
import functools
import math

import jax
import jax.numpy as jnp
from jax import lax
from jax.experimental import pallas as pl
from jax.experimental.pallas import tpu as pltpu
from jax.sharding import PartitionSpec as P

HD = 64

EPSILON = 1e-05
NEGATIVE = -1000000000.0


def wide_parts(mesh):
    bits = mesh.shape["wide"].bit_length() - 1
    low = [(0, 1)] if bits % 2 else []
    low = low + [(at, 2) for at in range(bits % 2, bits, 2)]
    return [(at, 2**count) for at, count in low[::-1]]


class Place:
    def __init__(self, mesh):
        self.parts = wide_parts(mesh)
        self.n = lax.axis_index("narrow")
        self.w = lax.axis_index("wide")
        self.core = lax.rem(self.n, 2)
        self.x = lax.div(self.n, 2)
        self.digits = [lax.rem(lax.div(self.w, 2**low), size) for low, size in self.parts]

    def flip(self, value, d, size):
        out = 0
        bit = 1
        while bit < size:
            digit = lax.rem(lax.div(value, bit), 2)
            out = out + bit * (1 - digit if d & bit else digit)
            bit *= 2
        return out

    def digit_peer(self, j, d):
        low, size = self.parts[j]
        other = self.flip(self.digits[j], d, size)
        return (self.n, self.w + (other - self.digits[j]) * 2**low)

    def x_peer(self):
        return ((1 - self.x) * 2 + self.core, self.w)

    def core_peer(self):
        return (self.x * 2 + 1 - self.core, self.w)

    def peers(self, stage):
        if stage == "x":
            return [self.x_peer()]
        if stage == "core":
            return [self.core_peer()]
        return [self.digit_peer(stage, d) for d in range(1, self.parts[stage][1])]

    def everyone(self):
        return [p for s in list(range(len(self.parts))) + ["x", "core"] for p in self.peers(s)]

    def greet(self):
        barrier = pltpu.get_barrier_semaphore()
        others = self.everyone()
        for peer in others:
            pl.semaphore_signal(barrier, inc=1, device_id=peer, device_id_type=pl.DeviceIdType.MESH)
        pl.semaphore_wait(barrier, len(others))


def stage_orders(mesh):
    count = len(wide_parts(mesh))
    early = list(range(count - 1)) + ["x", count - 1, "core"]
    late = list(range(count))[::-1] + ["x", "core"]
    return early, late


def gather_kernel(mesh, chunks, sizes, *refs):
    count = len(sizes)
    shards, fulls = refs[:count], refs[count : 2 * count]
    send, recv, own = refs[2 * count :]
    place = Place(mesh)
    place.greet()
    digits = len(place.parts)
    used = [0]

    def views(chunk, stage, done):
        which, row, rows, col, cols, split, _ = chunk
        quarter, half = cols // 4, cols // 2
        lanes = pl.ds(col, cols)
        if split:
            lanes = pl.ds(pl.multiple_of(col + place.core * half, 128), half)
            if "x" not in done:
                lanes = pl.ds(pl.multiple_of(col + place.core * half + place.x * quarter, 128), quarter)
        spot = tuple(slice(None) if j in done else place.digits[j] for j in range(digits))
        target = fulls[which].at[spot + (pl.ds(row, rows), lanes)]
        if done:
            return target, target
        return shards[which].at[pl.ds(row, rows), lanes], target

    states = []
    for k, chunk in enumerate(chunks):
        states.append({"done": [], "copies": [], "order": chunk[6]})
        src, target = views(chunk, None, [])
        mine = pltpu.make_async_copy(src, target, own.at[k])
        mine.start()
        states[k]["mine"] = mine
    sent = []

    def advance(k, s):
        state = states[k]
        if s >= len(state["order"]):
            return
        if s == 1:
            state["mine"].wait()
        for copy in state["copies"]:
            copy.wait_recv()
        state["copies"] = []
        stage = state["order"][s]
        src, target = views(chunks[k], stage, state["done"])
        for peer in place.peers(stage):
            at = used[0]
            used[0] += 1
            copy = pltpu.make_async_remote_copy(
                src_ref=src, dst_ref=target, send_sem=send.at[at], recv_sem=recv.at[at],
                device_id=peer, device_id_type=pl.DeviceIdType.MESH,
            )
            copy.start()
            state["copies"].append(copy)
            sent.append(copy)
        state["done"] = state["done"] + [stage]

    stages = max(len(c[6]) for c in chunks)
    for t in range(len(chunks) + stages * GATHER_LAG):
        for s in reversed(range(stages)):
            k = t - s * GATHER_LAG
            if 0 <= k < len(chunks):
                advance(k, s)
    for state in states:
        for copy in state["copies"]:
            copy.wait_recv()
    for copy in sent:
        copy.wait_send()


GATHER_LAG = 4


def gather_weights(mesh, shards, collective):
    early, late = stage_orders(mesh)
    digits = tuple(size for _, size in wide_parts(mesh))
    small_order = [s for s in early if not isinstance(s, str)]
    chunks = []
    for which, shard in enumerate(shards):
        rows, cols = shard.shape
        if cols < 512:
            chunks.append((which, 0, rows, 0, cols, False, small_order))
            continue
        cut = max(1, rows // 64)
        for r in range(cut):
            for c in range(cols // 512):
                order = late if len(chunks) % 8 in (1, 4, 6) else early
                chunks.append((which, r * (rows // cut), rows // cut, c * 512, 512, True, order))
    copies = sum(stage_copies(mesh, c[6]) for c in chunks)
    sizes = [s.shape for s in shards]
    fulls = pl.pallas_call(
        functools.partial(gather_kernel, mesh, chunks, sizes),
        out_shape=tuple(jax.ShapeDtypeStruct(digits + s.shape, s.dtype) for s in shards),
        in_specs=[pl.BlockSpec(memory_space=pl.ANY)] * len(shards),
        out_specs=tuple(pl.BlockSpec(memory_space=pl.ANY) for _ in shards),
        scratch_shapes=[
            pltpu.SemaphoreType.DMA((copies,)),
            pltpu.SemaphoreType.DMA((copies,)),
            pltpu.SemaphoreType.DMA((len(chunks),)),
        ],
        compiler_params=pltpu.CompilerParams(collective_id=collective, has_side_effects=True),
        name="gather_weights",
    )(*shards)
    return [full.reshape((-1, full.shape[-1])) for full in fulls]


def stage_copies(mesh, order):
    parts = wide_parts(mesh)
    return sum(1 if isinstance(s, str) else parts[s][1] - 1 for s in order)


BF = jnp.bfloat16
F32 = jnp.float32
QB = 64
WIN = 256
GROUP = 256
SIDE = GROUP // HD
VMEM_BYTES = 56 * 2**20


def dot(left, right):
    return lax.dot_general(left, right, (((1,), (0,)), ((), ())), preferred_element_type=F32)


def dot_nt(left, right):
    return lax.dot_general(left, right, (((1,), (1,)), ((), ())), preferred_element_type=F32)


def dot_tn(left, right):
    return lax.dot_general(left, right, (((0,), (0,)), ((), ())), preferred_element_type=F32)


def norm_parts(resid):
    middle = jnp.mean(resid, axis=-1, keepdims=True)
    centred = resid - middle
    spread = jnp.mean(centred * centred, axis=-1, keepdims=True)
    scale = lax.rsqrt(spread + EPSILON)
    return centred * scale, scale


def norm_back(grad, normal, scale, gain):
    scaled = grad * gain
    middle = jnp.mean(scaled, axis=-1, keepdims=True)
    along = jnp.mean(scaled * normal, axis=-1, keepdims=True)
    return (scaled - middle - normal * along) * scale


def down_sum(value):
    return jnp.sum(value, axis=0, keepdims=True)


def head_masks(scale):
    rows = lax.broadcasted_iota(jnp.int32, (SIDE * QB, GROUP), 0) // QB
    lanes = lax.broadcasted_iota(jnp.int32, (SIDE * QB, GROUP), 1) // HD
    return jnp.where(rows == lanes, scale, 0.0).astype(BF)


def pick_heads(stacked):
    lanes = lax.broadcasted_iota(jnp.int32, (QB, GROUP), 1) // HD
    out = stacked[:QB]
    for h in range(1, SIDE):
        out = jnp.where(lanes == h, stacked[h * QB : (h + 1) * QB], out)
    return out


def stack_heads(block, mask):
    return jnp.concatenate([block] * SIDE, axis=0) * mask


def window(first, step, length):
    begin = first + step * WIN
    start = pl.multiple_of(jnp.minimum(begin, length - WIN), 16)
    return begin, start


def attend_fwd(q_ref, q_at, k_ref, k_at, v_at, lo_s, hi_s, lohi_ref, o_ref):
    length = k_ref.shape[0]
    mask = head_masks(HD**-0.5)

    def one(b, carry):
        q0 = pl.multiple_of(b * QB, QB)
        first = (lo_s[q0] // 16) * 16
        last = hi_s[q0 + QB - 1]
        low = lohi_ref[pl.ds(q0, QB), 0:1]
        high = lohi_ref[pl.ds(q0, QB), 1:2]

        def scores(g, begin, start):
            places = start + lax.broadcasted_iota(jnp.int32, (QB, WIN), 1)
            ok = (places >= jnp.maximum(low, begin)) & (places <= high)
            ok = jnp.concatenate([ok] * SIDE, axis=0)
            query = stack_heads(q_ref[pl.ds(q0, QB), pl.ds(q_at + g * GROUP, GROUP)], mask)
            keys = k_ref[pl.ds(start, WIN), pl.ds(k_at + g * GROUP, GROUP)]
            return jnp.where(ok, dot_nt(query, keys), NEGATIVE)

        def values(g, start):
            return k_ref[pl.ds(start, WIN), pl.ds(v_at + g * GROUP, GROUP)]

        def store(g, stacked):
            o_ref[pl.ds(q0, QB), pl.ds(g * GROUP, GROUP)] = pick_heads(stacked).astype(BF)

        @pl.when(last - first < WIN)
        def _():
            begin, start = window(first, 0, length)
            for g in range(2):
                score = scores(g, begin, start)
                top = jnp.max(score, axis=-1, keepdims=True)
                raised = jnp.exp(score - top)
                total = jnp.sum(raised, axis=-1, keepdims=True)
                weights = (raised * (1.0 / total)).astype(BF)
                store(g, dot(weights, values(g, start)))

        @pl.when(last - first >= WIN)
        def _():
            count = (last - first) // WIN + 1
            for g in range(2):

                def stats(k, state):
                    top, total = state
                    begin, start = window(first, k, length)
                    score = scores(g, begin, start)
                    higher = jnp.maximum(top, jnp.max(score, axis=-1, keepdims=True))
                    raised = jnp.sum(jnp.exp(score - higher), axis=-1, keepdims=True)
                    return higher, total * jnp.exp(top - higher) + raised

                start_top = jnp.full((SIDE * QB, 1), 2 * NEGATIVE, F32)
                top, total = lax.fori_loop(0, count, stats, (start_top, jnp.zeros((SIDE * QB, 1), F32)))

                def mix(k, out):
                    begin, start = window(first, k, length)
                    weights = jnp.exp(scores(g, begin, start) - top) * (1.0 / total)
                    return out + dot(weights.astype(BF), values(g, start))

                store(g, lax.fori_loop(0, count, mix, jnp.zeros((SIDE * QB, GROUP), F32)))

        return carry

    lax.fori_loop(0, q_ref.shape[0] // QB, one, 0)


def attend_bwd(q_ref, q_at, k_ref, k_at, v_at, do_ref, lo_s, hi_s, lo_rows, hi_rows, dq_ref, dq_at, dk_acc, dv_acc):
    length = k_ref.shape[0]
    factor = HD**-0.5
    q_mask = head_masks(factor)
    do_mask = head_masks(1.0)
    dk_acc[...] = jnp.zeros_like(dk_acc)
    dv_acc[...] = jnp.zeros_like(dv_acc)

    def one(b, carry):
        q0 = pl.multiple_of(b * QB, QB)
        first = (lo_s[q0] // 16) * 16
        last = hi_s[q0 + QB - 1]
        low = lo_rows[pl.ds(b, 1), :]
        high = hi_rows[pl.ds(b, 1), :]

        def keys(g, start):
            return k_ref[pl.ds(start, WIN), pl.ds(k_at + g * GROUP, GROUP)]

        def values(g, start):
            return k_ref[pl.ds(start, WIN), pl.ds(v_at + g * GROUP, GROUP)]

        def query(g):
            return stack_heads(q_ref[pl.ds(q0, QB), pl.ds(q_at + g * GROUP, GROUP)], q_mask)

        def grad(g):
            return stack_heads(do_ref[pl.ds(q0, QB), pl.ds(g * GROUP, GROUP)], do_mask)

        def scores(g, begin, start):
            places = start + lax.broadcasted_iota(jnp.int32, (WIN, SIDE * QB), 0)
            ok = (places >= jnp.maximum(low, begin)) & (places <= high)
            return jnp.where(ok, dot_nt(keys(g, start), query(g)), NEGATIVE)

        def spread(g, start, probs, slopes, middle):
            delta = (probs * (slopes - middle)).astype(BF)
            rows = pl.ds(start, WIN)
            lanes = pl.ds(g * GROUP, GROUP)
            dv_acc[rows, lanes] += dot(probs.astype(BF), grad(g))
            dk_acc[rows, lanes] += dot(delta, query(g))
            return dot_tn(delta, keys(g, start))

        def store(g, stacked):
            dq = pick_heads(stacked) * factor
            dq_ref[pl.ds(q0, QB), pl.ds(dq_at + g * GROUP, GROUP)] = dq.astype(BF)

        @pl.when(last - first < WIN)
        def _():
            begin, start = window(first, 0, length)
            for g in range(2):
                score = scores(g, begin, start)
                slopes = dot_nt(values(g, start), grad(g))
                raised = jnp.exp(score - jnp.max(score, axis=0, keepdims=True))
                probs = raised * (1.0 / down_sum(raised))
                store(g, spread(g, start, probs, slopes, down_sum(probs * slopes)))

        @pl.when(last - first >= WIN)
        def _():
            count = (last - first) // WIN + 1
            for g in range(2):

                def stats(k, state):
                    top, total = state
                    begin, start = window(first, k, length)
                    score = scores(g, begin, start)
                    higher = jnp.maximum(top, jnp.max(score, axis=0, keepdims=True))
                    return higher, total * jnp.exp(top - higher) + down_sum(jnp.exp(score - higher))

                start_top = jnp.full((1, SIDE * QB), 2 * NEGATIVE, F32)
                top, total = lax.fori_loop(0, count, stats, (start_top, jnp.zeros((1, SIDE * QB), F32)))

                def probs_of(k):
                    begin, start = window(first, k, length)
                    probs = jnp.exp(scores(g, begin, start) - top) * (1.0 / total)
                    return start, probs, dot_nt(values(g, start), grad(g))

                def centre(k, middle):
                    _, probs, slopes = probs_of(k)
                    return middle + down_sum(probs * slopes)

                middle = lax.fori_loop(0, count, centre, jnp.zeros((1, SIDE * QB), F32))

                def last_pass(k, out):
                    start, probs, slopes = probs_of(k)
                    return out + spread(g, start, probs, slopes, middle)

                store(g, lax.fori_loop(0, count, last_pass, jnp.zeros((SIDE * QB, GROUP), F32)))

        return carry

    lax.fori_loop(0, q_ref.shape[0] // QB, one, 0)


def over_tiles(count, size, step):
    def one(t, carry):
        step(pl.multiple_of(t * size, size))
        return carry

    lax.fori_loop(0, count, one, 0)


def self_forward(lo_s, hi_s, tok_ref, w_ref, lohi_ref, qkv_ref, o_ref):
    def project(at):
        qkv_ref[:, pl.ds(at, 256)] = dot(tok_ref[...], w_ref[:, pl.ds(at, 256)]).astype(BF)

    over_tiles(w_ref.shape[1] // 256, 256, project)
    width = o_ref.shape[1]
    attend_fwd(qkv_ref, 0, qkv_ref, width, 2 * width, lo_s, hi_s, lohi_ref, o_ref)


def cross_forward(
    lo_s, hi_s, tok_ref, mem_ref, o1_ref, w_out, w_cq, w_ckv, par, lohi_ref, r1_ref, cq_ref, ckv_ref, o2_ref
):
    tokens = tok_ref.shape[0]

    def pairs(at):
        ckv_ref[:, pl.ds(at, 256)] = dot(mem_ref[...], w_ckv[:, pl.ds(at, 256)]).astype(BF)

    over_tiles(w_ckv.shape[1] // 256, 256, pairs)
    for t in range(tokens // 256):
        rows = pl.ds(t * 256, 256)
        resid = tok_ref[rows, :].astype(F32) * par[6:7, :] + dot(o1_ref[rows, :], w_out[...])
        r1_ref[rows, :] = resid
        normal, _ = norm_parts(resid)
        hidden = (normal * par[0:1, :] + par[3:4, :]).astype(BF)
        cq_ref[rows, :] = dot(hidden, w_cq[...]).astype(BF)
    attend_fwd(cq_ref, 0, ckv_ref, 0, cq_ref.shape[1], lo_s, hi_s, lohi_ref, o2_ref)


def gelu_parts(value):
    area = 0.5 * (1.0 + lax.erf(value * (0.5**0.5)))
    bell = jnp.exp(-0.5 * value * value) * 0.3989422804014327
    return value * area, area + value * bell


def ffn_both(
    r1_ref, o2_ref, cot_ref, w_co, w_in, w_down, par,
    out_ref, dr2_ref, do2_ref, g_in, g_down, g_co, vec_ref,
    r2_ref, h2_ref, z_ref, gp_ref, du_ref, dr3_ref, df_ref, da_ref,
):
    tokens, width = r1_ref.shape
    wide = w_in.shape[1]

    def resid_two(t):
        rows = pl.ds(t * 256, 256)
        hidden = norm_parts(r1_ref[rows, :])[0] * par[0:1, :] + par[3:4, :]
        resid = hidden * par[7:8, :] + dot(o2_ref[rows, :], w_co[...])
        r2_ref[rows, :] = resid
        h2_ref[rows, :] = (norm_parts(resid)[0] * par[1:2, :] + par[4:5, :]).astype(BF)

    for t in range(tokens // 256):
        resid_two(t)

    def up(at):
        lanes = pl.ds(at, 256)
        active, slope = gelu_parts(dot(h2_ref[...], w_in[:, lanes]))
        z_ref[:, lanes] = active.astype(BF)
        gp_ref[:, lanes] = slope

    over_tiles(wide // 256, 256, up)
    vec = [jnp.zeros((1, width), F32) for _ in range(6)]
    for t in range(tokens // 256):
        rows = pl.ds(t * 256, 256)
        hidden = norm_parts(r2_ref[rows, :])[0] * par[1:2, :] + par[4:5, :]
        resid = hidden * par[8:9, :] + dot(z_ref[rows, :], w_down[...])
        normal, scale = norm_parts(resid)
        out_ref[rows, :] = (normal * par[2:3, :] + par[5:6, :]).astype(BF)
        grad = cot_ref[rows, :].astype(F32)
        vec[0] += down_sum(grad * normal)
        vec[1] += down_sum(grad)
        back = norm_back(grad, normal, scale, par[2:3, :])
        vec[2] += down_sum(hidden * back)
        dr3_ref[rows, :] = back
        df_ref[rows, :] = back.astype(BF)

    def down(at):
        lanes = pl.ds(at, 256)
        grad = dot_nt(df_ref[...], w_down[pl.ds(at, 256), :])
        du_ref[:, lanes] = (grad * gp_ref[:, lanes]).astype(BF)

    over_tiles(wide // 256, 256, down)
    for t in range(tokens // 256):
        rows = pl.ds(t * 256, 256)
        grad = dr3_ref[rows, :] * par[8:9, :] + dot_nt(du_ref[rows, :], w_in[...])
        normal, scale = norm_parts(r2_ref[rows, :])
        vec[3] += down_sum(grad * normal)
        vec[4] += down_sum(grad)
        back = norm_back(grad, normal, scale, par[1:2, :])
        hidden = norm_parts(r1_ref[rows, :])[0] * par[0:1, :] + par[3:4, :]
        vec[5] += down_sum(hidden * back)
        dr2_ref[rows, :] = back
        low = back.astype(BF)
        da_ref[rows, :] = low
        do2_ref[rows, :] = dot_nt(low, w_co[...]).astype(BF)
    for k in range(6):
        vec_ref[k : k + 1, :] = vec[k]

    def grad_up(at):
        lanes = pl.ds(at, 256)
        g_in[:, lanes] = dot_tn(h2_ref[...], du_ref[:, lanes]).astype(BF)
        g_down[pl.ds(at, 256), :] = dot_tn(z_ref[:, lanes], df_ref[...]).astype(BF)

    over_tiles(wide // 256, 256, grad_up)

    def grad_co(at):
        lanes = pl.ds(at, 256)
        g_co[:, lanes] = dot_tn(o2_ref[...], da_ref[:, lanes]).astype(BF)

    over_tiles(width // 256, 256, grad_co)


def cross_backward(
    lo_s, hi_s, cq_ref, ckv_ref, do2_ref, lo_rows, hi_rows, mem_ref, tok_ref, r1_ref, dr2_ref, o1_ref, w_cq, w_out, par,
    dckv_ref, dr1_ref, do1_ref, g_cross, g_out, vec_ref,
    dq_ref, dk_acc, dv_acc, h1_ref, da_ref,
):
    tokens, width = r1_ref.shape
    attend_bwd(
        cq_ref, 0, ckv_ref, 0, width, do2_ref, lo_s, hi_s, lo_rows, hi_rows, dq_ref, 0, dk_acc, dv_acc
    )
    dckv_ref[:, :width] = dk_acc[...].astype(BF)
    dckv_ref[:, width:] = dv_acc[...].astype(BF)
    vec = [jnp.zeros((1, width), F32) for _ in range(3)]
    for t in range(tokens // 256):
        rows = pl.ds(t * 256, 256)
        grad = dr2_ref[rows, :] * par[7:8, :] + dot_nt(dq_ref[rows, :], w_cq[...])
        normal, scale = norm_parts(r1_ref[rows, :])
        h1_ref[rows, :] = (normal * par[0:1, :] + par[3:4, :]).astype(BF)
        vec[0] += down_sum(grad * normal)
        vec[1] += down_sum(grad)
        back = norm_back(grad, normal, scale, par[0:1, :])
        vec[2] += down_sum(tok_ref[rows, :].astype(F32) * back)
        dr1_ref[rows, :] = back
        low = back.astype(BF)
        da_ref[rows, :] = low
        do1_ref[rows, :] = dot_nt(low, w_out[...]).astype(BF)
    for k in range(3):
        vec_ref[k : k + 1, :] = vec[k]

    def grads(at):
        lanes = pl.ds(at, 256)
        g_out[:, lanes] = dot_tn(o1_ref[...], da_ref[:, lanes]).astype(BF)
        g_cross[:, lanes] = dot_tn(h1_ref[...], dq_ref[:, lanes]).astype(BF)

    over_tiles(width // 256, 256, grads)

    def pairs(at):
        g_cross[:, pl.ds(width + at, 256)] = dot_tn(mem_ref[...], dckv_ref[:, pl.ds(at, 256)]).astype(BF)

    over_tiles(2 * width // 256, 256, pairs)


def self_backward(
    lo_s, hi_s, qkv_ref, do1_ref, lo_rows, hi_rows, tok_ref, dqkv_ref, g_qkv, dk_acc, dv_acc
):
    width = tok_ref.shape[1]
    attend_bwd(
        qkv_ref, 0, qkv_ref, width, 2 * width, do1_ref, lo_s, hi_s, lo_rows, hi_rows, dqkv_ref, 0, dk_acc, dv_acc
    )
    dqkv_ref[:, width : 2 * width] = dk_acc[...].astype(BF)
    dqkv_ref[:, 2 * width :] = dv_acc[...].astype(BF)

    def grads(at):
        lanes = pl.ds(at, 256)
        g_qkv[:, lanes] = dot_tn(tok_ref[...], dqkv_ref[:, lanes]).astype(BF)

    over_tiles(3 * width // 256, 256, grads)


def last_grads(dqkv_ref, w_qkv, dr1_ref, dckv_ref, w_ckv, par, gt_ref, gm_ref):
    for t in range(gt_ref.shape[0] // 256):
        rows = pl.ds(t * 256, 256)
        gt_ref[rows, :] = dr1_ref[rows, :] * par[6:7, :] + dot_nt(dqkv_ref[rows, :], w_qkv[...])
        gm_ref[rows, :] = dot_nt(dckv_ref[rows, :], w_ckv[...])


def shaped(*dims, dtype=BF):
    return jax.ShapeDtypeStruct(dims, dtype)


def call(kernel, name, scalars, arrays, outs, scratch=(), flops=0):
    smem = [pl.BlockSpec(memory_space=pltpu.SMEM)] * len(scalars)
    vmem = [pl.BlockSpec(memory_space=pltpu.VMEM)] * len(arrays)
    moved = sum(a.size * a.dtype.itemsize for a in arrays) + sum(
        math.prod(o.shape) * jnp.dtype(o.dtype).itemsize for o in outs
    )
    return pl.pallas_call(
        kernel,
        out_shape=tuple(outs),
        in_specs=smem + vmem,
        out_specs=tuple(pl.BlockSpec(memory_space=pltpu.VMEM) for _ in outs),
        scratch_shapes=list(scratch),
        compiler_params=pltpu.CompilerParams(vmem_limit_bytes=VMEM_BYTES),
        cost_estimate=pl.CostEstimate(flops=flops, bytes_accessed=moved, transcendentals=0),
        name=name,
    )(*scalars, *arrays)


def count_below(values, bounds, strict):
    hit = values[None, :] < bounds[:, None] if strict else values[None, :] <= bounds[:, None]
    return jnp.sum(hit.astype(jnp.int32), axis=1)


def head_rows(values):
    return jnp.tile(values.reshape(-1, QB), (1, SIDE))


def layer(tokens, memory, target_segments, memory_segments, cotangent, w_qkv, w_out, w_cq, w_ckv, w_co, w_in, w_down, par):
    length, width = tokens.shape
    ff = w_in.shape[1]
    own_lo = count_below(target_segments, target_segments, True)
    own_hi = jnp.arange(length, dtype=jnp.int32)
    far_lo = count_below(memory_segments, target_segments, True)
    far_hi = count_below(memory_segments, target_segments, False) - 1
    own = jnp.stack([own_lo, own_hi], axis=1)
    far = jnp.stack([far_lo, far_hi], axis=1)
    vm = pltpu.VMEM
    g = 10**9
    qkv, o1 = call(
        self_forward, "self_forward", (own_lo, own_hi), (tokens, w_qkv, own),
        (shaped(length, 3 * width), shaped(length, width)), flops=8 * g,
    )
    r1, cq, ckv, o2 = call(
        cross_forward, "cross_forward", (far_lo, far_hi), (tokens, memory, o1, w_out, w_cq, w_ckv, par, far),
        (shaped(length, width, dtype=F32), shaped(length, width), shaped(length, 2 * width), shaped(length, width)),
        flops=10 * g,
    )
    out, dr2, do2, g_in, g_down, g_co, vec_two = call(
        ffn_both, "ffn_both", (), (r1, o2, cotangent, w_co, w_in, w_down, par),
        (
            shaped(length, width), shaped(length, width, dtype=F32), shaped(length, width),
            shaped(width, ff), shaped(ff, width), shaped(width, width), shaped(8, width, dtype=F32),
        ),
        (
            vm((length, width), F32), vm((length, width), BF), vm((length, ff), BF), vm((length, ff), F32),
            vm((length, ff), BF), vm((length, width), F32), vm((length, width), BF), vm((length, width), BF),
        ),
        flops=20 * g,
    )
    dckv, dr1, do1, g_cross, g_out, vec_one = call(
        cross_backward, "cross_backward", (far_lo, far_hi),
        (cq, ckv, do2, head_rows(far_lo), head_rows(far_hi), memory, tokens, r1, dr2, o1, w_cq, w_out, par),
        (
            shaped(length, 2 * width), shaped(length, width, dtype=F32), shaped(length, width),
            shaped(width, 3 * width), shaped(width, width), shaped(8, width, dtype=F32),
        ),
        (
            vm((length, width), BF), vm((length, width), F32), vm((length, width), F32),
            vm((length, width), BF), vm((length, width), BF),
        ),
        flops=20 * g,
    )
    dqkv, g_qkv = call(
        self_backward, "self_backward", (own_lo, own_hi),
        (qkv, do1, head_rows(own_lo), head_rows(own_hi), tokens),
        (shaped(length, 3 * width), shaped(width, 3 * width)),
        (vm((length, width), F32), vm((length, width), F32)),
        flops=15 * g,
    )
    grad_tokens, grad_memory = call(
        last_grads, "last_grads", (), (dqkv, w_qkv, dr1, dckv, w_ckv, par),
        (shaped(length, width, dtype=F32), shaped(length, width, dtype=F32)), flops=3 * g,
    )
    vec = jnp.concatenate([vec_one[:3], vec_two[3:6], vec_two[:3]], axis=0)
    return out, grad_tokens, grad_memory, g_in, g_down, g_co, g_cross, g_out, g_qkv, vec


REDUCE_LAG = 4


def reduce_orders(mesh):
    digits = list(range(len(wide_parts(mesh))))[::-1]
    return ["core", "x"] + digits, ["core", digits[0], "x"] + digits[1:]


def reduce_kernel(mesh, chunks, count, *refs):
    grads, sums = refs[:count], refs[count : 2 * count]
    held = refs[2 * count : 2 * count + len(chunks)]
    pool = list(refs[2 * count + len(chunks) : -3])
    send, recv, own = refs[-3:]
    place = Place(mesh)
    place.greet()
    bits = {"core": place.core, "x": place.x}
    used = [0]
    sent = []

    def ship(src, target, peer):
        at = used[0]
        used[0] += 1
        copy = pltpu.make_async_remote_copy(
            src_ref=src, dst_ref=target, send_sem=send.at[at], recv_sem=recv.at[at],
            device_id=peer, device_id_type=pl.DeviceIdType.MESH,
        )
        copy.start()
        sent.append(copy)
        return copy

    def digit_view(ref, j, index, done):
        spot = [slice(None)] * len(place.parts)
        spot[j] = pl.ds(index, 1)
        return ref.at[tuple(spot)]

    def lanes_view(ref, start, size):
        return ref.at[..., pl.ds(pl.multiple_of(start, 128), size)]

    states = []
    for k, (which, sub, col, cols, order, split) in enumerate(chunks):
        source = grads[which].at[..., sub, :, pl.ds(col, cols)]
        if split:
            half = cols // 2
            wanted = lanes_view(grads[which].at[..., sub, :, :], col + place.core * half, half)
            other = lanes_view(grads[which].at[..., sub, :, :], col + (1 - place.core) * half, half)
        else:
            wanted = other = source
        mine = pltpu.make_async_copy(wanted, held[k], own.at[k])
        mine.start()
        states.append({"mine": mine, "other": other, "copies": [], "bufs": [], "cur": held[k], "sel": None})

    def finish_stage(k, stage):
        state = states[k]
        split = chunks[k][5]
        for copy in state["copies"]:
            copy.wait_recv()
        cur = state["cur"]
        if stage == "core" or (stage == "x" and not split):
            if stage == "core":
                state["mine"].wait()
            value = cur[...].astype(F32)
        elif stage == "x":
            half = cur.shape[-1] // 2
            value = lanes_view(cur, place.x * half, half)[...].astype(F32)
        else:
            value = digit_view(cur, stage, place.digits[stage], None)[...].astype(F32)
        for buf in state["bufs"]:
            value = value + buf[...].astype(F32)
        total = pool.pop(0)
        total[...] = value.astype(BF)
        state["cur"] = total
        state["copies"], state["bufs"] = [], []

    def start_stage(k, stage):
        state = states[k]
        split = chunks[k][5]
        cur = state["cur"]
        if stage == "core":
            buf = pool.pop(0)
            state["copies"] = [ship(state["other"], buf, place.core_peer())]
            state["bufs"] = [buf]
        elif stage == "x":
            buf = pool.pop(0)
            src = cur
            if split:
                half = cur.shape[-1] // 2
                src = lanes_view(cur, (1 - place.x) * half, half)
            state["copies"] = [ship(src, buf, place.x_peer())]
            state["bufs"] = [buf]
        else:
            size = place.parts[stage][1]
            for d in range(1, size):
                buf = pool.pop(0)
                src = digit_view(cur, stage, place.flip(place.digits[stage], d, size), None)
                state["copies"].append(ship(src, buf, place.digit_peer(stage, d)))
                state["bufs"].append(buf)

    def out_view(k, size):
        which, sub, col, cols, order, split = chunks[k]
        start = col
        if size < cols:
            start = start + place.core * (cols // 2)
        if size < cols // 2:
            start = start + place.x * (cols // 4)
        rows = states[k]["cur"].shape[-2]
        if isinstance(start, int):
            return sums[which].at[pl.ds(sub * rows, rows), pl.ds(start, size)]
        return sums[which].at[pl.ds(sub * rows, rows), pl.ds(pl.multiple_of(start, 128), size)]

    def advance(k, s):
        order, split = chunks[k][4], chunks[k][5]
        state = states[k]
        stages = len(order)
        if s > 0 and s <= stages:
            finish_stage(k, order[s - 1])
        if s < stages:
            start_stage(k, order[s])
        elif s == stages:
            cols = chunks[k][3]
            size = cols // 4 if split else cols
            view = out_view(k, size)
            view[...] = state["cur"][...].reshape(view.shape)
            if split:
                state["copies"] = [ship(view, view, place.x_peer())]
        elif s == stages + 1 and split:
            for copy in state["copies"]:
                copy.wait_recv()
            view = out_view(k, chunks[k][3] // 2)
            state["copies"] = [ship(view, view, place.core_peer())]
        elif s == stages + 2 and split:
            for copy in state["copies"]:
                copy.wait_recv()

    steps = max(len(c[4]) for c in chunks) + 3
    for t in range(len(chunks) + steps * REDUCE_LAG):
        for s in reversed(range(steps)):
            k = t - s * REDUCE_LAG
            if 0 <= k < len(chunks):
                advance(k, s)
    for copy in sent:
        copy.wait_send()


def buffers_of(mesh, order, split, shape):
    parts = wide_parts(mesh)
    per_stage = []
    shape = list(shape)
    for stage in order:
        if stage == "x" and split:
            shape[-1] //= 2
        arrived = 1
        if not isinstance(stage, str):
            shape[stage] = 1
            arrived = parts[stage][1] - 1
        per_stage.append((tuple(shape), arrived))
    return per_stage


def reduce_grads(mesh, grads, collective):
    early, late = reduce_orders(mesh)
    digits = tuple(size for _, size in wide_parts(mesh))
    wide = mesh.shape["wide"]
    views, chunks, sums = [], [], []
    for which, grad in enumerate(grads):
        rows, cols = grad.shape[0] // wide, grad.shape[1]
        sub = rows * wide // cols if cols == 512 and rows * wide > 512 else 1
        views.append(grad.reshape(digits + (sub, rows // sub, cols)))
        sums.append(jax.ShapeDtypeStruct((rows, cols), BF))
        if cols < 512:
            chunks.append((which, 0, 0, cols, early, False))
            continue
        for j in range(sub):
            for c in range(cols // 512):
                chunks.append((which, j, c * 512, 512, late if len(chunks) % 2 else early, True))
    held, plan = [], []
    for which, sub, col, cols, order, split in chunks:
        shape = digits + (views[which].shape[-2], cols // 2 if split else cols)
        held.append(pltpu.VMEM(shape, BF))
        plan.append(buffers_of(mesh, order, split, shape))
    pool = []
    steps = max(len(c[4]) for c in chunks) + 3
    for t in range(len(chunks) + steps * REDUCE_LAG):
        for s in reversed(range(steps)):
            k = t - s * REDUCE_LAG
            if 0 <= k < len(chunks):
                if 0 < s <= len(plan[k]):
                    pool.append(pltpu.VMEM(plan[k][s - 1][0], BF))
                if s < len(plan[k]):
                    pool += [pltpu.VMEM(plan[k][s][0], BF)] * plan[k][s][1]
    copies = sum(sum(n for _, n in p) + 2 for p in plan)
    return pl.pallas_call(
        functools.partial(reduce_kernel, mesh, chunks, len(grads)),
        out_shape=tuple(sums),
        in_specs=[pl.BlockSpec(memory_space=pl.ANY)] * len(grads),
        out_specs=tuple(pl.BlockSpec(memory_space=pltpu.VMEM) for _ in grads),
        scratch_shapes=held + pool + [
            pltpu.SemaphoreType.DMA((copies,)),
            pltpu.SemaphoreType.DMA((copies,)),
            pltpu.SemaphoreType.DMA((len(chunks),)),
        ],
        compiler_params=pltpu.CompilerParams(
            collective_id=collective, has_side_effects=True, vmem_limit_bytes=VMEM_BYTES
        ),
        name="reduce_grads",
    )(*views)


def widen_kernel(count, *refs):
    for src, out in zip(refs[:count], refs[count:]):
        out[...] = src[...].astype(F32)


def body(
    mesh,
    tokens,
    memory,
    target_segments,
    memory_segments,
    self_qkv,
    self_out,
    cross_q,
    cross_kv,
    cross_out,
    ffn_in,
    ffn_out,
    norm_gain,
    norm_bias,
    omega,
    cotangent,
):
    wide = mesh.shape["wide"]
    rows = self_qkv.shape[0]
    width = rows * wide
    small = jnp.concatenate([norm_gain, norm_bias, omega], axis=1).T
    small = jnp.pad(small, ((0, 7), (0, 128 - rows)))
    w_qkv, w_out, w_cq, w_ckv, w_co, w_in, w_down, spread = gather_weights(
        mesh, (self_qkv, self_out, cross_q, cross_kv, cross_out, ffn_in, ffn_out, small), 1
    )
    par = spread.reshape(wide, 16, 128)[:, :, :rows].transpose(1, 0, 2).reshape(16, width).astype(jnp.float32)
    output, grad_tokens, grad_memory, g_in, g_down, g_co, g_cross, g_out, g_qkv, vec = layer(
        tokens, memory, target_segments, memory_segments, cotangent, w_qkv, w_out, w_cq, w_ckv, w_co, w_in, w_down, par
    )
    vectors = vec.astype(BF).reshape(9, wide, rows).transpose(1, 0, 2)
    vectors = jnp.pad(vectors, ((0, 0), (0, 7), (0, 128 - rows))).reshape(wide * 16, 128)
    sums = reduce_grads(mesh, (g_in, g_down, g_co, g_cross, g_out, g_qkv, vectors), 2)
    s_in, s_down, s_co, s_cross, s_out, s_qkv = call(
        functools.partial(widen_kernel, 6), "widen", (), sums[:6], tuple(shaped(*s.shape, dtype=F32) for s in sums[:6])
    )
    small = sums[6][:9, :rows].astype(jnp.float32).reshape(3, 3, rows).transpose(1, 2, 0)
    summed = (s_qkv, s_out, s_cross[:, :width], s_cross[:, width:], s_co, s_in, s_down, small[0], small[1], small[2])
    return (output, grad_tokens, grad_memory) + summed


def solution(mesh):
    in_specs = (
        P(("narrow", "wide"), None),
        P(("narrow", "wide"), None),
        P(("narrow", "wide")),
        P(("narrow", "wide")),
        P("wide", None),
        P("wide", None),
        P("wide", None),
        P("wide", None),
        P("wide", None),
        P("wide", None),
        P("wide", None),
        P("wide", None),
        P("wide", None),
        P("wide", None),
        P(("narrow", "wide"), None),
    )
    out_specs = (
        P(("narrow", "wide"), None),
        P(("narrow", "wide"), None),
        P(("narrow", "wide"), None),
        P("wide", None),
        P("wide", None),
        P("wide", None),
        P("wide", None),
        P("wide", None),
        P("wide", None),
        P("wide", None),
        P("wide", None),
        P("wide", None),
        P("wide", None),
    )
    return jax.shard_map(functools.partial(body, mesh), mesh=mesh, in_specs=in_specs, out_specs=out_specs, check_vma=False)
```

```python
import functools
import math

import jax
import jax.numpy as jnp
from jax import lax
from jax.experimental import pallas as pl
from jax.experimental.pallas import tpu as pltpu
from jax.sharding import PartitionSpec as P

HD = 64

EPSILON = 1e-05
NEGATIVE = -1000000000.0
SEGS = 32


def wide_parts(mesh):
    bits = mesh.shape["wide"].bit_length() - 1
    low = [(0, 1)] if bits % 2 else []
    low = low + [(at, 2) for at in range(bits % 2, bits, 2)]
    return [(at, 2**count) for at, count in low[::-1]]


class Place:
    def __init__(self, mesh):
        self.parts = wide_parts(mesh)
        self.n = lax.axis_index("narrow")
        self.w = lax.axis_index("wide")
        self.core = lax.rem(self.n, 2)
        self.x = lax.div(self.n, 2)
        self.digits = [lax.rem(lax.div(self.w, 2**low), size) for low, size in self.parts]

    def flip(self, value, d, size):
        out = 0
        bit = 1
        while bit < size:
            digit = lax.rem(lax.div(value, bit), 2)
            out = out + bit * (1 - digit if d & bit else digit)
            bit *= 2
        return out

    def digit_peer(self, j, d):
        low, size = self.parts[j]
        other = self.flip(self.digits[j], d, size)
        return (self.n, self.w + (other - self.digits[j]) * 2**low)

    def x_peer(self):
        return ((1 - self.x) * 2 + self.core, self.w)

    def core_peer(self):
        return (self.x * 2 + 1 - self.core, self.w)

    def peers(self, stage):
        if stage == "x":
            return [self.x_peer()]
        if stage == "core":
            return [self.core_peer()]
        return [self.digit_peer(stage, d) for d in range(1, self.parts[stage][1])]

    def everyone(self):
        return [p for s in list(range(len(self.parts))) + ["x", "core"] for p in self.peers(s)]

    def greet(self):
        barrier = pltpu.get_barrier_semaphore()
        others = self.everyone()
        for peer in others:
            pl.semaphore_signal(barrier, inc=1, device_id=peer, device_id_type=pl.DeviceIdType.MESH)
        pl.semaphore_wait(barrier, len(others))


def stage_orders(mesh):
    count = len(wide_parts(mesh))
    early = list(range(count - 1)) + ["x", count - 1, "core"]
    late = list(range(count))[::-1] + ["x", "core"]
    return early, late


def stage_copies(mesh, order):
    parts = wide_parts(mesh)
    return sum(1 if isinstance(s, str) else parts[s][1] - 1 for s in order)


BF = jnp.bfloat16
F32 = jnp.float32
def dot(left, right):
    return lax.dot_general(left, right, (((1,), (0,)), ((), ())), preferred_element_type=F32)


def dot_nt(left, right):
    return lax.dot_general(left, right, (((1,), (1,)), ((), ())), preferred_element_type=F32)


def dot_tn(left, right):
    return lax.dot_general(left, right, (((0,), (0,)), ((), ())), preferred_element_type=F32)


def norm_parts(resid):
    middle = jnp.mean(resid, axis=-1, keepdims=True)
    centred = resid - middle
    spread = jnp.mean(centred * centred, axis=-1, keepdims=True)
    scale = lax.rsqrt(spread + EPSILON)
    return centred * scale, scale


def norm_back(grad, normal, scale, gain):
    scaled = grad * gain
    middle = jnp.mean(scaled, axis=-1, keepdims=True)
    along = jnp.mean(scaled * normal, axis=-1, keepdims=True)
    return (scaled - middle - normal * along) * scale


def down_sum(value):
    return jnp.sum(value, axis=0, keepdims=True)


QB = 64
WIN = 256
WIDER = 512
TOGETHER = 2
GROUP = 256
SIDE = GROUP // HD
VMEM_BYTES = 56 * 2**20


def head_masks(scale):
    rows = lax.broadcasted_iota(jnp.int32, (SIDE * QB, GROUP), 0) // QB
    lanes = lax.broadcasted_iota(jnp.int32, (SIDE * QB, GROUP), 1) // HD
    return jnp.where(rows == lanes, scale, 0.0).astype(BF)


def pick_heads(stacked):
    lanes = lax.broadcasted_iota(jnp.int32, (QB, GROUP), 1) // HD
    out = stacked[:QB]
    for h in range(1, SIDE):
        out = jnp.where(lanes == h, stacked[h * QB : (h + 1) * QB], out)
    return out


def stack_heads(block, mask):
    return jnp.concatenate([block] * SIDE, axis=0) * mask


class Block:
    def __init__(self, b, lo_s, hi_s, length):
        self.b = b
        self.q0 = pl.multiple_of(b * QB, QB)
        self.first = (lo_s[self.q0] // 16) * 16
        self.last = hi_s[self.q0 + QB - 1]
        self.span = self.last - self.first
        self.length = length

    def window(self, step, size):
        begin = self.first + step * size
        return begin, pl.multiple_of(jnp.minimum(begin, self.length - size), 16)


def for_blocks(count, make, together, alone, steps):
    def one(t, carry):
        blocks = [make(t * TOGETHER + i) for i in range(TOGETHER)]
        close = blocks[0].span < WIN
        for block in blocks[1:]:
            close = close & (block.span < WIN)

        @pl.when(close)
        def _():
            together(blocks)

        @pl.when(jnp.logical_not(close))
        def _():
            for block in blocks:

                @pl.when(block.span < WIDER)
                def _():
                    alone(block)

                @pl.when(block.span >= WIDER)
                def _():
                    steps(block)

        return carry

    lax.fori_loop(0, count // TOGETHER, one, 0)


def attend_bwd(q_ref, q_at, k_ref, k_at, v_at, do_ref, lo_s, hi_s, lo_rows, hi_rows, dq_ref, dq_at, dk_acc, dv_acc):
    length = k_ref.shape[0]
    factor = HD**-0.5
    q_mask = head_masks(factor)
    do_mask = head_masks(1.0)
    groups = range(do_ref.shape[1] // GROUP)
    dk_acc[...] = jnp.zeros_like(dk_acc)
    dv_acc[...] = jnp.zeros_like(dv_acc)

    def keys(g, start, size):
        return k_ref[pl.ds(start, size), pl.ds(k_at + g * GROUP, GROUP)]

    def values(g, start, size):
        return k_ref[pl.ds(start, size), pl.ds(v_at + g * GROUP, GROUP)]

    def query(block, g):
        return stack_heads(q_ref[pl.ds(block.q0, QB), pl.ds(q_at + g * GROUP, GROUP)], q_mask)

    def grad(block, g):
        return stack_heads(do_ref[pl.ds(block.q0, QB), pl.ds(g * GROUP, GROUP)], do_mask)

    def allowed(block, begin, start, size):
        low = lo_rows[pl.ds(block.b, 1), :]
        high = hi_rows[pl.ds(block.b, 1), :]
        places = start + lax.broadcasted_iota(jnp.int32, (size, SIDE * QB), 0)
        return (places >= jnp.maximum(low, begin)) & (places <= high)

    def scores(block, g, start, size, ok):
        return jnp.where(ok, dot_nt(keys(g, start, size), query(block, g)), NEGATIVE)

    def accumulate(g, start, size, dv, dk):
        rows = pl.ds(start, size)
        lanes = pl.ds(g * GROUP, GROUP)
        dv_acc[rows, lanes] += dv
        dk_acc[rows, lanes] += dk

    def store(block, g, stacked):
        dq = pick_heads(stacked) * factor
        dq_ref[pl.ds(block.q0, QB), pl.ds(dq_at + g * GROUP, GROUP)] = dq.astype(BF)

    def at_once(blocks, size):
        todo, score, slopes = [], [], []
        for block in blocks:
            begin, start = block.window(0, size)
            ok = allowed(block, begin, start, size)
            for g in groups:
                todo.append((block, g, start))
                score.append(scores(block, g, start, size, ok))
                slopes.append(dot_nt(values(g, start, size), grad(block, g)))
        raised = [jnp.exp(s - jnp.max(s, axis=0, keepdims=True)) for s in score]
        probs = [r * (1.0 / down_sum(r)) for r in raised]
        delta = [(p * (s - down_sum(p * s))).astype(BF) for p, s in zip(probs, slopes)]
        dv = [dot(p.astype(BF), grad(block, g)) for p, (block, g, _) in zip(probs, todo)]
        dk = [dot(d, query(block, g)) for d, (block, g, _) in zip(delta, todo)]
        dq = [dot_tn(d, keys(g, start, size)) for d, (_, g, start) in zip(delta, todo)]
        for i, (block, g, start) in enumerate(todo):
            store(block, g, dq[i])
            accumulate(g, start, size, dv[i], dk[i])

    def steps(block):
        count = block.span // WIN + 1
        for g in groups:

            def score_at(k):
                begin, start = block.window(k, WIN)
                return start, scores(block, g, start, WIN, allowed(block, begin, start, WIN))

            def stats(k, state):
                top, total = state
                _, score = score_at(k)
                higher = jnp.maximum(top, jnp.max(score, axis=0, keepdims=True))
                return higher, total * jnp.exp(top - higher) + down_sum(jnp.exp(score - higher))

            start_top = jnp.full((1, SIDE * QB), 2 * NEGATIVE, F32)
            top, total = lax.fori_loop(0, count, stats, (start_top, jnp.zeros((1, SIDE * QB), F32)))

            def probs_of(k):
                start, score = score_at(k)
                return start, jnp.exp(score - top) * (1.0 / total), dot_nt(values(g, start, WIN), grad(block, g))

            def centre(k, middle):
                _, probs, slopes = probs_of(k)
                return middle + down_sum(probs * slopes)

            middle = lax.fori_loop(0, count, centre, jnp.zeros((1, SIDE * QB), F32))

            def last_pass(k, out):
                start, probs, slopes = probs_of(k)
                delta = (probs * (slopes - middle)).astype(BF)
                accumulate(g, start, WIN, dot(probs.astype(BF), grad(block, g)), dot(delta, query(block, g)))
                return out + dot_tn(delta, keys(g, start, WIN))

            store(block, g, lax.fori_loop(0, count, last_pass, jnp.zeros((SIDE * QB, GROUP), F32)))

    for_blocks(
        q_ref.shape[0] // QB,
        lambda b: Block(b, lo_s, hi_s, length),
        lambda blocks: at_once(blocks, WIN),
        lambda block: at_once([block], WIDER),
        steps,
    )


def over_tiles(count, size, step):
    for t in range(count):
        step(t * size)


def gelu_parts(value):
    area = 0.5 * (1.0 + lax.erf(value * (0.5**0.5)))
    bell = jnp.exp(-0.5 * value * value) * 0.3989422804014327
    return value * area, area + value * bell


def ffn_both(
    r1_ref, o2_ref, cot_ref, w_co, w_in, w_down, par,
    out_ref, dr2_ref, do2_ref, g_in, g_down, g_co, vec_ref,
    r2_ref, h2_ref, z_ref, gp_ref, du_ref, dr3_ref, df_ref, da_ref,
):
    tokens, width = r1_ref.shape
    wide = w_in.shape[1]

    def resid_two(t):
        rows = pl.ds(t * 256, 256)
        hidden = norm_parts(r1_ref[rows, :])[0] * par[0:1, :] + par[3:4, :]
        resid = hidden * par[7:8, :] + dot(o2_ref[rows, :], w_co[...])
        r2_ref[rows, :] = resid
        h2_ref[rows, :] = (norm_parts(resid)[0] * par[1:2, :] + par[4:5, :]).astype(BF)

    for t in range(tokens // 256):
        resid_two(t)

    def up(at):
        lanes = pl.ds(at, 256)
        active, slope = gelu_parts(dot(h2_ref[...], w_in[:, lanes]))
        z_ref[:, lanes] = active.astype(BF)
        gp_ref[:, lanes] = slope

    over_tiles(wide // 256, 256, up)
    vec = [jnp.zeros((1, width), F32) for _ in range(6)]
    for t in range(tokens // 256):
        rows = pl.ds(t * 256, 256)
        hidden = norm_parts(r2_ref[rows, :])[0] * par[1:2, :] + par[4:5, :]
        resid = hidden * par[8:9, :] + dot(z_ref[rows, :], w_down[...])
        normal, scale = norm_parts(resid)
        out_ref[rows, :] = (normal * par[2:3, :] + par[5:6, :]).astype(BF)
        grad = cot_ref[rows, :].astype(F32)
        vec[0] += down_sum(grad * normal)
        vec[1] += down_sum(grad)
        back = norm_back(grad, normal, scale, par[2:3, :])
        vec[2] += down_sum(hidden * back)
        dr3_ref[rows, :] = back
        df_ref[rows, :] = back.astype(BF)

    def down(at):
        lanes = pl.ds(at, 256)
        grad = dot_nt(df_ref[...], w_down[pl.ds(at, 256), :])
        du_ref[:, lanes] = (grad * gp_ref[:, lanes]).astype(BF)

    over_tiles(wide // 256, 256, down)
    for t in range(tokens // 256):
        rows = pl.ds(t * 256, 256)
        grad = dr3_ref[rows, :] * par[8:9, :] + dot_nt(du_ref[rows, :], w_in[...])
        normal, scale = norm_parts(r2_ref[rows, :])
        vec[3] += down_sum(grad * normal)
        vec[4] += down_sum(grad)
        back = norm_back(grad, normal, scale, par[1:2, :])
        hidden = norm_parts(r1_ref[rows, :])[0] * par[0:1, :] + par[3:4, :]
        vec[5] += down_sum(hidden * back)
        dr2_ref[rows, :] = back
        low = back.astype(BF)
        da_ref[rows, :] = low
        do2_ref[rows, :] = dot_nt(low, w_co[...]).astype(BF)
    for k in range(6):
        vec_ref[k : k + 1, :] = vec[k]

    def grad_up(at):
        lanes = pl.ds(at, 256)
        g_in[:, lanes] = dot_tn(h2_ref[...], du_ref[:, lanes]).astype(BF)
        g_down[pl.ds(at, 256), :] = dot_tn(z_ref[:, lanes], df_ref[...]).astype(BF)

    over_tiles(wide // 256, 256, grad_up)

    def grad_co(at):
        lanes = pl.ds(at, 256)
        g_co[:, lanes] = dot_tn(o2_ref[...], da_ref[:, lanes]).astype(BF)

    over_tiles(width // 256, 256, grad_co)


def cross_backward(
    lo_s, hi_s, cq_ref, ckv_ref, do2_ref, lo_rows, hi_rows, mem_ref, tok_ref, r1_ref, dr2_ref, o1_ref, w_cq, w_out, par,
    dckv_ref, dr1_ref, do1_ref, g_cross, g_out, vec_ref,
    dq_ref, dk_acc, dv_acc, h1_ref, da_ref,
):
    tokens, width = r1_ref.shape
    attend_bwd(
        cq_ref, 0, ckv_ref, 0, width, do2_ref, lo_s, hi_s, lo_rows, hi_rows, dq_ref, 0, dk_acc, dv_acc
    )
    dckv_ref[:, :width] = dk_acc[...].astype(BF)
    dckv_ref[:, width:] = dv_acc[...].astype(BF)
    vec = [jnp.zeros((1, width), F32) for _ in range(3)]
    for t in range(tokens // 256):
        rows = pl.ds(t * 256, 256)
        grad = dr2_ref[rows, :] * par[7:8, :] + dot_nt(dq_ref[rows, :], w_cq[...])
        normal, scale = norm_parts(r1_ref[rows, :])
        h1_ref[rows, :] = (normal * par[0:1, :] + par[3:4, :]).astype(BF)
        vec[0] += down_sum(grad * normal)
        vec[1] += down_sum(grad)
        back = norm_back(grad, normal, scale, par[0:1, :])
        vec[2] += down_sum(tok_ref[rows, :].astype(F32) * back)
        dr1_ref[rows, :] = back
        low = back.astype(BF)
        da_ref[rows, :] = low
        do1_ref[rows, :] = dot_nt(low, w_out[...]).astype(BF)
    for k in range(3):
        vec_ref[k : k + 1, :] = vec[k]

    def grads(at):
        lanes = pl.ds(at, 256)
        g_out[:, lanes] = dot_tn(o1_ref[...], da_ref[:, lanes]).astype(BF)
        g_cross[:, lanes] = dot_tn(h1_ref[...], dq_ref[:, lanes]).astype(BF)

    over_tiles(width // 256, 256, grads)

    def pairs(at):
        g_cross[:, pl.ds(width + at, 256)] = dot_tn(mem_ref[...], dckv_ref[:, pl.ds(at, 256)]).astype(BF)

    over_tiles(2 * width // 256, 256, pairs)


def self_backward(
    lo_s, hi_s, qkv_ref, do1_ref, lo_rows, hi_rows, tok_ref, dqkv_ref, g_qkv, dk_acc, dv_acc
):
    width = tok_ref.shape[1]
    attend_bwd(
        qkv_ref, 0, qkv_ref, width, 2 * width, do1_ref, lo_s, hi_s, lo_rows, hi_rows, dqkv_ref, 0, dk_acc, dv_acc
    )
    dqkv_ref[:, width : 2 * width] = dk_acc[...].astype(BF)
    dqkv_ref[:, 2 * width :] = dv_acc[...].astype(BF)

    def grads(at):
        lanes = pl.ds(at, 256)
        g_qkv[:, lanes] = dot_tn(tok_ref[...], dqkv_ref[:, lanes]).astype(BF)

    over_tiles(3 * width // 256, 256, grads)


def last_grads(dqkv_ref, w_qkv, dr1_ref, dckv_ref, w_ckv, par, gt_ref, gm_ref):
    for t in range(gt_ref.shape[0] // 256):
        rows = pl.ds(t * 256, 256)
        gt_ref[rows, :] = dr1_ref[rows, :] * par[6:7, :] + dot_nt(dqkv_ref[rows, :], w_qkv[...])
        gm_ref[rows, :] = dot_nt(dckv_ref[rows, :], w_ckv[...])


def shaped(*dims, dtype=BF):
    return jax.ShapeDtypeStruct(dims, dtype)


def call(kernel, name, scalars, arrays, outs, scratch=(), flops=0):
    smem = [pl.BlockSpec(memory_space=pltpu.SMEM)] * len(scalars)
    vmem = [pl.BlockSpec(memory_space=pltpu.VMEM)] * len(arrays)
    moved = sum(a.size * a.dtype.itemsize for a in arrays) + sum(
        math.prod(o.shape) * jnp.dtype(o.dtype).itemsize for o in outs
    )
    return pl.pallas_call(
        kernel,
        out_shape=tuple(outs),
        in_specs=smem + vmem,
        out_specs=tuple(pl.BlockSpec(memory_space=pltpu.VMEM) for _ in outs),
        scratch_shapes=list(scratch),
        compiler_params=pltpu.CompilerParams(vmem_limit_bytes=VMEM_BYTES),
        cost_estimate=pl.CostEstimate(flops=flops, bytes_accessed=moved, transcendentals=0),
        name=name,
    )(*scalars, *arrays)


def head_rows(values):
    return jnp.tile(values.reshape(-1, QB), (1, SIDE))


STEP_US = 1.35
FIRST_CHUNKS, FIRST_LAG, LATER_LAG = 8, 3, 4


def run_plan(events, advance, work):
    now, whole, work = 0.0, set(), list(work)

    def do_work(until):
        nonlocal now
        while work and set(work[0][0]) <= whole and now < until:
            _, us, run = work.pop(0)
            run()
            now += us

    for time, k, s in events:
        do_work(time)
        now = max(now, time)
        if advance(k, s):
            whole.add(k)
    do_work(float("inf"))
    assert not work


DENSE = 128


class Gather:
    def __init__(self, place, chunks, shards, fulls, send, recv, own):
        self.place, self.chunks, self.shards, self.fulls = place, chunks, shards, fulls
        self.send, self.recv, self.used, self.sent = send, recv, 0, []
        self.states = []
        for k, chunk in enumerate(chunks):
            src, target = self.views(chunk, [])
            mine = pltpu.make_async_copy(src, target, own.at[k])
            mine.start()
            self.states.append({"done": [], "copies": [], "order": chunk[6], "mine": mine})

    def views(self, chunk, done):
        which, row, rows, col, cols, split, _ = chunk
        place = self.place
        quarter, half = cols // 4, cols // 2
        lanes = pl.ds(col, cols)
        if split:
            lanes = pl.ds(pl.multiple_of(col + place.core * half, 128), half)
            if "x" not in done:
                lanes = pl.ds(pl.multiple_of(col + place.core * half + place.x * quarter, 128), quarter)
        spot = tuple(slice(None) if j in done else place.digits[j] for j in range(len(place.parts)))
        target = self.fulls[which].at[spot + (pl.ds(row, rows), lanes)]
        if done:
            return target, target
        return self.shards[which].at[pl.ds(row, rows), lanes], target

    def advance(self, k, s):
        state = self.states[k]
        stages = len(state["order"])
        if s > stages:
            return False
        if s == 1:
            state["mine"].wait()
        for copy in state["copies"]:
            copy.wait_recv()
        state["copies"] = []
        if s == stages:
            return True
        stage = state["order"][s]
        src, target = self.views(self.chunks[k], state["done"])
        for peer in self.place.peers(stage):
            at = self.used
            self.used += 1
            copy = pltpu.make_async_remote_copy(
                src_ref=src, dst_ref=target, send_sem=self.send.at[at], recv_sem=self.recv.at[at],
                device_id=peer, device_id_type=pl.DeviceIdType.MESH,
            )
            copy.start()
            state["copies"].append(copy)
            self.sent.append(copy)
        state["done"] = state["done"] + [stage]
        return False

    def events(self):
        events = []
        for k, chunk in enumerate(self.chunks):
            lag = FIRST_LAG if k < FIRST_CHUNKS else LATER_LAG
            events += [(STEP_US * (k + s * lag), k, s) for s in range(len(chunk[6]) + 1)]
        return sorted(events, key=lambda e: (e[0], e[1]))

    def finish(self):
        for copy in self.sent:
            copy.wait_send()


def segment_ranges(own, far, out):
    width = own.shape[1]
    numbers = lax.broadcasted_iota(jnp.int32, (SEGS, width), 0).astype(F32)
    mine = (own == numbers).astype(F32)

    def counted(hit):
        return jnp.sum(mine * jnp.sum(hit.astype(F32), axis=1, keepdims=True), axis=0, keepdims=True)

    out[0:1, :] = counted(own < numbers).astype(jnp.int32)
    out[1:2, :] = counted(far < numbers).astype(jnp.int32)
    out[2:3, :] = (counted(far <= numbers) - 1.0).astype(jnp.int32)


def dense_attend(q_ref, q_at, q0, k_ref, k_at, v_at, limit, allowed, o_ref):
    rows = lax.broadcasted_iota(jnp.int32, (SIDE * DENSE, GROUP), 0) // DENSE
    lanes = lax.broadcasted_iota(jnp.int32, (SIDE * DENSE, GROUP), 1) // HD
    mask = jnp.where(rows == lanes, HD**-0.5, 0.0).astype(BF)
    shift = jnp.where(allowed, 0.0, NEGATIVE)
    shift = jnp.concatenate([shift] * SIDE, axis=0)
    places = lax.broadcasted_iota(jnp.int32, (DENSE, GROUP), 1) // HD
    for g in range(o_ref.shape[1] // GROUP):
        block = q_ref[pl.ds(q0, DENSE), pl.ds(q_at + g * GROUP, GROUP)]
        query = jnp.concatenate([block] * SIDE, axis=0) * mask
        score = dot_nt(query, k_ref[pl.ds(0, limit), pl.ds(k_at + g * GROUP, GROUP)]) + shift
        raised = jnp.exp(score - jnp.max(score, axis=-1, keepdims=True))
        total = jnp.sum(raised, axis=-1, keepdims=True)
        mixed = dot(raised.astype(BF), k_ref[pl.ds(0, limit), pl.ds(v_at + g * GROUP, GROUP)]) * (1.0 / total)
        out = mixed[:DENSE]
        for h in range(1, SIDE):
            out = jnp.where(places == h, mixed[h * DENSE : (h + 1) * DENSE], out)
        o_ref[pl.ds(q0, DENSE), pl.ds(g * GROUP, GROUP)] = out.astype(BF)


def front_kernel(mesh, chunks, count, sizes, *refs):
    shards, rest = refs[:count], refs[count:]
    tok_in, mem_in, own_seg, far_seg = rest[:4]
    rest = rest[4:]
    fulls, rest = rest[:count], rest[count:]
    outs, rest = rest[:8], rest[8:]
    (qkv, o1, r1, cq, ckv, o2, ranges, par, tok, mem, w_qkv, w_out, w_cq, w_ckv, small, seg_col) = rest[:16]
    send, recv, own, load, load_in, store = rest[16:]
    place = Place(mesh)
    place.greet()
    gather = Gather(place, chunks, shards, fulls, send, recv, own)
    taken = [
        pltpu.make_async_copy(tok_in, tok, load_in.at[0]),
        pltpu.make_async_copy(mem_in, mem, load_in.at[1]),
    ]
    for copy in taken:
        copy.start()
    length, width = tok.shape
    held = {0: w_qkv, 1: w_out, 2: w_cq, 3: w_ckv, count - 1: small}
    loads = {}

    def fetch(k):
        which, row, rows, col, cols, split, _ = chunks[k]
        if which not in held:
            return
        loads[k] = pltpu.make_async_copy(
            fulls[which].at[..., pl.ds(col, cols)], held[which].at[..., pl.ds(col, cols)], load.at[k]
        )
        loads[k].start()

    def chunk_of(which, col):
        return [k for k, c in enumerate(chunks) if c[0] == which and c[3] == col][0]

    def weight(ref, col, cols):
        flat = ref.shape[:-2]
        return ref[..., pl.ds(col, cols)].reshape(math.prod(flat) * ref.shape[-2], cols)

    def give(at, ref):
        copy = pltpu.make_async_copy(ref, outs[at], store.at[at])
        copy.start()
        given.append(copy)

    given = []

    def project(t):
        def run():
            loads[chunk_of(0, t * 512)].wait()
            if t == 0:
                taken[0].wait()
            qkv[:, pl.ds(t * 512, 512)] = dot(tok[...], weight(w_qkv, t * 512, 512)).astype(BF)
            if t == 2:
                give(0, qkv)

        return run

    def columns():
        own_row = own_seg[...].astype(F32)
        segment_ranges(own_row, far_seg[...].astype(F32), ranges)
        give(6, ranges)
        seg_col[...] = jnp.broadcast_to(own_row, (8, length)).T

    def attend_self(b):
        def run():
            q0, limit = b * DENSE, (b + 1) * DENSE
            same = seg_col[pl.ds(q0, DENSE), 0:1] == own_seg[:, pl.ds(0, limit)].astype(F32)
            key = lax.broadcasted_iota(jnp.int32, (DENSE, limit), 1)
            query = q0 + lax.broadcasted_iota(jnp.int32, (DENSE, limit), 0)
            dense_attend(qkv, 0, q0, qkv, width, 2 * width, limit, same & (key <= query), o1)
            if limit == length:
                give(1, o1)

        return run

    def pairs(t):
        def run():
            loads[chunk_of(3, t * 512)].wait()
            if t == 0:
                taken[1].wait()
            ckv[:, pl.ds(t * 512, 512)] = dot(mem[...], weight(w_ckv, t * 512, 512)).astype(BF)
            if t == 1:
                give(4, ckv)

        return run

    def params():
        loads[chunk_of(count - 1, 0)].wait()
        each = sizes[count - 1]
        flat = small[...].reshape(math.prod(small.shape[:-2]), small.shape[-2], small.shape[-1])
        par[...] = jnp.concatenate([flat[w, :, :each].astype(F32) for w in range(flat.shape[0])], axis=1)
        give(7, par)

    def hidden(t):
        def run():
            if t == 0:
                loads[chunk_of(1, 0)].wait()
                loads[chunk_of(2, 0)].wait()
            rows = pl.ds(t * 256, 256)
            resid = tok[rows, :].astype(F32) * par[6:7, :] + dot(o1[rows, :], weight(w_out, 0, width))
            r1[rows, :] = resid
            normal, _ = norm_parts(resid)
            low = (normal * par[0:1, :] + par[3:4, :]).astype(BF)
            cq[rows, :] = dot(low, weight(w_cq, 0, width)).astype(BF)
            if (t + 1) * 256 == length:
                give(2, r1)
                give(3, cq)

        return run

    def attend_cross(b):
        def run():
            q0 = b * DENSE
            same = seg_col[pl.ds(q0, DENSE), 0:1] == far_seg[...].astype(F32)
            dense_attend(cq, 0, q0, ckv, 0, width, length, same, o2)
            if q0 + DENSE == length:
                give(5, o2)

        return run

    work = [((), 0.5, columns)]
    work += [((chunk_of(0, t * 512),), 0.8, project(t)) for t in range(3)]
    work += [((), 0.2 + 0.15 * b, attend_self(b)) for b in range(length // DENSE)]
    work += [((chunk_of(count - 1, 0),), 0.2, params)]
    work += [((chunk_of(1, 0), chunk_of(2, 0)), 0.9, hidden(t)) for t in range(length // 256)]
    work += [((chunk_of(3, t * 512),), 0.8, pairs(t)) for t in range(2)]
    work += [((), 1.6, attend_cross(b)) for b in range(length // DENSE)]

    def advance(k, s):
        whole = gather.advance(k, s)
        if whole:
            fetch(k)
        return whole

    run_plan(gather.events(), advance, work)
    gather.finish()
    for copy in given:
        copy.wait()


def front(mesh, shards, tokens, memory, own_seg, far_seg, rows, collective):
    early, late = stage_orders(mesh)
    digits = tuple(size for _, size in wide_parts(mesh))
    small_order = [s for s in early if not isinstance(s, str)]
    count = len(shards)
    length, width = tokens.shape
    chunks = []
    for which in [0, count - 1] + list(range(1, count - 1)):
        high, cols = shards[which].shape
        if cols < 512:
            chunks.append((which, 0, high, 0, cols, False, small_order))
            continue
        cut = max(1, high // 64)
        for r in range(cut):
            for c in range(cols // 512):
                order = late if len(chunks) % 8 in LATE_CHUNKS else early
                chunks.append((which, r * (high // cut), high // cut, c * 512, 512, True, order))
    copies = sum(stage_copies(mesh, c[6]) for c in chunks)
    fulls = tuple(jax.ShapeDtypeStruct(digits + s.shape, s.dtype) for s in shards)
    made = (
        shaped(length, 3 * width), shaped(length, width), shaped(length, width, dtype=F32), shaped(length, width),
        shaped(length, 2 * width), shaped(length, width), shaped(8, length, dtype=jnp.int32),
        shaped(16, width, dtype=F32),
    )
    vm = pltpu.VMEM
    kept = [0, 1, 2, 3, count - 1]
    results = pl.pallas_call(
        functools.partial(front_kernel, mesh, chunks, count, [s.shape[0] for s in shards[:-1]] + [rows]),
        out_shape=fulls + made,
        in_specs=[pl.BlockSpec(memory_space=pl.ANY)] * (count + 2) + [pl.BlockSpec(memory_space=vm)] * 2,
        out_specs=tuple(pl.BlockSpec(memory_space=pl.ANY) for _ in fulls + made),
        scratch_shapes=[vm(m.shape, m.dtype) for m in made]
        + [vm(tokens.shape, BF), vm(memory.shape, BF)]
        + [vm(fulls[k].shape, BF) for k in kept]
        + [
            vm((length, 8), F32),
            pltpu.SemaphoreType.DMA((copies,)),
            pltpu.SemaphoreType.DMA((copies,)),
            pltpu.SemaphoreType.DMA((len(chunks),)),
            pltpu.SemaphoreType.DMA((len(chunks),)),
            pltpu.SemaphoreType.DMA((2,)),
            pltpu.SemaphoreType.DMA((len(made),)),
        ],
        compiler_params=pltpu.CompilerParams(
            collective_id=collective, has_side_effects=True, vmem_limit_bytes=VMEM_BYTES
        ),
        name="front",
    )(*shards, tokens, memory, own_seg.reshape(1, length), far_seg.reshape(1, length))
    return [full.reshape((-1, full.shape[-1])) for full in results[:count]], results[count:]


LATE_CHUNKS = (1, 4, 6)


def layer(tokens, memory, cotangent, weights, made):
    w_qkv, w_out, w_cq, w_ckv, w_co, w_in, w_down, _ = weights
    qkv, o1, r1, cq, ckv, o2, ranges, par = made
    length, width = tokens.shape
    ff = w_in.shape[1]
    own_lo, far_lo, far_hi = ranges[0], ranges[1], ranges[2]
    own_hi = jnp.arange(length, dtype=jnp.int32)
    vm = pltpu.VMEM
    g = 10**9
    out, dr2, do2, g_in, g_down, g_co, vec_two = call(
        ffn_both, "ffn_both", (), (r1, o2, cotangent, w_co, w_in, w_down, par),
        (
            shaped(length, width), shaped(length, width, dtype=F32), shaped(length, width),
            shaped(width, ff), shaped(ff, width), shaped(width, width), shaped(8, width, dtype=F32),
        ),
        (
            vm((length, width), F32), vm((length, width), BF), vm((length, ff), BF), vm((length, ff), F32),
            vm((length, ff), BF), vm((length, width), F32), vm((length, width), BF), vm((length, width), BF),
        ),
        flops=20 * g,
    )
    dckv, dr1, do1, g_cross, g_out, vec_one = call(
        cross_backward, "cross_backward", (far_lo, far_hi),
        (cq, ckv, do2, head_rows(far_lo), head_rows(far_hi), memory, tokens, r1, dr2, o1, w_cq, w_out, par),
        (
            shaped(length, 2 * width), shaped(length, width, dtype=F32), shaped(length, width),
            shaped(width, 3 * width), shaped(width, width), shaped(8, width, dtype=F32),
        ),
        (
            vm((length, width), BF), vm((length, width), F32), vm((length, width), F32),
            vm((length, width), BF), vm((length, width), BF),
        ),
        flops=20 * g,
    )
    dqkv, g_qkv = call(
        self_backward, "self_backward", (own_lo, own_hi),
        (qkv, do1, head_rows(own_lo), head_rows(own_hi), tokens),
        (shaped(length, 3 * width), shaped(width, 3 * width)),
        (vm((length, width), F32), vm((length, width), F32)),
        flops=15 * g,
    )
    grad_tokens, grad_memory = call(
        last_grads, "last_grads", (), (dqkv, w_qkv, dr1, dckv, w_ckv, par),
        (shaped(length, width, dtype=F32), shaped(length, width, dtype=F32)), flops=3 * g,
    )
    vec = jnp.concatenate([vec_one[:3], vec_two[3:6], vec_two[:3]], axis=0)
    return out, grad_tokens, grad_memory, g_in, g_down, g_co, g_cross, g_out, g_qkv, vec


REDUCE_LAG = 4


def reduce_orders(mesh):
    digits = list(range(len(wide_parts(mesh))))[::-1]
    return ["core", "x"] + digits, ["core", digits[0], "x"] + digits[1:]


def reduce_kernel(mesh, chunks, count, *refs):
    grads, sums = refs[:count], refs[count : 2 * count]
    held = refs[2 * count : 2 * count + len(chunks)]
    pool = list(refs[2 * count + len(chunks) : -3])
    send, recv, own = refs[-3:]
    place = Place(mesh)
    place.greet()
    bits = {"core": place.core, "x": place.x}
    used = [0]
    sent = []

    def ship(src, target, peer):
        at = used[0]
        used[0] += 1
        copy = pltpu.make_async_remote_copy(
            src_ref=src, dst_ref=target, send_sem=send.at[at], recv_sem=recv.at[at],
            device_id=peer, device_id_type=pl.DeviceIdType.MESH,
        )
        copy.start()
        sent.append(copy)
        return copy

    def digit_view(ref, j, index, done):
        spot = [slice(None)] * len(place.parts)
        spot[j] = pl.ds(index, 1)
        return ref.at[tuple(spot)]

    def lanes_view(ref, start, size):
        return ref.at[..., pl.ds(pl.multiple_of(start, 128), size)]

    states = []
    for k, (which, sub, col, cols, order, split) in enumerate(chunks):
        source = grads[which].at[..., sub, :, pl.ds(col, cols)]
        if split:
            half = cols // 2
            wanted = lanes_view(grads[which].at[..., sub, :, :], col + place.core * half, half)
            other = lanes_view(grads[which].at[..., sub, :, :], col + (1 - place.core) * half, half)
        else:
            wanted = other = source
        mine = pltpu.make_async_copy(wanted, held[k], own.at[k])
        mine.start()
        states.append({"mine": mine, "other": other, "copies": [], "bufs": [], "cur": held[k], "sel": None})

    def finish_stage(k, stage):
        state = states[k]
        split = chunks[k][5]
        for copy in state["copies"]:
            copy.wait_recv()
        cur = state["cur"]
        if stage == "core" or (stage == "x" and not split):
            if stage == "core":
                state["mine"].wait()
            value = cur[...].astype(F32)
        elif stage == "x":
            half = cur.shape[-1] // 2
            value = lanes_view(cur, place.x * half, half)[...].astype(F32)
        else:
            value = digit_view(cur, stage, place.digits[stage], None)[...].astype(F32)
        for buf in state["bufs"]:
            value = value + buf[...].astype(F32)
        total = pool.pop(0)
        total[...] = value.astype(BF)
        state["cur"] = total
        state["copies"], state["bufs"] = [], []

    def start_stage(k, stage):
        state = states[k]
        split = chunks[k][5]
        cur = state["cur"]
        if stage == "core":
            buf = pool.pop(0)
            state["copies"] = [ship(state["other"], buf, place.core_peer())]
            state["bufs"] = [buf]
        elif stage == "x":
            buf = pool.pop(0)
            src = cur
            if split:
                half = cur.shape[-1] // 2
                src = lanes_view(cur, (1 - place.x) * half, half)
            state["copies"] = [ship(src, buf, place.x_peer())]
            state["bufs"] = [buf]
        else:
            size = place.parts[stage][1]
            for d in range(1, size):
                buf = pool.pop(0)
                src = digit_view(cur, stage, place.flip(place.digits[stage], d, size), None)
                state["copies"].append(ship(src, buf, place.digit_peer(stage, d)))
                state["bufs"].append(buf)

    def out_view(k, size):
        which, sub, col, cols, order, split = chunks[k]
        start = col
        if size < cols:
            start = start + place.core * (cols // 2)
        if size < cols // 2:
            start = start + place.x * (cols // 4)
        rows = states[k]["cur"].shape[-2]
        if isinstance(start, int):
            return sums[which].at[pl.ds(sub * rows, rows), pl.ds(start, size)]
        return sums[which].at[pl.ds(sub * rows, rows), pl.ds(pl.multiple_of(start, 128), size)]

    def advance(k, s):
        order, split = chunks[k][4], chunks[k][5]
        state = states[k]
        stages = len(order)
        if s > 0 and s <= stages:
            finish_stage(k, order[s - 1])
        if s < stages:
            start_stage(k, order[s])
        elif s == stages:
            cols = chunks[k][3]
            size = cols // 4 if split else cols
            view = out_view(k, size)
            view[...] = state["cur"][...].reshape(view.shape)
            if split:
                state["copies"] = [ship(view, view, place.x_peer())]
        elif s == stages + 1 and split:
            for copy in state["copies"]:
                copy.wait_recv()
            view = out_view(k, chunks[k][3] // 2)
            state["copies"] = [ship(view, view, place.core_peer())]
        elif s == stages + 2 and split:
            for copy in state["copies"]:
                copy.wait_recv()

    steps = max(len(c[4]) for c in chunks) + 3
    for t in range(len(chunks) + steps * REDUCE_LAG):
        for s in reversed(range(steps)):
            k = t - s * REDUCE_LAG
            if 0 <= k < len(chunks):
                advance(k, s)
    for copy in sent:
        copy.wait_send()


def buffers_of(mesh, order, split, shape):
    parts = wide_parts(mesh)
    per_stage = []
    shape = list(shape)
    for stage in order:
        if stage == "x" and split:
            shape[-1] //= 2
        arrived = 1
        if not isinstance(stage, str):
            shape[stage] = 1
            arrived = parts[stage][1] - 1
        per_stage.append((tuple(shape), arrived))
    return per_stage


def reduce_grads(mesh, grads, collective):
    early, late = reduce_orders(mesh)
    digits = tuple(size for _, size in wide_parts(mesh))
    wide = mesh.shape["wide"]
    views, chunks, sums = [], [], []
    for which, grad in enumerate(grads):
        rows, cols = grad.shape[0] // wide, grad.shape[1]
        sub = rows * wide // cols if cols == 512 and rows * wide > 512 else 1
        views.append(grad.reshape(digits + (sub, rows // sub, cols)))
        sums.append(jax.ShapeDtypeStruct((rows, cols), BF))
        if cols < 512:
            chunks.append((which, 0, 0, cols, early, False))
            continue
        for j in range(sub):
            for c in range(cols // 512):
                chunks.append((which, j, c * 512, 512, late if len(chunks) % 2 else early, True))
    held, plan = [], []
    for which, sub, col, cols, order, split in chunks:
        shape = digits + (views[which].shape[-2], cols // 2 if split else cols)
        held.append(pltpu.VMEM(shape, BF))
        plan.append(buffers_of(mesh, order, split, shape))
    pool = []
    steps = max(len(c[4]) for c in chunks) + 3
    for t in range(len(chunks) + steps * REDUCE_LAG):
        for s in reversed(range(steps)):
            k = t - s * REDUCE_LAG
            if 0 <= k < len(chunks):
                if 0 < s <= len(plan[k]):
                    pool.append(pltpu.VMEM(plan[k][s - 1][0], BF))
                if s < len(plan[k]):
                    pool += [pltpu.VMEM(plan[k][s][0], BF)] * plan[k][s][1]
    copies = sum(sum(n for _, n in p) + 2 for p in plan)
    return pl.pallas_call(
        functools.partial(reduce_kernel, mesh, chunks, len(grads)),
        out_shape=tuple(sums),
        in_specs=[pl.BlockSpec(memory_space=pl.ANY)] * len(grads),
        out_specs=tuple(pl.BlockSpec(memory_space=pltpu.VMEM) for _ in grads),
        scratch_shapes=held + pool + [
            pltpu.SemaphoreType.DMA((copies,)),
            pltpu.SemaphoreType.DMA((copies,)),
            pltpu.SemaphoreType.DMA((len(chunks),)),
        ],
        compiler_params=pltpu.CompilerParams(
            collective_id=collective, has_side_effects=True, vmem_limit_bytes=VMEM_BYTES
        ),
        name="reduce_grads",
    )(*views)


def widen_kernel(count, *refs):
    for src, out in zip(refs[:count], refs[count:]):
        out[...] = src[...].astype(F32)


def body(
    mesh,
    tokens,
    memory,
    target_segments,
    memory_segments,
    self_qkv,
    self_out,
    cross_q,
    cross_kv,
    cross_out,
    ffn_in,
    ffn_out,
    norm_gain,
    norm_bias,
    omega,
    cotangent,
):
    wide = mesh.shape["wide"]
    rows = self_qkv.shape[0]
    width = rows * wide
    small = jnp.concatenate([norm_gain, norm_bias, omega], axis=1).T
    small = jnp.pad(small, ((0, 7), (0, 128 - rows)))
    weights, made = front(
        mesh, (self_qkv, self_out, cross_q, cross_kv, cross_out, ffn_in, ffn_out, small),
        tokens, memory, target_segments, memory_segments, rows, 1,
    )
    output, grad_tokens, grad_memory, g_in, g_down, g_co, g_cross, g_out, g_qkv, vec = layer(
        tokens, memory, cotangent, weights, made
    )
    vectors = vec.astype(BF).reshape(9, wide, rows).transpose(1, 0, 2)
    vectors = jnp.pad(vectors, ((0, 0), (0, 7), (0, 128 - rows))).reshape(wide * 16, 128)
    sums = reduce_grads(mesh, (g_in, g_down, g_co, g_cross, g_out, g_qkv, vectors), 2)
    s_in, s_down, s_co, s_cross, s_out, s_qkv = call(
        functools.partial(widen_kernel, 6), "widen", (), sums[:6], tuple(shaped(*s.shape, dtype=F32) for s in sums[:6])
    )
    small = sums[6][:9, :rows].astype(jnp.float32).reshape(3, 3, rows).transpose(1, 2, 0)
    summed = (s_qkv, s_out, s_cross[:, :width], s_cross[:, width:], s_co, s_in, s_down, small[0], small[1], small[2])
    return (output, grad_tokens, grad_memory) + summed


def solution(mesh):
    in_specs = (
        P(("narrow", "wide"), None),
        P(("narrow", "wide"), None),
        P(("narrow", "wide")),
        P(("narrow", "wide")),
        P("wide", None),
        P("wide", None),
        P("wide", None),
        P("wide", None),
        P("wide", None),
        P("wide", None),
        P("wide", None),
        P("wide", None),
        P("wide", None),
        P("wide", None),
        P(("narrow", "wide"), None),
    )
    out_specs = (
        P(("narrow", "wide"), None),
        P(("narrow", "wide"), None),
        P(("narrow", "wide"), None),
        P("wide", None),
        P("wide", None),
        P("wide", None),
        P("wide", None),
        P("wide", None),
        P("wide", None),
        P("wide", None),
        P("wide", None),
        P("wide", None),
        P("wide", None),
    )
    return jax.shard_map(functools.partial(body, mesh), mesh=mesh, in_specs=in_specs, out_specs=out_specs, check_vma=False)
```

```python
import functools
import itertools
import math

import jax
import jax.numpy as jnp
from jax import lax
from jax.experimental import pallas as pl
from jax.experimental.pallas import tpu as pltpu
from jax.sharding import PartitionSpec as P

HD = 64

EPSILON = 1e-05
NEGATIVE = -1000000000.0
SEGS = 32


def wide_parts(mesh):
    bits = mesh.shape["wide"].bit_length() - 1
    low = [(0, 1)] if bits % 2 else []
    low = low + [(at, 2) for at in range(bits % 2, bits, 2)]
    return [(at, 2**count) for at, count in low[::-1]]


class Place:
    def __init__(self, mesh):
        self.parts = wide_parts(mesh)
        self.n = lax.axis_index("narrow")
        self.w = lax.axis_index("wide")
        self.core = lax.rem(self.n, 2)
        self.x = lax.div(self.n, 2)
        self.digits = [lax.rem(lax.div(self.w, 2**low), size) for low, size in self.parts]

    def flip(self, value, d, size):
        out = 0
        bit = 1
        while bit < size:
            digit = lax.rem(lax.div(value, bit), 2)
            out = out + bit * (1 - digit if d & bit else digit)
            bit *= 2
        return out

    def digit_peer(self, j, d):
        low, size = self.parts[j]
        other = self.flip(self.digits[j], d, size)
        return (self.n, self.w + (other - self.digits[j]) * 2**low)

    def x_peer(self):
        return ((1 - self.x) * 2 + self.core, self.w)

    def core_peer(self):
        return (self.x * 2 + 1 - self.core, self.w)

    def peers(self, stage):
        if stage == "x":
            return [self.x_peer()]
        if stage == "core":
            return [self.core_peer()]
        return [self.digit_peer(stage, d) for d in range(1, self.parts[stage][1])]

    def wide_peer(self, offsets):
        w = 0
        for (low, size), digit, d in zip(self.parts, self.digits, offsets):
            w = w + self.flip(digit, d, size) * 2**low
        return (self.n, w)

    def greet(self, whole=False):
        others = [self.x_peer(), self.core_peer()]
        if whole:
            choices = itertools.product(*[range(size) for _, size in self.parts])
            others += [self.wide_peer(d) for d in choices if any(d)]
        else:
            others += [p for j in range(len(self.parts)) for p in self.peers(j)]
        barrier = pltpu.get_barrier_semaphore()
        for peer in others:
            pl.semaphore_signal(barrier, inc=1, device_id=peer, device_id_type=pl.DeviceIdType.MESH)
        pl.semaphore_wait(barrier, len(others))


def stage_orders(mesh):
    count = len(wide_parts(mesh))
    early = list(range(count - 1)) + ["x", count - 1, "core"]
    late = list(range(count))[::-1] + ["x", "core"]
    return early, late


def stage_copies(mesh, order):
    parts = wide_parts(mesh)
    return sum(1 if isinstance(s, str) else parts[s][1] - 1 for s in order)


BF = jnp.bfloat16
F32 = jnp.float32
def dot(left, right):
    return lax.dot_general(left, right, (((1,), (0,)), ((), ())), preferred_element_type=F32)


def dot_nt(left, right):
    return lax.dot_general(left, right, (((1,), (1,)), ((), ())), preferred_element_type=F32)


def dot_tn(left, right):
    return lax.dot_general(left, right, (((0,), (0,)), ((), ())), preferred_element_type=F32)


def norm_parts(resid):
    middle = jnp.mean(resid, axis=-1, keepdims=True)
    centred = resid - middle
    spread = jnp.mean(centred * centred, axis=-1, keepdims=True)
    scale = lax.rsqrt(spread + EPSILON)
    return centred * scale, scale


def norm_back(grad, normal, scale, gain):
    scaled = grad * gain
    middle = jnp.mean(scaled, axis=-1, keepdims=True)
    along = jnp.mean(scaled * normal, axis=-1, keepdims=True)
    return (scaled - middle - normal * along) * scale


def down_sum(value):
    return jnp.sum(value, axis=0, keepdims=True)


QB = 64
WIN = 256
WIDER = 512
GROUP = 256
SIDE = GROUP // HD
VMEM_BYTES = 56 * 2**20


def head_masks(scale):
    rows = lax.broadcasted_iota(jnp.int32, (SIDE * QB, GROUP), 0) // QB
    lanes = lax.broadcasted_iota(jnp.int32, (SIDE * QB, GROUP), 1) // HD
    return jnp.where(rows == lanes, scale, 0.0).astype(BF)


def pick_heads(stacked):
    lanes = lax.broadcasted_iota(jnp.int32, (QB, GROUP), 1) // HD
    out = stacked[:QB]
    for h in range(1, SIDE):
        out = jnp.where(lanes == h, stacked[h * QB : (h + 1) * QB], out)
    return out


def stack_heads(block, mask):
    return jnp.concatenate([block] * SIDE, axis=0) * mask


class Block:
    def __init__(self, b, ranges_s, length):
        self.b = b
        self.q0 = pl.multiple_of(b * QB, QB)
        self.first = (ranges_s[1, self.q0] // 16) * 16
        self.last = ranges_s[2, self.q0 + QB - 1]
        self.span = self.last - self.first
        self.length = length

    def window(self, step, size):
        begin = self.first + step * size
        return begin, pl.multiple_of(jnp.minimum(begin, self.length - size), 16)


def for_blocks(count, at_a_time, make, together, alone, steps):
    def one(t, carry):
        blocks = [make(t * at_a_time + i) for i in range(at_a_time)]
        close = blocks[0].span < WIN
        for block in blocks[1:]:
            close = close & (block.span < WIN)

        @pl.when(close)
        def _():
            together(blocks)

        @pl.when(jnp.logical_not(close))
        def _():
            for block in blocks:

                @pl.when(block.span < WIDER)
                def _():
                    alone(block)

                @pl.when(block.span >= WIDER)
                def _():
                    steps(block)

        return carry

    lax.fori_loop(0, count // at_a_time, one, 0)


def attend_fwd(q_ref, q_at, k_ref, k_at, v_at, ranges_s, cols_ref, o_ref):
    length = k_ref.shape[0]
    mask = head_masks(HD**-0.5)
    groups = range(o_ref.shape[1] // GROUP)

    def allowed(block, begin, start, size):
        low = cols_ref[pl.ds(block.q0, QB), 1:2]
        high = cols_ref[pl.ds(block.q0, QB), 2:3]
        places = start + lax.broadcasted_iota(jnp.int32, (QB, size), 1)
        ok = (places >= jnp.maximum(low, begin)) & (places <= high)
        return jnp.concatenate([ok] * SIDE, axis=0)

    def scores(block, g, start, size, ok):
        query = stack_heads(q_ref[pl.ds(block.q0, QB), pl.ds(q_at + g * GROUP, GROUP)], mask)
        keys = k_ref[pl.ds(start, size), pl.ds(k_at + g * GROUP, GROUP)]
        return jnp.where(ok, dot_nt(query, keys), NEGATIVE)

    def values(g, start, size):
        return k_ref[pl.ds(start, size), pl.ds(v_at + g * GROUP, GROUP)]

    def store(block, g, stacked):
        o_ref[pl.ds(block.q0, QB), pl.ds(g * GROUP, GROUP)] = pick_heads(stacked).astype(BF)

    def at_once(blocks, size):
        todo = []
        for block in blocks:
            begin, start = block.window(0, size)
            ok = allowed(block, begin, start, size)
            todo += [(block, g, start, scores(block, g, start, size, ok)) for g in groups]
        tops = [jnp.max(score, axis=-1, keepdims=True) for _, _, _, score in todo]
        raised = [jnp.exp(score - top) for (_, _, _, score), top in zip(todo, tops)]
        totals = [jnp.sum(r, axis=-1, keepdims=True) for r in raised]
        weights = [(r * (1.0 / total)).astype(BF) for r, total in zip(raised, totals)]
        mixed = [dot(w, values(g, start, size)) for w, (_, g, start, _) in zip(weights, todo)]
        for m, (block, g, _, _) in zip(mixed, todo):
            store(block, g, m)

    def steps(block):
        count = block.span // WIN + 1
        for g in groups:

            def score_at(k):
                begin, start = block.window(k, WIN)
                return start, scores(block, g, start, WIN, allowed(block, begin, start, WIN))

            def stats(k, state):
                top, total = state
                _, score = score_at(k)
                higher = jnp.maximum(top, jnp.max(score, axis=-1, keepdims=True))
                raised = jnp.sum(jnp.exp(score - higher), axis=-1, keepdims=True)
                return higher, total * jnp.exp(top - higher) + raised

            start_top = jnp.full((SIDE * QB, 1), 2 * NEGATIVE, F32)
            top, total = lax.fori_loop(0, count, stats, (start_top, jnp.zeros((SIDE * QB, 1), F32)))

            def mix(k, out):
                start, score = score_at(k)
                weights = jnp.exp(score - top) * (1.0 / total)
                return out + dot(weights.astype(BF), values(g, start, WIN))

            store(block, g, lax.fori_loop(0, count, mix, jnp.zeros((SIDE * QB, GROUP), F32)))

    for_blocks(
        q_ref.shape[0] // QB,
        4,
        lambda b: Block(b, ranges_s, length),
        lambda blocks: at_once(blocks, WIN),
        lambda block: at_once([block], WIDER),
        steps,
    )


def attend_bwd(q_ref, q_at, k_ref, k_at, v_at, do_ref, ranges_s, lo_rows, hi_rows, dq_ref, dq_at, dk_acc, dv_acc):
    length = k_ref.shape[0]
    factor = HD**-0.5
    q_mask = head_masks(factor)
    do_mask = head_masks(1.0)
    groups = range(do_ref.shape[1] // GROUP)
    dk_acc[...] = jnp.zeros(dk_acc.shape, F32)
    dv_acc[...] = jnp.zeros(dv_acc.shape, F32)

    def keys(g, start, size):
        return k_ref[pl.ds(start, size), pl.ds(k_at + g * GROUP, GROUP)]

    def values(g, start, size):
        return k_ref[pl.ds(start, size), pl.ds(v_at + g * GROUP, GROUP)]

    def query(block, g):
        return stack_heads(q_ref[pl.ds(block.q0, QB), pl.ds(q_at + g * GROUP, GROUP)], q_mask)

    def grad(block, g):
        return stack_heads(do_ref[pl.ds(block.q0, QB), pl.ds(g * GROUP, GROUP)], do_mask)

    def allowed(block, begin, start, size):
        low = lo_rows[pl.ds(block.b, 1), :]
        high = hi_rows[pl.ds(block.b, 1), :]
        places = start + lax.broadcasted_iota(jnp.int32, (size, SIDE * QB), 0)
        return (places >= jnp.maximum(low, begin)) & (places <= high)

    def scores(block, g, start, size, ok):
        return jnp.where(ok, dot_nt(keys(g, start, size), query(block, g)), NEGATIVE)

    def accumulate(g, start, size, dv, dk):
        rows = pl.ds(start, size)
        lanes = pl.ds(g * GROUP, GROUP)
        dv_acc[rows, lanes] += dv
        dk_acc[rows, lanes] += dk

    def store(block, g, stacked):
        dq = pick_heads(stacked) * factor
        dq_ref[pl.ds(block.q0, QB), pl.ds(dq_at + g * GROUP, GROUP)] = dq.astype(BF)

    def at_once(blocks, size):
        todo, score, slopes = [], [], []
        for block in blocks:
            begin, start = block.window(0, size)
            ok = allowed(block, begin, start, size)
            for g in groups:
                todo.append((block, g, start))
                score.append(scores(block, g, start, size, ok))
                slopes.append(dot_nt(values(g, start, size), grad(block, g)))
        raised = [jnp.exp(s - jnp.max(s, axis=0, keepdims=True)) for s in score]
        probs = [r * (1.0 / down_sum(r)) for r in raised]
        delta = [(p * (s - down_sum(p * s))).astype(BF) for p, s in zip(probs, slopes)]
        dv = [dot(p.astype(BF), grad(block, g)) for p, (block, g, _) in zip(probs, todo)]
        dk = [dot(d, query(block, g)) for d, (block, g, _) in zip(delta, todo)]
        dq = [dot_tn(d, keys(g, start, size)) for d, (_, g, start) in zip(delta, todo)]
        for i, (block, g, start) in enumerate(todo):
            store(block, g, dq[i])
            accumulate(g, start, size, dv[i], dk[i])

    def steps(block):
        count = block.span // WIN + 1
        for g in groups:

            def score_at(k):
                begin, start = block.window(k, WIN)
                return start, scores(block, g, start, WIN, allowed(block, begin, start, WIN))

            def stats(k, state):
                top, total = state
                _, score = score_at(k)
                higher = jnp.maximum(top, jnp.max(score, axis=0, keepdims=True))
                return higher, total * jnp.exp(top - higher) + down_sum(jnp.exp(score - higher))

            start_top = jnp.full((1, SIDE * QB), 2 * NEGATIVE, F32)
            top, total = lax.fori_loop(0, count, stats, (start_top, jnp.zeros((1, SIDE * QB), F32)))

            def probs_of(k):
                start, score = score_at(k)
                return start, jnp.exp(score - top) * (1.0 / total), dot_nt(values(g, start, WIN), grad(block, g))

            def centre(k, middle):
                _, probs, slopes = probs_of(k)
                return middle + down_sum(probs * slopes)

            middle = lax.fori_loop(0, count, centre, jnp.zeros((1, SIDE * QB), F32))

            def last_pass(k, out):
                start, probs, slopes = probs_of(k)
                delta = (probs * (slopes - middle)).astype(BF)
                accumulate(g, start, WIN, dot(probs.astype(BF), grad(block, g)), dot(delta, query(block, g)))
                return out + dot_tn(delta, keys(g, start, WIN))

            store(block, g, lax.fori_loop(0, count, last_pass, jnp.zeros((SIDE * QB, GROUP), F32)))

    for_blocks(
        q_ref.shape[0] // QB,
        2,
        lambda b: Block(b, ranges_s, length),
        lambda blocks: at_once(blocks, WIN),
        lambda block: at_once([block], WIDER),
        steps,
    )


def over_tiles(count, size, step):
    for t in range(count):
        step(t * size)


def gelu_parts(value):
    area = 0.5 * (1.0 + lax.erf(value * (0.5**0.5)))
    bell = jnp.exp(-0.5 * value * value) * 0.3989422804014327
    return value * area, area + value * bell


def middle_kernel(ranges_s, *refs):
    inputs, refs = refs[:10], refs[10:]
    outs, refs = refs[:8], refs[8:]
    loaded, refs = refs[:10], refs[10:]
    (out_ref, dr2_ref, dckv, g_in, g_down, g_co, vec_ref), refs = refs[:7], refs[7:]
    (o2_ref, do2_ref, r2_ref, h2_ref, z_ref, gp_ref, du_ref, dr3_ref, df_ref, da_ref), refs = refs[:10], refs[10:]
    lo_rows, hi_rows, load, store = refs
    loads = [pltpu.make_async_copy(src, dst, load.at[i]) for i, (src, dst) in enumerate(zip(inputs, loaded))]
    for copy in loads:
        copy.start()
    waiting, given = list(range(len(loads))), []
    (cq, ckv, cols, ranges, par, r1_ref, w_co, w_in, w_down, cot_ref) = loaded

    def need(upto):
        while waiting and waiting[0] <= upto:
            loads[waiting.pop(0)].wait()

    def give(at, ref):
        copy = pltpu.make_async_copy(ref, outs[at], store.at[at])
        copy.start()
        given.append(copy)

    tokens, width = r1_ref.shape
    wide = w_in.shape[1]
    need(3)
    attend_fwd(cq, 0, ckv, 0, width, ranges_s, cols, o2_ref)
    need(6)

    def resid_two(t):
        rows = pl.ds(t * 256, 256)
        hidden = norm_parts(r1_ref[rows, :])[0] * par[0:1, :] + par[3:4, :]
        resid = hidden * par[7:8, :] + dot(o2_ref[rows, :], w_co[...])
        r2_ref[rows, :] = resid
        h2_ref[rows, :] = (norm_parts(resid)[0] * par[1:2, :] + par[4:5, :]).astype(BF)

    for t in range(tokens // 256):
        resid_two(t)

    def up(at):
        lanes = pl.ds(at, 256)
        active, slope = gelu_parts(dot(h2_ref[...], w_in[:, lanes]))
        z_ref[:, lanes] = active.astype(BF)
        gp_ref[:, lanes] = slope

    need(7)
    over_tiles(wide // 256, 256, up)
    need(9)
    vec = [jnp.zeros((1, width), F32) for _ in range(6)]
    for t in range(tokens // 256):
        rows = pl.ds(t * 256, 256)
        hidden = norm_parts(r2_ref[rows, :])[0] * par[1:2, :] + par[4:5, :]
        resid = hidden * par[8:9, :] + dot(z_ref[rows, :], w_down[...])
        normal, scale = norm_parts(resid)
        out_ref[rows, :] = (normal * par[2:3, :] + par[5:6, :]).astype(BF)
        grad = cot_ref[rows, :].astype(F32)
        vec[0] += down_sum(grad * normal)
        vec[1] += down_sum(grad)
        back = norm_back(grad, normal, scale, par[2:3, :])
        vec[2] += down_sum(hidden * back)
        dr3_ref[rows, :] = back
        df_ref[rows, :] = back.astype(BF)

    give(0, out_ref)

    def grad_down(at):
        g_down[pl.ds(at, 256), :] = dot_tn(z_ref[:, pl.ds(at, 256)], df_ref[...]).astype(BF)

    over_tiles(wide // 256, 256, grad_down)
    give(5, g_down)

    def down(at):
        lanes = pl.ds(at, 256)
        grad = dot_nt(df_ref[...], w_down[pl.ds(at, 256), :])
        du_ref[:, lanes] = (grad * gp_ref[:, lanes]).astype(BF)

    over_tiles(wide // 256, 256, down)
    for t in range(tokens // 256):
        rows = pl.ds(t * 256, 256)
        grad = dr3_ref[rows, :] * par[8:9, :] + dot_nt(du_ref[rows, :], w_in[...])
        normal, scale = norm_parts(r2_ref[rows, :])
        vec[3] += down_sum(grad * normal)
        vec[4] += down_sum(grad)
        back = norm_back(grad, normal, scale, par[1:2, :])
        hidden = norm_parts(r1_ref[rows, :])[0] * par[0:1, :] + par[3:4, :]
        vec[5] += down_sum(hidden * back)
        dr2_ref[rows, :] = back
        low = back.astype(BF)
        da_ref[rows, :] = low
        do2_ref[rows, :] = dot_nt(low, w_co[...]).astype(BF)
    for k in range(6):
        vec_ref[k : k + 1, :] = vec[k]
    give(7, vec_ref)
    give(1, dr2_ref)

    def grad_up(at):
        lanes = pl.ds(at, 256)
        g_in[:, lanes] = dot_tn(h2_ref[...], du_ref[:, lanes]).astype(BF)

    over_tiles(wide // 256, 256, grad_up)
    give(4, g_in)

    def grad_co(at):
        lanes = pl.ds(at, 256)
        g_co[:, lanes] = dot_tn(o2_ref[...], da_ref[:, lanes]).astype(BF)

    over_tiles(width // 256, 256, grad_co)
    give(6, g_co)
    for b in range(tokens // QB):
        for at, ref in ((1, lo_rows), (2, hi_rows)):
            row = ranges[at : at + 1, b * QB : (b + 1) * QB]
            ref[b : b + 1, :] = jnp.concatenate([row] * SIDE, axis=1)
    dk_acc, dv_acc = gp_ref.at[:, pl.ds(0, width)], gp_ref.at[:, pl.ds(width, width)]
    attend_bwd(cq, 0, ckv, 0, width, do2_ref, ranges_s, lo_rows, hi_rows, df_ref, 0, dk_acc, dv_acc)
    give(2, df_ref)
    dckv[:, :width] = dk_acc[...].astype(BF)
    dckv[:, width:] = dv_acc[...].astype(BF)
    give(3, dckv)
    for copy in given:
        copy.wait()


def middle(ranges, arrays):
    cq, ckv, w_in = arrays[0], arrays[1], arrays[7]
    length, width = cq.shape
    ff = w_in.shape[1]
    vm, anywhere = pltpu.VMEM, pl.BlockSpec(memory_space=pl.ANY)
    outs = (
        shaped(length, width), shaped(length, width, dtype=F32), shaped(length, width), shaped(length, 2 * width),
        shaped(width, ff), shaped(ff, width), shaped(width, width), shaped(8, width, dtype=F32),
    )
    scratch = [vm(a.shape, a.dtype) for a in arrays]
    scratch += [vm(o.shape, o.dtype) for i, o in enumerate(outs) if i != 2]
    scratch += [vm((length, width), BF)] * 2 + [vm((length, width), F32), vm((length, width), BF), vm((length, ff), BF)]
    scratch += [vm((length, ff), F32), vm((length, ff), BF), vm((length, width), F32)] + [vm((length, width), BF)] * 2
    scratch += [vm((length // QB, SIDE * QB), jnp.int32)] * 2
    scratch += [pltpu.SemaphoreType.DMA((len(arrays),)), pltpu.SemaphoreType.DMA((len(outs),))]
    return pl.pallas_call(
        middle_kernel,
        out_shape=outs,
        in_specs=[pl.BlockSpec(memory_space=pltpu.SMEM)] + [anywhere] * len(arrays),
        out_specs=(anywhere,) * len(outs),
        scratch_shapes=scratch,
        compiler_params=pltpu.CompilerParams(vmem_limit_bytes=VMEM_BYTES),
        name="middle",
    )(ranges, *arrays)


def shaped(*dims, dtype=BF):
    return jax.ShapeDtypeStruct(dims, dtype)


STEP_US = 1.35
FIRST_CHUNKS, FIRST_LAG, LATER_LAG = 8, 3, 4


def run_plan(events, advance, work):
    now, whole, work = 0.0, set(), list(work)

    def do_work(until):
        nonlocal now
        while work and set(work[0][0]) <= whole and now < until:
            _, us, run = work.pop(0)
            run()
            now += us

    for time, k, s in events:
        do_work(time)
        now = max(now, time)
        if advance(k, s):
            whole.add(k)
    do_work(float("inf"))
    assert not work


DENSE = 128


class Gather:
    def __init__(self, place, chunks, shards, fulls, send, recv, own):
        self.place, self.chunks, self.shards, self.fulls = place, chunks, shards, fulls
        self.send, self.recv, self.used, self.sent = send, recv, 0, []
        self.states = []
        for k, chunk in enumerate(chunks):
            src, target = self.views(chunk, [])
            mine = pltpu.make_async_copy(src, target, own.at[k])
            mine.start()
            self.states.append({"done": [], "copies": [], "order": chunk[6], "mine": mine})

    def views(self, chunk, done):
        which, row, rows, col, cols, split, _ = chunk
        place = self.place
        quarter, half = cols // 4, cols // 2
        lanes = pl.ds(col, cols)
        if split:
            lanes = pl.ds(pl.multiple_of(col + place.core * half, 128), half)
            if "x" not in done:
                lanes = pl.ds(pl.multiple_of(col + place.core * half + place.x * quarter, 128), quarter)
        spot = tuple(slice(None) if j in done else place.digits[j] for j in range(len(place.parts)))
        target = self.fulls[which].at[spot + (pl.ds(row, rows), lanes)]
        if done:
            return target, target
        return self.shards[which].at[pl.ds(row, rows), lanes], target

    def advance(self, k, s):
        state = self.states[k]
        stages = len(state["order"])
        if s > stages:
            return False
        if s == 1:
            state["mine"].wait()
        for copy in state["copies"]:
            copy.wait_recv()
        state["copies"] = []
        if s == stages:
            return True
        stage = state["order"][s]
        src, target = self.views(self.chunks[k], state["done"])
        for peer in self.place.peers(stage):
            at = self.used
            self.used += 1
            copy = pltpu.make_async_remote_copy(
                src_ref=src, dst_ref=target, send_sem=self.send.at[at], recv_sem=self.recv.at[at],
                device_id=peer, device_id_type=pl.DeviceIdType.MESH,
            )
            copy.start()
            state["copies"].append(copy)
            self.sent.append(copy)
        state["done"] = state["done"] + [stage]
        return False

    def events(self):
        events = []
        for k, chunk in enumerate(self.chunks):
            lag = FIRST_LAG if k < FIRST_CHUNKS else LATER_LAG
            events += [(STEP_US * (k + s * lag), k, s) for s in range(len(chunk[6]) + 1)]
        return sorted(events, key=lambda e: (e[0], e[1]))

    def finish(self):
        for copy in self.sent:
            copy.wait_send()


def segment_ranges(own, far, out):
    width = own.shape[1]
    numbers = lax.broadcasted_iota(jnp.int32, (SEGS, width), 0).astype(F32)
    mine = (own == numbers).astype(F32)

    def counted(hit):
        return jnp.sum(mine * jnp.sum(hit.astype(F32), axis=1, keepdims=True), axis=0, keepdims=True)

    out[0:1, :] = counted(own < numbers).astype(jnp.int32)
    out[1:2, :] = counted(far < numbers).astype(jnp.int32)
    out[2:3, :] = (counted(far <= numbers) - 1.0).astype(jnp.int32)
    out[3:8, :] = jnp.zeros((5, width), jnp.int32)


def dense_attend(q_ref, q_at, q0, k_ref, k_at, v_at, limit, allowed, o_ref):
    rows = lax.broadcasted_iota(jnp.int32, (SIDE * DENSE, GROUP), 0) // DENSE
    lanes = lax.broadcasted_iota(jnp.int32, (SIDE * DENSE, GROUP), 1) // HD
    mask = jnp.where(rows == lanes, HD**-0.5, 0.0).astype(BF)
    shift = jnp.where(allowed, 0.0, NEGATIVE)
    shift = jnp.concatenate([shift] * SIDE, axis=0)
    places = lax.broadcasted_iota(jnp.int32, (DENSE, GROUP), 1) // HD
    for g in range(o_ref.shape[1] // GROUP):
        block = q_ref[pl.ds(q0, DENSE), pl.ds(q_at + g * GROUP, GROUP)]
        query = jnp.concatenate([block] * SIDE, axis=0) * mask
        score = dot_nt(query, k_ref[pl.ds(0, limit), pl.ds(k_at + g * GROUP, GROUP)]) + shift
        raised = jnp.exp(score - jnp.max(score, axis=-1, keepdims=True))
        total = jnp.sum(raised, axis=-1, keepdims=True)
        mixed = dot(raised.astype(BF), k_ref[pl.ds(0, limit), pl.ds(v_at + g * GROUP, GROUP)]) * (1.0 / total)
        out = mixed[:DENSE]
        for h in range(1, SIDE):
            out = jnp.where(places == h, mixed[h * DENSE : (h + 1) * DENSE], out)
        o_ref[pl.ds(q0, DENSE), pl.ds(g * GROUP, GROUP)] = out.astype(BF)


def front_kernel(mesh, chunks, count, sizes, *refs):
    shards, rest = refs[:count], refs[count:]
    tok_in, mem_in, own_seg, far_seg = rest[:4]
    rest = rest[4:]
    fulls, rest = rest[:count], rest[count:]
    outs, rest = rest[:8], rest[8:]
    (qkv, o1, r1, cq, ckv, cols, ranges, par, tok, mem, w_qkv, w_out, w_cq, w_ckv, small, seg_col) = rest[:16]
    send, recv, own, load, load_in, store = rest[16:]
    place = Place(mesh)
    place.greet()
    gather = Gather(place, chunks, shards, fulls, send, recv, own)
    taken = [
        pltpu.make_async_copy(tok_in, tok, load_in.at[0]),
        pltpu.make_async_copy(mem_in, mem, load_in.at[1]),
    ]
    for copy in taken:
        copy.start()
    length, width = tok.shape
    held = {0: w_qkv, 1: w_out, 2: w_cq, 3: w_ckv, count - 1: small}
    loads = {}

    def fetch(k):
        which, row, rows, col, cols, split, _ = chunks[k]
        if which not in held:
            return
        loads[k] = pltpu.make_async_copy(
            fulls[which].at[..., pl.ds(col, cols)], held[which].at[..., pl.ds(col, cols)], load.at[k]
        )
        loads[k].start()

    def chunk_of(which, col):
        return [k for k, c in enumerate(chunks) if c[0] == which and c[3] == col][0]

    def weight(ref, col, cols):
        flat = ref.shape[:-2]
        return ref[..., pl.ds(col, cols)].reshape(math.prod(flat) * ref.shape[-2], cols)

    def give(at, ref):
        copy = pltpu.make_async_copy(ref, outs[at], store.at[at])
        copy.start()
        given.append(copy)

    given = []

    def project(t):
        def run():
            loads[chunk_of(0, t * 512)].wait()
            if t == 0:
                taken[0].wait()
            qkv[:, pl.ds(t * 512, 512)] = dot(tok[...], weight(w_qkv, t * 512, 512)).astype(BF)
            if t == 2:
                give(0, qkv)

        return run

    def columns():
        own_row = own_seg[...].astype(F32)
        segment_ranges(own_row, far_seg[...].astype(F32), ranges)
        cols[...] = ranges[...].astype(F32).T.astype(jnp.int32)
        give(6, ranges)
        give(5, cols)
        seg_col[...] = jnp.broadcast_to(own_row, (8, length)).T

    def attend_self(b):
        def run():
            q0, limit = b * DENSE, (b + 1) * DENSE
            same = seg_col[pl.ds(q0, DENSE), 0:1] == own_seg[:, pl.ds(0, limit)].astype(F32)
            key = lax.broadcasted_iota(jnp.int32, (DENSE, limit), 1)
            query = q0 + lax.broadcasted_iota(jnp.int32, (DENSE, limit), 0)
            dense_attend(qkv, 0, q0, qkv, width, 2 * width, limit, same & (key <= query), o1)
            if limit == length:
                give(1, o1)

        return run

    def pairs(t):
        def run():
            loads[chunk_of(3, t * 512)].wait()
            if t == 0:
                taken[1].wait()
            ckv[:, pl.ds(t * 512, 512)] = dot(mem[...], weight(w_ckv, t * 512, 512)).astype(BF)
            if t == 1:
                give(4, ckv)

        return run

    def params():
        loads[chunk_of(count - 1, 0)].wait()
        each = sizes[count - 1]
        flat = small[...].reshape(math.prod(small.shape[:-2]), small.shape[-2], small.shape[-1])
        par[...] = jnp.concatenate([flat[w, :, :each].astype(F32) for w in range(flat.shape[0])], axis=1)
        give(7, par)

    def hidden(t):
        def run():
            if t == 0:
                loads[chunk_of(1, 0)].wait()
                loads[chunk_of(2, 0)].wait()
            rows = pl.ds(t * 256, 256)
            resid = tok[rows, :].astype(F32) * par[6:7, :] + dot(o1[rows, :], weight(w_out, 0, width))
            r1[rows, :] = resid
            normal, _ = norm_parts(resid)
            low = (normal * par[0:1, :] + par[3:4, :]).astype(BF)
            cq[rows, :] = dot(low, weight(w_cq, 0, width)).astype(BF)
            if (t + 1) * 256 == length:
                give(2, r1)
                give(3, cq)

        return run

    work = [((), 0.5, columns)]
    work += [((chunk_of(0, t * 512),), 0.8, project(t)) for t in range(3)]
    work += [((), 0.2 + 0.15 * b, attend_self(b)) for b in range(length // DENSE)]
    work += [((chunk_of(count - 1, 0),), 0.2, params)]
    work += [((chunk_of(1, 0), chunk_of(2, 0)), 0.9, hidden(t)) for t in range(length // 256)]
    work += [((chunk_of(3, t * 512),), 0.8, pairs(t)) for t in range(2)]

    def advance(k, s):
        whole = gather.advance(k, s)
        if whole:
            fetch(k)
        return whole

    run_plan(gather.events(), advance, work)
    gather.finish()
    for copy in given:
        copy.wait()


def front(mesh, shards, tokens, memory, own_seg, far_seg, rows, collective):
    early, late = stage_orders(mesh)
    digits = tuple(size for _, size in wide_parts(mesh))
    small_order = [s for s in early if not isinstance(s, str)]
    count = len(shards)
    length, width = tokens.shape
    chunks = []
    for which in [0, count - 1] + list(range(1, count - 1)):
        high, cols = shards[which].shape
        if cols < 512:
            chunks.append((which, 0, high, 0, cols, False, small_order))
            continue
        cut = max(1, high // 64)
        for r in range(cut):
            for c in range(cols // 512):
                order = late if len(chunks) % 8 in LATE_CHUNKS else early
                chunks.append((which, r * (high // cut), high // cut, c * 512, 512, True, order))
    copies = sum(stage_copies(mesh, c[6]) for c in chunks)
    fulls = tuple(jax.ShapeDtypeStruct(digits + s.shape, s.dtype) for s in shards)
    made = (
        shaped(length, 3 * width), shaped(length, width), shaped(length, width, dtype=F32), shaped(length, width),
        shaped(length, 2 * width), shaped(length, 8, dtype=jnp.int32), shaped(8, length, dtype=jnp.int32),
        shaped(16, width, dtype=F32),
    )
    vm = pltpu.VMEM
    kept = [0, 1, 2, 3, count - 1]
    results = pl.pallas_call(
        functools.partial(front_kernel, mesh, chunks, count, [s.shape[0] for s in shards[:-1]] + [rows]),
        out_shape=fulls + made,
        in_specs=[pl.BlockSpec(memory_space=pl.ANY)] * (count + 2) + [pl.BlockSpec(memory_space=vm)] * 2,
        out_specs=tuple(pl.BlockSpec(memory_space=pl.ANY) for _ in fulls + made),
        scratch_shapes=[vm(m.shape, m.dtype) for m in made]
        + [vm(tokens.shape, BF), vm(memory.shape, BF)]
        + [vm(fulls[k].shape, BF) for k in kept]
        + [
            vm((length, 8), F32),
            pltpu.SemaphoreType.DMA((copies,)),
            pltpu.SemaphoreType.DMA((copies,)),
            pltpu.SemaphoreType.DMA((len(chunks),)),
            pltpu.SemaphoreType.DMA((len(chunks),)),
            pltpu.SemaphoreType.DMA((2,)),
            pltpu.SemaphoreType.DMA((len(made),)),
        ],
        compiler_params=pltpu.CompilerParams(
            collective_id=collective, has_side_effects=True, vmem_limit_bytes=VMEM_BYTES
        ),
        name="front",
    )(*shards, tokens, memory, own_seg.reshape(1, length), far_seg.reshape(1, length))
    return [full.reshape((-1, full.shape[-1])) for full in results[:count]], results[count:]


LATE_CHUNKS = (1, 4, 6)


def layer(mesh, tokens, memory, segments, cotangent, weights, made, rows):
    w_qkv, w_out, w_cq, w_ckv, w_co, w_in, w_down, _ = weights
    qkv, o1, r1, cq, ckv, cols, ranges, par = made
    arrays = (cq, ckv, cols, ranges, par, r1, w_co, w_in, w_down, cotangent)
    out, dr2, dcq, dckv, g_in, g_down, g_co, vec_two = middle(ranges, arrays)
    inputs = (dr2, dcq, w_cq, r1, par, vec_two, tokens, w_out, o1, memory, dckv, qkv, w_ckv, w_qkv)
    return out, back(mesh, (g_in, g_down, g_co), inputs, segments, rows, 2)


PACE_US, LAG_US, LAST_LAG_US = 1.3, 5.0, 3.0
PATTERN = "yxyxyxyxyxyxyxyxy"


def reduce_orders(mesh):
    digits = list(range(len(wide_parts(mesh))))[::-1]
    return {
        "x": ["core", "x"] + digits,
        "y": ["core", digits[0], "x"] + digits[1:],
        "z": ["core"] + digits[::-1] + ["x"],
        "a": ["core", "x", "all"],
        "b": ["core", digits[0], "x"] + digits[1:],
    }


def stage_peers(mesh, stage):
    sizes = [size for _, size in wide_parts(mesh)]
    if stage == "all":
        return [d for d in itertools.product(*[range(size) for size in sizes]) if any(d)]
    return [tuple(d if j == stage else 0 for j in range(len(sizes))) for d in range(1, sizes[stage])]


class Chunk:
    def __init__(self, mesh, which, sub, rows, col, cols, order, split, held):
        self.which, self.sub, self.rows, self.col, self.cols = which, sub, rows, col, cols
        self.order, self.split, self.held = order, split, held
        sizes = [size for _, size in wide_parts(mesh)]
        self.received = []
        self.copies = 2 if split else 0
        lanes = cols // 2 if split else cols
        self.shape = tuple(sizes) + (rows, lanes)
        for stage in order:
            if isinstance(stage, str) and stage != "all":
                lanes = lanes // 2 if stage == "x" and split else lanes
                count = 1
            else:
                sizes = [1 if stage in ("all", j) else size for j, size in enumerate(sizes)]
                count = len(stage_peers(mesh, stage))
            self.received.append([tuple(sizes) + (rows, lanes)] * count)
            self.copies += count


class Reduce:
    def __init__(self, mesh, place, chunks, grads, held, received, sums, send, recv, own):
        self.mesh, self.place, self.chunks, self.grads, self.sums = mesh, place, chunks, grads, sums
        self.send, self.recv, self.used, self.sent = send, recv, 0, []
        held, received = list(held), list(received)
        self.states = []
        for k, chunk in enumerate(chunks):
            half = chunk.cols // 2 if chunk.split else chunk.cols
            source = grads[chunk.which]
            near = chunk.col + place.core * half if chunk.split else chunk.col
            far = chunk.col + (1 - place.core) * half if chunk.split else chunk.col
            state = {"copies": [], "bufs": [], "mine": None}
            if chunk.held:
                cur = (held.pop(0), 0, half, None)
                mine = pltpu.make_async_copy(self.view((source, near, half, chunk.sub)), cur[0], own.at[k])
                mine.start()
                state["mine"] = mine
            else:
                cur = (source, near, half, chunk.sub)
            state["cur"], state["other"] = cur, (source, far, half, chunk.sub)
            state["pool"] = [[received.pop(0) for _ in shapes] for shapes in chunk.received]
            self.states.append(state)

    def view(self, cur, digits=None, lane=None, size=None):
        ref, off, lanes, sub = cur
        spot = [slice(None)] * len(self.place.parts)
        for j, index in (digits or {}).items():
            spot[j] = pl.ds(index, 1)
        if sub is not None:
            spot.append(sub)
        start = off if lane is None else off + lane
        if not isinstance(start, int):
            start = pl.multiple_of(start, 128)
        return ref.at[tuple(spot) + (slice(None), pl.ds(start, size or lanes))]

    def ship(self, src, target, peer):
        at = self.used
        self.used += 1
        copy = pltpu.make_async_remote_copy(
            src_ref=src, dst_ref=target, send_sem=self.send.at[at], recv_sem=self.recv.at[at],
            device_id=peer, device_id_type=pl.DeviceIdType.MESH,
        )
        copy.start()
        self.sent.append(copy)
        return copy

    def spots(self, stage, offsets):
        return {
            j: self.place.flip(self.place.digits[j], d, self.place.parts[j][1])
            for j, d in enumerate(offsets)
            if stage in ("all", j)
        }

    def begin(self, k, s):
        chunk, state, place = self.chunks[k], self.states[k], self.place
        stage, cur = chunk.order[s], state["cur"]
        bufs = state["pool"][s]
        if stage == "core":
            state["copies"] = [self.ship(self.view(state["other"]), bufs[0], place.core_peer())]
        elif stage == "x":
            src = self.view(cur)
            if chunk.split:
                half = cur[2] // 2
                src = self.view(cur, lane=(1 - place.x) * half, size=half)
            state["copies"] = [self.ship(src, bufs[0], place.x_peer())]
        else:
            for buf, offsets in zip(bufs, stage_peers(self.mesh, stage)):
                src = self.view(cur, self.spots(stage, offsets))
                state["copies"].append(self.ship(src, buf, place.wide_peer(offsets)))

    def end(self, k, s):
        chunk, state, place = self.chunks[k], self.states[k], self.place
        stage, cur, bufs = chunk.order[s], state["cur"], state["pool"][s]
        for copy in state["copies"]:
            copy.wait_recv()
        state["copies"] = []
        if stage == "core":
            if state["mine"] is not None:
                state["mine"].wait()
            mine = self.view(cur)
        elif stage == "x":
            half = cur[2] // 2 if chunk.split else cur[2]
            mine = self.view(cur, lane=place.x * half, size=half) if chunk.split else self.view(cur)
        else:
            mine = self.view(cur, self.spots(stage, (0,) * len(place.parts)))
        if len(bufs) == 1:
            bufs[0][...] = mine[...] + bufs[0][...]
        else:
            value = mine[...].astype(F32)
            for buf in bufs:
                value = value + buf[...].astype(F32)
            bufs[0][...] = value.astype(BF)
        state["cur"] = (bufs[0], 0, bufs[0].shape[-1], None)

    def out_view(self, k, size):
        chunk, start = self.chunks[k], self.chunks[k].col
        if size < chunk.cols:
            start = start + self.place.core * (chunk.cols // 2)
        if size < chunk.cols // 2:
            start = start + self.place.x * (chunk.cols // 4)
        if not isinstance(start, int):
            start = pl.multiple_of(start, 128)
        return self.sums[chunk.which].at[pl.ds((chunk.sub or 0) * chunk.rows, chunk.rows), pl.ds(start, size)]

    def advance(self, k, s):
        chunk, state = self.chunks[k], self.states[k]
        stages = len(chunk.order)
        if 0 < s <= stages:
            self.end(k, s - 1)
        if s < stages:
            self.begin(k, s)
            return
        if s > stages:
            for copy in state["copies"]:
                copy.wait_recv()
            state["copies"] = []
        if s == stages:
            view = self.out_view(k, chunk.cols // 4 if chunk.split else chunk.cols)
            view[...] = state["cur"][0][...].reshape(view.shape)
            if chunk.split:
                state["copies"] = [self.ship(view, view, self.place.x_peer())]
        elif s == stages + 1 and chunk.split:
            view = self.out_view(k, chunk.cols // 2)
            state["copies"] = [self.ship(view, view, self.place.core_peer())]

    def finish(self):
        for copy in self.sent:
            copy.wait_send()


def run_back(reduce, chunks, work):
    ready, now = {}, 0.0
    for us, _, gives in work:
        now += us
        for k in gives:
            ready[k] = now
    events, free = [], 0.0
    for k, chunk in enumerate(chunks):
        begin = max(free, ready.get(k, 0.0))
        free = begin + (PACE_US if chunk.split else 0.0)
        lag = LAST_LAG_US if k >= len(chunks) - 3 else LAG_US
        events += [(begin + s * lag, k, s) for s in range(len(chunk.order) + 3)]
    made, now, work = {k for k in range(len(chunks)) if k not in ready}, 0.0, list(work)
    for time, k, s in sorted(events):
        while work and (now < time or k not in made):
            us, run, gives = work.pop(0)
            run()
            made |= set(gives)
            now += us
        now = max(now, time)
        reduce.advance(k, s)
    for _, run, _ in work:
        run()


def back_kernel(mesh, chunks, count, *refs):
    far, rest = refs[:3], refs[3:]
    inputs, rest = rest[:15], rest[15:]
    sums, rest = rest[:count], rest[count:]
    gt_out, gm_out, rest = rest[0], rest[1], rest[2:]
    loaded, rest = rest[:14], rest[14:]
    (dk_acc, dv_acc, dqkv, h1, da, do1, g_cross, g_out, g_qkv, vectors, seg_col) = rest[:11]
    rest = rest[11:]
    held, rest = rest[: sum(c.held for c in chunks)], rest[sum(c.held for c in chunks) :]
    received, (send, recv, own, load, store) = rest[:-5], rest[-5:]
    own_seg = inputs[14]
    place = Place(mesh)
    place.greet(True)
    grads = list(far) + [g_cross, g_out, vectors, g_qkv]
    reduce = Reduce(mesh, place, chunks, grads, held, received, sums, send, recv, own)
    loads = [pltpu.make_async_copy(src, dst, load.at[i]) for i, (src, dst) in enumerate(zip(inputs[:14], loaded))]
    waiting = list(range(14))
    (dr2, dq, w_cq, r1, par, vec_two, tok, w_out, o1, mem, dckv, qkv, w_ckv, w_qkv) = loaded
    length, width = tok.shape
    given = []
    vec = [jnp.zeros((1, width), F32) for _ in range(3)]

    def fetch(first, last):
        def run():
            for copy in loads[first:last]:
                copy.start()

        return run

    def need(upto):
        while waiting and waiting[0] <= upto:
            loads[waiting.pop(0)].wait()

    def give(at, ref, out):
        copy = pltpu.make_async_copy(ref, out, store.at[at])
        copy.start()
        given.append(copy)

    def hidden(t):
        def run():
            need(7)
            if t == 0:
                seg_col[...] = jnp.broadcast_to(own_seg[...].astype(F32), (8, length)).T
                dk_acc[...] = jnp.zeros_like(dk_acc)
                dv_acc[...] = jnp.zeros_like(dv_acc)
            rows = pl.ds(t * 256, 256)
            grad = dr2[rows, :] * par[7:8, :] + dot_nt(dq[rows, :], w_cq[...])
            normal, scale = norm_parts(r1[rows, :])
            h1[rows, :] = (normal * par[0:1, :] + par[3:4, :]).astype(BF)
            vec[0] += down_sum(grad * normal)
            vec[1] += down_sum(grad)
            back = norm_back(grad, normal, scale, par[0:1, :])
            vec[2] += down_sum(tok[rows, :].astype(F32) * back)
            dr2[rows, :] = back
            low = back.astype(BF)
            da[rows, :] = low
            do1[rows, :] = dot_nt(low, w_out[...]).astype(BF)
            if (t + 1) * 256 == length:
                every = jnp.concatenate(vec + [vec_two[3:6, :], vec_two[0:3, :], jnp.zeros((7, width), F32)], axis=0)
                wide = mesh.shape["wide"]
                each = width // wide
                for w in range(wide):
                    part = every[:, w * each : (w + 1) * each]
                    part = jnp.concatenate([part, jnp.zeros((16, 128 - each), F32)], axis=1)
                    spot, rest = [], w
                    for low_bit, size in place.parts:
                        spot.append((w >> low_bit) % size)
                    vectors[tuple(spot)] = part.astype(BF)

        return run

    def put(ref, at, cols, value):
        ref[..., pl.ds(at, cols)] = value.astype(BF).reshape(ref.shape[:-1] + (cols,))

    def grad_out():
        need(8)
        put(g_out, 0, width, dot_tn(o1[...], da[...]))

    def grad_cq():
        put(g_cross, 0, width, dot_tn(h1[...], dq[...]))

    def grad_ckv(t):
        def run():
            need(10)
            put(g_cross, (t + 1) * width, width, dot_tn(mem[...], dckv[:, pl.ds(t * width, width)]))

        return run

    def grad_mem(t):
        def run():
            need(12)
            rows = pl.ds(t * 256, 256)
            r1[rows, :] = dot_nt(dckv[rows, :], w_ckv[...])
            if (t + 1) * 256 == length:
                give(0, r1, gm_out)

        return run

    def attend(b):
        def run():
            need(11)
            limit = (b + 1) * QB
            mine = own_seg[:, b * QB : (b + 1) * QB].astype(F32)
            same = seg_col[pl.ds(0, limit), 0:1] == jnp.concatenate([mine] * SIDE, axis=1)
            key = lax.broadcasted_iota(jnp.int32, (limit, SIDE * QB), 0)
            query = lax.rem(lax.broadcasted_iota(jnp.int32, (limit, SIDE * QB), 1), QB) + b * QB
            shift = jnp.where(same & (key <= query), 0.0, NEGATIVE)
            dense_attend_bwd(qkv, do1, b * QB, limit, shift, dqkv, dk_acc, dv_acc)

        return run

    def grad_qkv(t):
        def run():
            if t == 1:
                dqkv[:, width : 2 * width] = dk_acc[...].astype(BF)
            if t == 2:
                dqkv[:, 2 * width :] = dv_acc[...].astype(BF)
            put(g_qkv, t * width, width, dot_tn(tok[...], dqkv[:, pl.ds(t * width, width)]))

        return run

    def grad_tok(t):
        def run():
            need(13)
            rows = pl.ds(t * 256, 256)
            dr2[rows, :] = dr2[rows, :] * par[6:7, :] + dot_nt(dqkv[rows, :], w_qkv[...])
            if (t + 1) * 256 == length:
                give(1, dr2, gt_out)

        return run

    def chunks_of(which, col=None):
        return [k for k, c in enumerate(chunks) if c.which == which and col in (None, c.col)]

    parts = length // 256
    work = [(0.1, fetch(0, 8), [])]
    work += [(1.2, hidden(t), chunks_of(5) if t + 1 == parts else []) for t in range(parts)]
    work[2:2] = [(0.1, fetch(8, 14), [])]
    work += [(0.9, grad_out, chunks_of(4)), (0.9, grad_cq, chunks_of(3, 0))]
    work += [(0.9, grad_ckv(t), chunks_of(3, (t + 1) * width)) for t in range(2)]
    work += [(0.3 + 0.13 * b, attend(b), []) for b in range(length // QB)]
    work += [(1.0, grad_qkv(t), chunks_of(6, t * width)) for t in range(3)]
    work += [(0.4, grad_mem(t), []) for t in range(parts)]
    work += [(0.6, grad_tok(t), []) for t in range(parts)]
    run_back(reduce, chunks, work)
    need(13)
    reduce.finish()
    for copy in given:
        copy.wait()


def dense_attend_bwd(qkv, do_ref, q0, limit, shift, dqkv, dk_acc, dv_acc):
    width = do_ref.shape[1]
    factor = HD**-0.5
    q_mask, do_mask = head_masks(factor), head_masks(1.0)
    for g in range(width // GROUP):
        lanes = pl.ds(g * GROUP, GROUP)
        query = stack_heads(qkv[pl.ds(q0, QB), lanes], q_mask)
        grad = stack_heads(do_ref[pl.ds(q0, QB), lanes], do_mask)
        keys = qkv[pl.ds(0, limit), pl.ds(width + g * GROUP, GROUP)]
        values = qkv[pl.ds(0, limit), pl.ds(2 * width + g * GROUP, GROUP)]
        score = dot_nt(keys, query) + shift
        slopes = dot_nt(values, grad)
        raised = jnp.exp(score - jnp.max(score, axis=0, keepdims=True))
        probs = raised * (1.0 / down_sum(raised))
        delta = (probs * (slopes - down_sum(probs * slopes))).astype(BF)
        dv_acc[pl.ds(0, limit), lanes] += dot(probs.astype(BF), grad)
        dk_acc[pl.ds(0, limit), lanes] += dot(delta, query)
        dq = pick_heads(dot_tn(delta, keys)) * factor
        dqkv[pl.ds(q0, QB), lanes] = dq.astype(BF)


def back(mesh, far, inputs, own_seg, rows, collective):
    kinds = reduce_orders(mesh)
    digits = tuple(size for _, size in wide_parts(mesh))
    wide = mesh.shape["wide"]
    length, width = inputs[0].shape
    each = width // wide
    views, chunks, sums = [], [], []

    def add(which, sub, high, cols, split, held):
        for j in range(sub or 1):
            for c in range(cols // 512 if split else 1):
                order = kinds[PATTERN[len(chunks) % len(PATTERN)]]
                at = j if sub is not None else None
                chunks.append(Chunk(mesh, which, at, high, c * 512, min(cols, 512), order, split, held))

    for which, grad in enumerate(far):
        high, cols = grad.shape[0] // wide, grad.shape[1]
        sub = high * wide // cols if cols == width and high * wide > width else 1
        views.append(grad.reshape(digits + (sub, high // sub, cols)))
        sums.append(shaped(high, cols))
        add(which, sub, high // sub, cols, True, True)
    for which, cols in ((3, 3 * width), (4, width), (5, 128), (6, 3 * width)):
        high, split = (16, False) if which == 5 else (each, True)
        sums.append(shaped(high, cols))
        add(which, None, high, cols, split, False)
    vm = pltpu.VMEM
    arrays = list(inputs)
    scratch = [vm(a.shape, a.dtype) for a in arrays]
    scratch += [vm((length, width), F32)] * 2 + [vm((length, 3 * width), BF)] + [vm((length, width), BF)] * 3
    scratch += [vm(digits + (each, cols), BF) for cols in (3 * width, width, 3 * width)]
    scratch += [vm(digits + (16, 128), BF), vm((length, 8), F32)]
    scratch += [vm(c.shape, BF) for c in chunks if c.held]
    scratch += [vm(shape, BF) for c in chunks for shapes in c.received for shape in shapes]
    copies = sum(c.copies for c in chunks)
    scratch += [pltpu.SemaphoreType.DMA((n,)) for n in (copies, copies, len(chunks), len(arrays), 2)]
    large = shaped(length, width, dtype=F32)
    return pl.pallas_call(
        functools.partial(back_kernel, mesh, chunks, len(sums)),
        out_shape=tuple(sums) + (large, large),
        in_specs=[pl.BlockSpec(memory_space=pl.ANY)] * (len(far) + len(arrays)) + [pl.BlockSpec(memory_space=vm)],
        out_specs=tuple(pl.BlockSpec(memory_space=vm) for _ in sums) + (pl.BlockSpec(memory_space=pl.ANY),) * 2,
        scratch_shapes=scratch,
        compiler_params=pltpu.CompilerParams(
            collective_id=collective, has_side_effects=True, vmem_limit_bytes=VMEM_BYTES
        ),
        name="back",
    )(*views, *arrays, own_seg.reshape(1, length))


def finish_kernel(count, rows, *refs):
    s_in, s_down, s_co, s_cross, s_out, s_vec, s_qkv = refs[:count]
    large, outs, held, sems = refs[count : count + 2], refs[count + 2 : -3], refs[-3:-1], refs[-1]
    moves = [pltpu.make_async_copy(large[i], held[i], sems.at[i]) for i in range(2)]
    for move in moves:
        move.start()
    width = s_out.shape[1]
    plain = (s_qkv[...], s_out[...], s_cross[:, :width], s_cross[:, width:], s_co[...], s_in[...], s_down[...])
    for value, out in zip(plain, outs[2:]):
        out[...] = value.astype(F32)
    for i in range(2):
        moves[i].wait()
        moves[i] = pltpu.make_async_copy(held[i], outs[i], sems.at[i])
        moves[i].start()
    vectors = s_vec[...].astype(F32)
    for at, out in enumerate(outs[2 + len(plain) :]):
        for j in range(3):
            out[j : j + 1, :] = vectors[3 * j + at : 3 * j + at + 1, :rows]
    for move in moves:
        move.wait()


def finish(sums, large, shapes, rows):
    vmem = pl.BlockSpec(memory_space=pltpu.VMEM)
    anywhere = pl.BlockSpec(memory_space=pl.ANY)
    outs = [shaped(*a.shape, dtype=F32) for a in large] + [shaped(*s, dtype=F32) for s in shapes]
    return pl.pallas_call(
        functools.partial(finish_kernel, len(sums), rows),
        out_shape=tuple(outs),
        in_specs=[vmem] * len(sums) + [anywhere] * 2,
        out_specs=(anywhere,) * 2 + (vmem,) * len(shapes),
        scratch_shapes=[pltpu.VMEM(a.shape, F32) for a in large] + [pltpu.SemaphoreType.DMA((2,))],
        compiler_params=pltpu.CompilerParams(vmem_limit_bytes=VMEM_BYTES),
        name="finish",
    )(*sums, *large)


def body(
    mesh,
    tokens,
    memory,
    target_segments,
    memory_segments,
    self_qkv,
    self_out,
    cross_q,
    cross_kv,
    cross_out,
    ffn_in,
    ffn_out,
    norm_gain,
    norm_bias,
    omega,
    cotangent,
):
    wide = mesh.shape["wide"]
    rows = self_qkv.shape[0]
    width = rows * wide
    small = jnp.concatenate([norm_gain, norm_bias, omega], axis=1).T
    small = jnp.pad(small, ((0, 7), (0, 128 - rows)))
    weights, made = front(
        mesh, (self_qkv, self_out, cross_q, cross_kv, cross_out, ffn_in, ffn_out, small),
        tokens, memory, target_segments, memory_segments, rows, 1,
    )
    output, (*sums, grad_tokens, grad_memory) = layer(
        mesh, tokens, memory, target_segments, cotangent, weights, made, rows
    )
    shapes = ((rows, 3 * width), (rows, width), (rows, width), (rows, 2 * width), (rows, width))
    shapes += (ffn_in.shape, ffn_out.shape, (3, rows), (3, rows), (3, rows))
    grad_tokens, grad_memory, *summed = finish(sums, (grad_tokens, grad_memory), shapes, rows)
    summed = tuple(summed[:7]) + tuple(vector.T for vector in summed[7:])
    return (output, grad_tokens, grad_memory) + summed


def solution(mesh):
    in_specs = (
        P(("narrow", "wide"), None),
        P(("narrow", "wide"), None),
        P(("narrow", "wide")),
        P(("narrow", "wide")),
        P("wide", None),
        P("wide", None),
        P("wide", None),
        P("wide", None),
        P("wide", None),
        P("wide", None),
        P("wide", None),
        P("wide", None),
        P("wide", None),
        P("wide", None),
        P(("narrow", "wide"), None),
    )
    out_specs = (
        P(("narrow", "wide"), None),
        P(("narrow", "wide"), None),
        P(("narrow", "wide"), None),
        P("wide", None),
        P("wide", None),
        P("wide", None),
        P("wide", None),
        P("wide", None),
        P("wide", None),
        P("wide", None),
        P("wide", None),
        P("wide", None),
        P("wide", None),
    )
    return jax.shard_map(functools.partial(body, mesh), mesh=mesh, in_specs=in_specs, out_specs=out_specs, check_vma=False)
```

```python
import functools
import itertools
import math

import jax
import jax.numpy as jnp
from jax import lax
from jax.experimental import pallas as pl
from jax.experimental.pallas import tpu as pltpu
from jax.sharding import PartitionSpec as P

HD = 64

EPSILON = 1e-05
NEGATIVE = -1000000000.0
SEGS = 32


def wide_parts(mesh):
    bits = mesh.shape["wide"].bit_length() - 1
    low = [(0, 1)] if bits % 2 else []
    low = low + [(at, 2) for at in range(bits % 2, bits, 2)]
    return [(at, 2**count) for at, count in low[::-1]]


class Place:
    def __init__(self, mesh):
        self.parts = wide_parts(mesh)
        self.n = lax.axis_index("narrow")
        self.w = lax.axis_index("wide")
        self.core = lax.rem(self.n, 2)
        self.x = lax.div(self.n, 2)
        self.digits = [lax.rem(lax.div(self.w, 2**low), size) for low, size in self.parts]

    def flip(self, value, d, size):
        out = 0
        bit = 1
        while bit < size:
            digit = lax.rem(lax.div(value, bit), 2)
            out = out + bit * (1 - digit if d & bit else digit)
            bit *= 2
        return out

    def digit_peer(self, j, d):
        low, size = self.parts[j]
        other = self.flip(self.digits[j], d, size)
        return (self.n, self.w + (other - self.digits[j]) * 2**low)

    def x_peer(self):
        return ((1 - self.x) * 2 + self.core, self.w)

    def core_peer(self):
        return (self.x * 2 + 1 - self.core, self.w)

    def peers(self, stage):
        if stage == "x":
            return [self.x_peer()]
        if stage == "core":
            return [self.core_peer()]
        return [self.digit_peer(stage, d) for d in range(1, self.parts[stage][1])]

    def wide_peer(self, offsets):
        w = 0
        for (low, size), digit, d in zip(self.parts, self.digits, offsets):
            w = w + self.flip(digit, d, size) * 2**low
        return (self.n, w)

    def greet(self, whole=False):
        others = [self.x_peer(), self.core_peer()]
        if whole:
            choices = itertools.product(*[range(size) for _, size in self.parts])
            others += [self.wide_peer(d) for d in choices if any(d)]
        else:
            others += [p for j in range(len(self.parts)) for p in self.peers(j)]
        barrier = pltpu.get_barrier_semaphore()
        for peer in others:
            pl.semaphore_signal(barrier, inc=1, device_id=peer, device_id_type=pl.DeviceIdType.MESH)
        pl.semaphore_wait(barrier, len(others))


def stage_orders(mesh):
    count = len(wide_parts(mesh))
    early = list(range(count - 1)) + ["x", count - 1, "core"]
    late = list(range(count))[::-1] + ["x", "core"]
    return early, late


def stage_copies(mesh, order):
    parts = wide_parts(mesh)
    return sum(1 if isinstance(s, str) else parts[s][1] - 1 for s in order)


BF = jnp.bfloat16
F32 = jnp.float32
def dot(left, right):
    return lax.dot_general(left, right, (((1,), (0,)), ((), ())), preferred_element_type=F32)


def dot_nt(left, right):
    return lax.dot_general(left, right, (((1,), (1,)), ((), ())), preferred_element_type=F32)


def dot_tn(left, right):
    return lax.dot_general(left, right, (((0,), (0,)), ((), ())), preferred_element_type=F32)


def norm_parts(resid):
    middle = jnp.mean(resid, axis=-1, keepdims=True)
    centred = resid - middle
    spread = jnp.mean(centred * centred, axis=-1, keepdims=True)
    scale = lax.rsqrt(spread + EPSILON)
    return centred * scale, scale


def norm_back(grad, normal, scale, gain):
    scaled = grad * gain
    middle = jnp.mean(scaled, axis=-1, keepdims=True)
    along = jnp.mean(scaled * normal, axis=-1, keepdims=True)
    return (scaled - middle - normal * along) * scale


def down_sum(value):
    return jnp.sum(value, axis=0, keepdims=True)


QB = 64
WIN = 256
WIDER = 512
GROUP = 256
SIDE = GROUP // HD
VMEM_BYTES = 56 * 2**20


def head_masks(scale):
    rows = lax.broadcasted_iota(jnp.int32, (SIDE * QB, GROUP), 0) // QB
    lanes = lax.broadcasted_iota(jnp.int32, (SIDE * QB, GROUP), 1) // HD
    return jnp.where(rows == lanes, scale, 0.0).astype(BF)


def pick_heads(stacked):
    lanes = lax.broadcasted_iota(jnp.int32, (QB, GROUP), 1) // HD
    out = stacked[:QB]
    for h in range(1, SIDE):
        out = jnp.where(lanes == h, stacked[h * QB : (h + 1) * QB], out)
    return out


def stack_heads(block, mask):
    return jnp.concatenate([block] * SIDE, axis=0) * mask


class Block:
    def __init__(self, b, ranges_s, length):
        self.b = b
        self.q0 = pl.multiple_of(b * QB, QB)
        self.first = (ranges_s[1, self.q0] // 16) * 16
        self.last = ranges_s[2, self.q0 + QB - 1]
        self.span = self.last - self.first
        self.length = length

    def window(self, step, size):
        begin = self.first + step * size
        return begin, pl.multiple_of(jnp.minimum(begin, self.length - size), 16)


def for_blocks(count, at_a_time, make, together, steps):
    def one(t, carry):
        blocks = [make(t * at_a_time + i) for i in range(at_a_time)]
        span = blocks[0].span
        for block in blocks[1:]:
            span = jnp.maximum(span, block.span)

        @pl.when(span < WIN)
        def _():
            together(blocks, WIN)

        @pl.when((span >= WIN) & (span < WIDER))
        def _():
            together(blocks, WIDER)

        @pl.when(span >= WIDER)
        def _():
            for block in blocks:
                steps(block)

        return carry

    lax.fori_loop(0, count // at_a_time, one, 0)


def attend_fwd(q_ref, q_at, k_ref, k_at, v_at, ranges_s, cols_ref, o_ref):
    length = k_ref.shape[0]
    mask = head_masks(HD**-0.5)
    groups = range(o_ref.shape[1] // GROUP)

    def allowed(block, begin, start, size):
        low = cols_ref[pl.ds(block.q0, QB), 1:2]
        high = cols_ref[pl.ds(block.q0, QB), 2:3]
        places = start + lax.broadcasted_iota(jnp.int32, (QB, size), 1)
        ok = (places >= jnp.maximum(low, begin)) & (places <= high)
        return jnp.concatenate([ok] * SIDE, axis=0)

    def scores(block, g, start, size, ok):
        query = stack_heads(q_ref[pl.ds(block.q0, QB), pl.ds(q_at + g * GROUP, GROUP)], mask)
        keys = k_ref[pl.ds(start, size), pl.ds(k_at + g * GROUP, GROUP)]
        return jnp.where(ok, dot_nt(query, keys), NEGATIVE)

    def values(g, start, size):
        return k_ref[pl.ds(start, size), pl.ds(v_at + g * GROUP, GROUP)]

    def store(block, g, stacked):
        o_ref[pl.ds(block.q0, QB), pl.ds(g * GROUP, GROUP)] = pick_heads(stacked).astype(BF)

    def at_once(blocks, size):
        todo = []
        for block in blocks:
            begin, start = block.window(0, size)
            ok = allowed(block, begin, start, size)
            todo += [(block, g, start, scores(block, g, start, size, ok)) for g in groups]
        tops = [jnp.max(score, axis=-1, keepdims=True) for _, _, _, score in todo]
        raised = [jnp.exp(score - top) for (_, _, _, score), top in zip(todo, tops)]
        totals = [jnp.sum(r, axis=-1, keepdims=True) for r in raised]
        weights = [(r * (1.0 / total)).astype(BF) for r, total in zip(raised, totals)]
        mixed = [dot(w, values(g, start, size)) for w, (_, g, start, _) in zip(weights, todo)]
        for m, (block, g, _, _) in zip(mixed, todo):
            store(block, g, m)

    def steps(block):
        count = block.span // WIN + 1
        for g in groups:

            def score_at(k):
                begin, start = block.window(k, WIN)
                return start, scores(block, g, start, WIN, allowed(block, begin, start, WIN))

            def stats(k, state):
                top, total = state
                _, score = score_at(k)
                higher = jnp.maximum(top, jnp.max(score, axis=-1, keepdims=True))
                raised = jnp.sum(jnp.exp(score - higher), axis=-1, keepdims=True)
                return higher, total * jnp.exp(top - higher) + raised

            start_top = jnp.full((SIDE * QB, 1), 2 * NEGATIVE, F32)
            top, total = lax.fori_loop(0, count, stats, (start_top, jnp.zeros((SIDE * QB, 1), F32)))

            def mix(k, out):
                start, score = score_at(k)
                weights = jnp.exp(score - top) * (1.0 / total)
                return out + dot(weights.astype(BF), values(g, start, WIN))

            store(block, g, lax.fori_loop(0, count, mix, jnp.zeros((SIDE * QB, GROUP), F32)))

    for_blocks(
        q_ref.shape[0] // QB,
        4,
        lambda b: Block(b, ranges_s, length),
        at_once,
        steps,
    )


def attend_bwd(q_ref, q_at, k_ref, k_at, v_at, do_ref, ranges_s, lo_rows, hi_rows, dq_ref, dq_at, dk_acc, dv_acc):
    length = k_ref.shape[0]
    factor = HD**-0.5
    q_mask = head_masks(factor)
    do_mask = head_masks(1.0)
    groups = range(do_ref.shape[1] // GROUP)
    dk_acc[...] = jnp.zeros(dk_acc.shape, F32)
    dv_acc[...] = jnp.zeros(dv_acc.shape, F32)

    def keys(g, start, size):
        return k_ref[pl.ds(start, size), pl.ds(k_at + g * GROUP, GROUP)]

    def values(g, start, size):
        return k_ref[pl.ds(start, size), pl.ds(v_at + g * GROUP, GROUP)]

    def query(block, g):
        return stack_heads(q_ref[pl.ds(block.q0, QB), pl.ds(q_at + g * GROUP, GROUP)], q_mask)

    def grad(block, g):
        return stack_heads(do_ref[pl.ds(block.q0, QB), pl.ds(g * GROUP, GROUP)], do_mask)

    def allowed(block, begin, start, size):
        low = lo_rows[pl.ds(block.b, 1), :]
        high = hi_rows[pl.ds(block.b, 1), :]
        places = start + lax.broadcasted_iota(jnp.int32, (size, SIDE * QB), 0)
        return (places >= jnp.maximum(low, begin)) & (places <= high)

    def scores(block, g, start, size, ok):
        return jnp.where(ok, dot_nt(keys(g, start, size), query(block, g)), NEGATIVE)

    def accumulate(g, start, size, dv, dk):
        rows = pl.ds(start, size)
        lanes = pl.ds(g * GROUP, GROUP)
        dv_acc[rows, lanes] += dv
        dk_acc[rows, lanes] += dk

    def store(block, g, stacked):
        dq = pick_heads(stacked) * factor
        dq_ref[pl.ds(block.q0, QB), pl.ds(dq_at + g * GROUP, GROUP)] = dq.astype(BF)

    def at_once(blocks, size):
        todo, score, slopes = [], [], []
        for block in blocks:
            begin, start = block.window(0, size)
            ok = allowed(block, begin, start, size)
            for g in groups:
                todo.append((block, g, start))
                score.append(scores(block, g, start, size, ok))
                slopes.append(dot_nt(values(g, start, size), grad(block, g)))
        raised = [jnp.exp(s - jnp.max(s, axis=0, keepdims=True)) for s in score]
        probs = [r * (1.0 / down_sum(r)) for r in raised]
        delta = [(p * (s - down_sum(p * s))).astype(BF) for p, s in zip(probs, slopes)]
        dv = [dot(p.astype(BF), grad(block, g)) for p, (block, g, _) in zip(probs, todo)]
        dk = [dot(d, query(block, g)) for d, (block, g, _) in zip(delta, todo)]
        dq = [dot_tn(d, keys(g, start, size)) for d, (_, g, start) in zip(delta, todo)]
        for i, (block, g, start) in enumerate(todo):
            store(block, g, dq[i])
            accumulate(g, start, size, dv[i], dk[i])

    def steps(block):
        count = block.span // WIN + 1
        for g in groups:

            def score_at(k):
                begin, start = block.window(k, WIN)
                return start, scores(block, g, start, WIN, allowed(block, begin, start, WIN))

            def stats(k, state):
                top, total = state
                _, score = score_at(k)
                higher = jnp.maximum(top, jnp.max(score, axis=0, keepdims=True))
                return higher, total * jnp.exp(top - higher) + down_sum(jnp.exp(score - higher))

            start_top = jnp.full((1, SIDE * QB), 2 * NEGATIVE, F32)
            top, total = lax.fori_loop(0, count, stats, (start_top, jnp.zeros((1, SIDE * QB), F32)))

            def probs_of(k):
                start, score = score_at(k)
                return start, jnp.exp(score - top) * (1.0 / total), dot_nt(values(g, start, WIN), grad(block, g))

            def centre(k, middle):
                _, probs, slopes = probs_of(k)
                return middle + down_sum(probs * slopes)

            middle = lax.fori_loop(0, count, centre, jnp.zeros((1, SIDE * QB), F32))

            def last_pass(k, out):
                start, probs, slopes = probs_of(k)
                delta = (probs * (slopes - middle)).astype(BF)
                accumulate(g, start, WIN, dot(probs.astype(BF), grad(block, g)), dot(delta, query(block, g)))
                return out + dot_tn(delta, keys(g, start, WIN))

            store(block, g, lax.fori_loop(0, count, last_pass, jnp.zeros((SIDE * QB, GROUP), F32)))

    for_blocks(
        q_ref.shape[0] // QB,
        2,
        lambda b: Block(b, ranges_s, length),
        at_once,
        steps,
    )


def over_tiles(count, size, step):
    for t in range(count):
        step(t * size)


def gelu_parts(value):
    area = 0.5 * (1.0 + lax.erf(value * (0.5**0.5)))
    bell = jnp.exp(-0.5 * value * value) * 0.3989422804014327
    return value * area, area + value * bell


def middle_kernel(ranges_s, *refs):
    inputs, refs = refs[:10], refs[10:]
    outs, refs = refs[:8], refs[8:]
    loaded, refs = refs[:10], refs[10:]
    (out_ref, dr2_ref, dckv, g_in, g_down, g_co, vec_ref), refs = refs[:7], refs[7:]
    (o2_ref, do2_ref, r2_ref, h2_ref, z_ref, gp_ref, du_ref, dr3_ref, df_ref, da_ref), refs = refs[:10], refs[10:]
    lo_rows, hi_rows, load, store = refs
    loads = [pltpu.make_async_copy(src, dst, load.at[i]) for i, (src, dst) in enumerate(zip(inputs, loaded))]
    for copy in loads:
        copy.start()
    waiting, given = list(range(len(loads))), []
    (cq, ckv, cols, ranges, par, r1_ref, w_co, w_in, w_down, cot_ref) = loaded

    def need(upto):
        while waiting and waiting[0] <= upto:
            loads[waiting.pop(0)].wait()

    def give(at, ref):
        copy = pltpu.make_async_copy(ref, outs[at], store.at[at])
        copy.start()
        given.append(copy)

    tokens, width = r1_ref.shape
    wide = w_in.shape[1]
    need(3)
    attend_fwd(cq, 0, ckv, 0, width, ranges_s, cols, o2_ref)
    need(6)

    def resid_two(t):
        rows = pl.ds(t * 256, 256)
        hidden = norm_parts(r1_ref[rows, :])[0] * par[0:1, :] + par[3:4, :]
        resid = hidden * par[7:8, :] + dot(o2_ref[rows, :], w_co[...])
        r2_ref[rows, :] = resid
        h2_ref[rows, :] = (norm_parts(resid)[0] * par[1:2, :] + par[4:5, :]).astype(BF)

    for t in range(tokens // 256):
        resid_two(t)

    def up(at):
        lanes = pl.ds(at, 256)
        active, slope = gelu_parts(dot(h2_ref[...], w_in[:, lanes]))
        z_ref[:, lanes] = active.astype(BF)
        gp_ref[:, lanes] = slope

    need(7)
    over_tiles(wide // 256, 256, up)
    need(9)
    vec = [jnp.zeros((1, width), F32) for _ in range(6)]
    for t in range(tokens // 256):
        rows = pl.ds(t * 256, 256)
        hidden = norm_parts(r2_ref[rows, :])[0] * par[1:2, :] + par[4:5, :]
        resid = hidden * par[8:9, :] + dot(z_ref[rows, :], w_down[...])
        normal, scale = norm_parts(resid)
        out_ref[rows, :] = (normal * par[2:3, :] + par[5:6, :]).astype(BF)
        grad = cot_ref[rows, :].astype(F32)
        vec[0] += down_sum(grad * normal)
        vec[1] += down_sum(grad)
        back = norm_back(grad, normal, scale, par[2:3, :])
        vec[2] += down_sum(hidden * back)
        dr3_ref[rows, :] = back
        df_ref[rows, :] = back.astype(BF)

    give(0, out_ref)

    def grad_down(at):
        g_down[pl.ds(at, 256), :] = dot_tn(z_ref[:, pl.ds(at, 256)], df_ref[...]).astype(BF)

    over_tiles(wide // 256, 256, grad_down)
    give(5, g_down)

    def down(at):
        lanes = pl.ds(at, 256)
        grad = dot_nt(df_ref[...], w_down[pl.ds(at, 256), :])
        du_ref[:, lanes] = (grad * gp_ref[:, lanes]).astype(BF)

    over_tiles(wide // 256, 256, down)
    for t in range(tokens // 256):
        rows = pl.ds(t * 256, 256)
        grad = dr3_ref[rows, :] * par[8:9, :] + dot_nt(du_ref[rows, :], w_in[...])
        normal, scale = norm_parts(r2_ref[rows, :])
        vec[3] += down_sum(grad * normal)
        vec[4] += down_sum(grad)
        back = norm_back(grad, normal, scale, par[1:2, :])
        hidden = norm_parts(r1_ref[rows, :])[0] * par[0:1, :] + par[3:4, :]
        vec[5] += down_sum(hidden * back)
        dr2_ref[rows, :] = back
        low = back.astype(BF)
        da_ref[rows, :] = low
        do2_ref[rows, :] = dot_nt(low, w_co[...]).astype(BF)
    for k in range(6):
        vec_ref[k : k + 1, :] = vec[k]
    give(7, vec_ref)
    give(1, dr2_ref)

    def grad_up(at):
        lanes = pl.ds(at, 256)
        g_in[:, lanes] = dot_tn(h2_ref[...], du_ref[:, lanes]).astype(BF)

    over_tiles(wide // 256, 256, grad_up)
    give(4, g_in)

    def grad_co(at):
        lanes = pl.ds(at, 256)
        g_co[:, lanes] = dot_tn(o2_ref[...], da_ref[:, lanes]).astype(BF)

    over_tiles(width // 256, 256, grad_co)
    give(6, g_co)
    for b in range(tokens // QB):
        for at, ref in ((1, lo_rows), (2, hi_rows)):
            row = ranges[at : at + 1, b * QB : (b + 1) * QB]
            ref[b : b + 1, :] = jnp.concatenate([row] * SIDE, axis=1)
    dk_acc, dv_acc = gp_ref.at[:, pl.ds(0, width)], gp_ref.at[:, pl.ds(width, width)]
    attend_bwd(cq, 0, ckv, 0, width, do2_ref, ranges_s, lo_rows, hi_rows, df_ref, 0, dk_acc, dv_acc)
    give(2, df_ref)
    dckv[:, :width] = dk_acc[...].astype(BF)
    dckv[:, width:] = dv_acc[...].astype(BF)
    give(3, dckv)
    for copy in given:
        copy.wait()


def middle(ranges, arrays):
    cq, ckv, w_in = arrays[0], arrays[1], arrays[7]
    length, width = cq.shape
    ff = w_in.shape[1]
    vm, anywhere = pltpu.VMEM, pl.BlockSpec(memory_space=pl.ANY)
    outs = (
        shaped(length, width), shaped(length, width, dtype=F32), shaped(length, width), shaped(length, 2 * width),
        shaped(width, ff), shaped(ff, width), shaped(width, width), shaped(8, width, dtype=F32),
    )
    scratch = [vm(a.shape, a.dtype) for a in arrays]
    scratch += [vm(o.shape, o.dtype) for i, o in enumerate(outs) if i != 2]
    scratch += [vm((length, width), BF)] * 2 + [vm((length, width), F32), vm((length, width), BF), vm((length, ff), BF)]
    scratch += [vm((length, ff), F32), vm((length, ff), BF), vm((length, width), F32)] + [vm((length, width), BF)] * 2
    scratch += [vm((length // QB, SIDE * QB), jnp.int32)] * 2
    scratch += [pltpu.SemaphoreType.DMA((len(arrays),)), pltpu.SemaphoreType.DMA((len(outs),))]
    return pl.pallas_call(
        middle_kernel,
        out_shape=outs,
        in_specs=[pl.BlockSpec(memory_space=pltpu.SMEM)] + [anywhere] * len(arrays),
        out_specs=(anywhere,) * len(outs),
        scratch_shapes=scratch,
        compiler_params=pltpu.CompilerParams(vmem_limit_bytes=VMEM_BYTES),
        name="middle",
    )(ranges, *arrays)


def shaped(*dims, dtype=BF):
    return jax.ShapeDtypeStruct(dims, dtype)


STEP_US = 1.35
FIRST_CHUNKS, FIRST_LAG, LATER_LAG = 8, 4, 4


def run_plan(events, advance, work):
    now, whole, work = 0.0, set(), list(work)

    def do_work(until):
        nonlocal now
        while work and set(work[0][0]) <= whole and now < until:
            _, us, run = work.pop(0)
            run()
            now += us

    for time, k, s in events:
        do_work(time)
        now = max(now, time)
        if advance(k, s):
            whole.add(k)
    do_work(float("inf"))
    assert not work


DENSE = 128


class Gather:
    def __init__(self, place, chunks, shards, fulls, send, recv, own):
        self.place, self.chunks, self.shards, self.fulls = place, chunks, shards, fulls
        self.send, self.recv, self.used, self.sent = send, recv, 0, []
        self.states = []
        for k, chunk in enumerate(chunks):
            src, target = self.views(chunk, [])
            mine = pltpu.make_async_copy(src, target, own.at[k])
            mine.start()
            self.states.append({"done": [], "copies": [], "order": chunk[6], "mine": mine})

    def views(self, chunk, done):
        which, row, rows, col, cols, split, _ = chunk
        place = self.place
        quarter, half = cols // 4, cols // 2
        lanes = pl.ds(col, cols)
        if split:
            lanes = pl.ds(pl.multiple_of(col + place.core * half, 128), half)
            if "x" not in done:
                lanes = pl.ds(pl.multiple_of(col + place.core * half + place.x * quarter, 128), quarter)
        spot = tuple(slice(None) if j in done else place.digits[j] for j in range(len(place.parts)))
        target = self.fulls[which].at[spot + (pl.ds(row, rows), lanes)]
        if done:
            return target, target
        return self.shards[which].at[pl.ds(row, rows), lanes], target

    def advance(self, k, s):
        state = self.states[k]
        stages = len(state["order"])
        if s > stages:
            return False
        if s == 1:
            state["mine"].wait()
        for copy in state["copies"]:
            copy.wait_recv()
        state["copies"] = []
        if s == stages:
            return True
        stage = state["order"][s]
        src, target = self.views(self.chunks[k], state["done"])
        for peer in self.place.peers(stage):
            at = self.used
            self.used += 1
            copy = pltpu.make_async_remote_copy(
                src_ref=src, dst_ref=target, send_sem=self.send.at[at], recv_sem=self.recv.at[at],
                device_id=peer, device_id_type=pl.DeviceIdType.MESH,
            )
            copy.start()
            state["copies"].append(copy)
            self.sent.append(copy)
        state["done"] = state["done"] + [stage]
        return False

    def events(self):
        events = []
        for k, chunk in enumerate(self.chunks):
            lag = FIRST_LAG if k < FIRST_CHUNKS else LATER_LAG
            events += [(STEP_US * (k + s * lag), k, s) for s in range(len(chunk[6]) + 1)]
        return sorted(events, key=lambda e: (e[0], e[1]))

    def finish(self):
        for copy in self.sent:
            copy.wait_send()


def segment_ranges(own, far, out):
    width = own.shape[1]
    numbers = lax.broadcasted_iota(jnp.int32, (SEGS, width), 0).astype(F32)
    mine = (own == numbers).astype(F32)

    def counted(hit):
        return jnp.sum(mine * jnp.sum(hit.astype(F32), axis=1, keepdims=True), axis=0, keepdims=True)

    out[0:1, :] = counted(own < numbers).astype(jnp.int32)
    out[1:2, :] = counted(far < numbers).astype(jnp.int32)
    out[2:3, :] = (counted(far <= numbers) - 1.0).astype(jnp.int32)
    out[3:8, :] = jnp.zeros((5, width), jnp.int32)


def dense_attend(q_ref, q_at, q0, k_ref, k_at, v_at, limit, allowed, o_ref):
    rows = lax.broadcasted_iota(jnp.int32, (SIDE * DENSE, GROUP), 0) // DENSE
    lanes = lax.broadcasted_iota(jnp.int32, (SIDE * DENSE, GROUP), 1) // HD
    mask = jnp.where(rows == lanes, HD**-0.5, 0.0).astype(BF)
    shift = jnp.where(allowed, 0.0, NEGATIVE)
    shift = jnp.concatenate([shift] * SIDE, axis=0)
    places = lax.broadcasted_iota(jnp.int32, (DENSE, GROUP), 1) // HD
    for g in range(o_ref.shape[1] // GROUP):
        block = q_ref[pl.ds(q0, DENSE), pl.ds(q_at + g * GROUP, GROUP)]
        query = jnp.concatenate([block] * SIDE, axis=0) * mask
        score = dot_nt(query, k_ref[pl.ds(0, limit), pl.ds(k_at + g * GROUP, GROUP)]) + shift
        raised = jnp.exp(score - jnp.max(score, axis=-1, keepdims=True))
        total = jnp.sum(raised, axis=-1, keepdims=True)
        mixed = dot(raised.astype(BF), k_ref[pl.ds(0, limit), pl.ds(v_at + g * GROUP, GROUP)]) * (1.0 / total)
        out = mixed[:DENSE]
        for h in range(1, SIDE):
            out = jnp.where(places == h, mixed[h * DENSE : (h + 1) * DENSE], out)
        o_ref[pl.ds(q0, DENSE), pl.ds(g * GROUP, GROUP)] = out.astype(BF)


def front_kernel(mesh, chunks, count, sizes, *refs):
    shards, rest = refs[:count], refs[count:]
    tok_in, mem_in, own_seg, far_seg = rest[:4]
    rest = rest[4:]
    fulls, rest = rest[:count], rest[count:]
    outs, rest = rest[:8], rest[8:]
    (qkv, o1, r1, cq, ckv, cols, ranges, par, tok, mem, w_qkv, w_out, w_cq, w_ckv, small, seg_col) = rest[:16]
    send, recv, own, load, load_in, store = rest[16:]
    place = Place(mesh)
    place.greet()
    gather = Gather(place, chunks, shards, fulls, send, recv, own)
    taken = [
        pltpu.make_async_copy(tok_in, tok, load_in.at[0]),
        pltpu.make_async_copy(mem_in, mem, load_in.at[1]),
    ]
    for copy in taken:
        copy.start()
    length, width = tok.shape
    held = {0: w_qkv, 1: w_out, 2: w_cq, 3: w_ckv, count - 1: small}
    loads = {}

    def fetch(k):
        which, row, rows, col, cols, split, _ = chunks[k]
        if which not in held:
            return
        loads[k] = pltpu.make_async_copy(
            fulls[which].at[..., pl.ds(col, cols)], held[which].at[..., pl.ds(col, cols)], load.at[k]
        )
        loads[k].start()

    def chunk_of(which, col):
        return [k for k, c in enumerate(chunks) if c[0] == which and c[3] == col][0]

    def weight(ref, col, cols):
        flat = ref.shape[:-2]
        return ref[..., pl.ds(col, cols)].reshape(math.prod(flat) * ref.shape[-2], cols)

    def give(at, ref):
        copy = pltpu.make_async_copy(ref, outs[at], store.at[at])
        copy.start()
        given.append(copy)

    given = []

    def project(t):
        def run():
            loads[chunk_of(0, t * 512)].wait()
            if t == 0:
                taken[0].wait()
            qkv[:, pl.ds(t * 512, 512)] = dot(tok[...], weight(w_qkv, t * 512, 512)).astype(BF)
            if t == 2:
                give(0, qkv)

        return run

    def columns():
        own_row = own_seg[...].astype(F32)
        segment_ranges(own_row, far_seg[...].astype(F32), ranges)
        cols[...] = ranges[...].astype(F32).T.astype(jnp.int32)
        give(6, ranges)
        give(5, cols)
        seg_col[...] = jnp.broadcast_to(own_row, (8, length)).T

    def attend_self(b):
        def run():
            q0, limit = b * DENSE, (b + 1) * DENSE
            same = seg_col[pl.ds(q0, DENSE), 0:1] == own_seg[:, pl.ds(0, limit)].astype(F32)
            key = lax.broadcasted_iota(jnp.int32, (DENSE, limit), 1)
            query = q0 + lax.broadcasted_iota(jnp.int32, (DENSE, limit), 0)
            dense_attend(qkv, 0, q0, qkv, width, 2 * width, limit, same & (key <= query), o1)
            if limit == length:
                give(1, o1)

        return run

    def pairs(t):
        def run():
            loads[chunk_of(3, t * 512)].wait()
            if t == 0:
                taken[1].wait()
            ckv[:, pl.ds(t * 512, 512)] = dot(mem[...], weight(w_ckv, t * 512, 512)).astype(BF)
            if t == 1:
                give(4, ckv)

        return run

    def params():
        loads[chunk_of(count - 1, 0)].wait()
        each = sizes[count - 1]
        flat = small[...].reshape(math.prod(small.shape[:-2]), small.shape[-2], small.shape[-1])
        par[...] = jnp.concatenate([flat[w, :, :each].astype(F32) for w in range(flat.shape[0])], axis=1)
        give(7, par)

    def hidden(t):
        def run():
            if t == 0:
                loads[chunk_of(1, 0)].wait()
                loads[chunk_of(2, 0)].wait()
            rows = pl.ds(t * 256, 256)
            resid = tok[rows, :].astype(F32) * par[6:7, :] + dot(o1[rows, :], weight(w_out, 0, width))
            r1[rows, :] = resid
            normal, _ = norm_parts(resid)
            low = (normal * par[0:1, :] + par[3:4, :]).astype(BF)
            cq[rows, :] = dot(low, weight(w_cq, 0, width)).astype(BF)
            if (t + 1) * 256 == length:
                give(2, r1)
                give(3, cq)

        return run

    work = [((), 0.5, columns)]
    work += [((chunk_of(0, t * 512),), 0.8, project(t)) for t in range(3)]
    work += [((), 0.2 + 0.15 * b, attend_self(b)) for b in range(length // DENSE)]
    work += [((chunk_of(count - 1, 0),), 0.2, params)]
    work += [((chunk_of(1, 0), chunk_of(2, 0)), 0.9, hidden(t)) for t in range(length // 256)]
    work += [((chunk_of(3, t * 512),), 0.8, pairs(t)) for t in range(2)]

    def advance(k, s):
        whole = gather.advance(k, s)
        if whole:
            fetch(k)
        return whole

    run_plan(gather.events(), advance, work)
    gather.finish()
    for copy in given:
        copy.wait()


def front(mesh, shards, tokens, memory, own_seg, far_seg, rows, collective):
    early, late = stage_orders(mesh)
    digits = tuple(size for _, size in wide_parts(mesh))
    small_order = [s for s in early if not isinstance(s, str)]
    count = len(shards)
    length, width = tokens.shape
    chunks = []
    for which in [0, count - 1] + list(range(1, count - 1)):
        high, cols = shards[which].shape
        if cols < 512:
            chunks.append((which, 0, high, 0, cols, False, small_order))
            continue
        cut = max(1, high // 64)
        for r in range(cut):
            for c in range(cols // 512):
                order = late if len(chunks) % 8 in LATE_CHUNKS else early
                chunks.append((which, r * (high // cut), high // cut, c * 512, 512, True, order))
    copies = sum(stage_copies(mesh, c[6]) for c in chunks)
    fulls = tuple(jax.ShapeDtypeStruct(digits + s.shape, s.dtype) for s in shards)
    made = (
        shaped(length, 3 * width), shaped(length, width), shaped(length, width, dtype=F32), shaped(length, width),
        shaped(length, 2 * width), shaped(length, 8, dtype=jnp.int32), shaped(8, length, dtype=jnp.int32),
        shaped(16, width, dtype=F32),
    )
    vm = pltpu.VMEM
    kept = [0, 1, 2, 3, count - 1]
    results = pl.pallas_call(
        functools.partial(front_kernel, mesh, chunks, count, [s.shape[0] for s in shards[:-1]] + [rows]),
        out_shape=fulls + made,
        in_specs=[pl.BlockSpec(memory_space=pl.ANY)] * (count + 2) + [pl.BlockSpec(memory_space=vm)] * 2,
        out_specs=tuple(pl.BlockSpec(memory_space=pl.ANY) for _ in fulls + made),
        scratch_shapes=[vm(m.shape, m.dtype) for m in made]
        + [vm(tokens.shape, BF), vm(memory.shape, BF)]
        + [vm(fulls[k].shape, BF) for k in kept]
        + [
            vm((length, 8), F32),
            pltpu.SemaphoreType.DMA((copies,)),
            pltpu.SemaphoreType.DMA((copies,)),
            pltpu.SemaphoreType.DMA((len(chunks),)),
            pltpu.SemaphoreType.DMA((len(chunks),)),
            pltpu.SemaphoreType.DMA((2,)),
            pltpu.SemaphoreType.DMA((len(made),)),
        ],
        compiler_params=pltpu.CompilerParams(
            collective_id=collective, has_side_effects=True, vmem_limit_bytes=VMEM_BYTES
        ),
        name="front",
    )(*shards, tokens, memory, own_seg.reshape(1, length), far_seg.reshape(1, length))
    return [full.reshape((-1, full.shape[-1])) for full in results[:count]], results[count:]


LATE_CHUNKS = (1, 4, 6)


def layer(mesh, tokens, memory, segments, cotangent, weights, made, rows):
    w_qkv, w_out, w_cq, w_ckv, w_co, w_in, w_down, _ = weights
    qkv, o1, r1, cq, ckv, cols, ranges, par = made
    arrays = (cq, ckv, cols, ranges, par, r1, w_co, w_in, w_down, cotangent)
    out, dr2, dcq, dckv, g_in, g_down, g_co, vec_two = middle(ranges, arrays)
    inputs = (dr2, dcq, w_cq, r1, par, vec_two, tokens, w_out, o1, memory, dckv, qkv, w_ckv, w_qkv)
    return out, back(mesh, (g_in, g_down, g_co), inputs, segments, rows, 2)


PACE_US, LAG_US, LAST_LAG_US = 1.3, 6.0, 3.0
PATTERN = "yxyxyxyxyxyxyxyxy"
FAR_COLS, FAR_PARTS = 512, 4


def reduce_orders(mesh):
    digits = list(range(len(wide_parts(mesh))))[::-1]
    return {
        "x": ["core", "x"] + digits,
        "y": ["core", digits[0], "x"] + digits[1:],
        "z": ["core"] + digits[::-1] + ["x"],
        "n": ["core"] + digits + ["sum x"],
    }


def stage_peers(mesh, stage):
    sizes = [size for _, size in wide_parts(mesh)]
    if stage == "all":
        return [d for d in itertools.product(*[range(size) for size in sizes]) if any(d)]
    return [tuple(d if j == stage else 0 for j in range(len(sizes))) for d in range(1, sizes[stage])]


class Chunk:
    def __init__(self, mesh, which, sub, rows, col, cols, order, split, held):
        self.which, self.sub, self.rows, self.col, self.cols = which, sub, rows, col, cols
        self.order, self.split, self.held = order, split, held
        sizes = [size for _, size in wide_parts(mesh)]
        self.received = []
        self.copies = 2 if split else 0
        lanes = cols // 2 if split else cols
        self.shape = tuple(sizes) + (rows, lanes)
        for stage in order:
            if isinstance(stage, str) and stage != "all":
                lanes = lanes // 2 if stage == "x" and split else lanes
                count = 1
            else:
                sizes = [1 if stage in ("all", j) else size for j, size in enumerate(sizes)]
                count = len(stage_peers(mesh, stage))
            self.received.append([tuple(sizes) + (rows, lanes)] * count)
            self.copies += count


class Reduce:
    def __init__(self, mesh, place, chunks, grads, held, received, sums, send, recv, own):
        self.mesh, self.place, self.chunks, self.grads, self.sums = mesh, place, chunks, grads, sums
        self.send, self.recv, self.used, self.sent = send, recv, 0, []
        held, received = list(held), list(received)
        self.states = []
        for k, chunk in enumerate(chunks):
            half = chunk.cols // 2 if chunk.split else chunk.cols
            source = grads[chunk.which]
            near = chunk.col + place.core * half if chunk.split else chunk.col
            far = chunk.col + (1 - place.core) * half if chunk.split else chunk.col
            state = {"copies": [], "bufs": [], "mine": None}
            if chunk.held:
                cur = (held.pop(0), 0, half, None)
                mine = pltpu.make_async_copy(self.view((source, near, half, chunk.sub)), cur[0], own.at[k])
                mine.start()
                state["mine"] = mine
            else:
                cur = (source, near, half, chunk.sub)
            state["cur"], state["other"] = cur, (source, far, half, chunk.sub)
            state["pool"] = [[received.pop(0) for _ in shapes] for shapes in chunk.received]
            self.states.append(state)

    def view(self, cur, digits=None, lane=None, size=None):
        ref, off, lanes, sub = cur
        spot = [slice(None)] * len(self.place.parts)
        for j, index in (digits or {}).items():
            spot[j] = pl.ds(index, 1)
        if sub is not None:
            spot.append(sub)
        start = off if lane is None else off + lane
        if not isinstance(start, int):
            start = pl.multiple_of(start, 128)
        return ref.at[tuple(spot) + (slice(None), pl.ds(start, size or lanes))]

    def ship(self, src, target, peer):
        at = self.used
        self.used += 1
        copy = pltpu.make_async_remote_copy(
            src_ref=src, dst_ref=target, send_sem=self.send.at[at], recv_sem=self.recv.at[at],
            device_id=peer, device_id_type=pl.DeviceIdType.MESH,
        )
        copy.start()
        self.sent.append(copy)
        return copy

    def spots(self, stage, offsets):
        return {
            j: self.place.flip(self.place.digits[j], d, self.place.parts[j][1])
            for j, d in enumerate(offsets)
            if stage in ("all", j)
        }

    def begin(self, k, s):
        chunk, state, place = self.chunks[k], self.states[k], self.place
        stage, cur = chunk.order[s], state["cur"]
        bufs = state["pool"][s]
        if stage == "core":
            state["copies"] = [self.ship(self.view(state["other"]), bufs[0], place.core_peer())]
        elif stage == "sum x":
            state["copies"] = [self.ship(self.view(cur), bufs[0], place.x_peer())]
        elif stage == "x":
            src = self.view(cur)
            if chunk.split:
                half = cur[2] // 2
                src = self.view(cur, lane=(1 - place.x) * half, size=half)
            state["copies"] = [self.ship(src, bufs[0], place.x_peer())]
        else:
            for buf, offsets in zip(bufs, stage_peers(self.mesh, stage)):
                src = self.view(cur, self.spots(stage, offsets))
                state["copies"].append(self.ship(src, buf, place.wide_peer(offsets)))

    def end(self, k, s):
        chunk, state, place = self.chunks[k], self.states[k], self.place
        stage, cur, bufs = chunk.order[s], state["cur"], state["pool"][s]
        for copy in state["copies"]:
            copy.wait_recv()
        state["copies"] = []
        if stage == "core":
            if state["mine"] is not None:
                state["mine"].wait()
            mine = self.view(cur)
        elif stage == "sum x":
            mine = self.view(cur)
        elif stage == "x":
            half = cur[2] // 2 if chunk.split else cur[2]
            mine = self.view(cur, lane=place.x * half, size=half) if chunk.split else self.view(cur)
        else:
            mine = self.view(cur, self.spots(stage, (0,) * len(place.parts)))
        if len(bufs) == 1:
            bufs[0][...] = mine[...] + bufs[0][...]
        else:
            value = mine[...].astype(F32)
            for buf in bufs:
                value = value + buf[...].astype(F32)
            bufs[0][...] = value.astype(BF)
        state["cur"] = (bufs[0], 0, bufs[0].shape[-1], None)

    def out_view(self, k, size):
        chunk, start = self.chunks[k], self.chunks[k].col
        if size < chunk.cols:
            start = start + self.place.core * (chunk.cols // 2)
        if size < chunk.cols // 2:
            start = start + self.place.x * (chunk.cols // 4)
        if not isinstance(start, int):
            start = pl.multiple_of(start, 128)
        return self.sums[chunk.which].at[pl.ds((chunk.sub or 0) * chunk.rows, chunk.rows), pl.ds(start, size)]

    def advance(self, k, s):
        chunk, state = self.chunks[k], self.states[k]
        stages = len(chunk.order)
        if 0 < s <= stages:
            self.end(k, s - 1)
        if s < stages:
            self.begin(k, s)
            return
        if s > stages:
            for copy in state["copies"]:
                copy.wait_recv()
            state["copies"] = []
        summed = "sum x" in chunk.order
        if s == stages:
            parts = 1 if not chunk.split else 2 if summed else 4
            view = self.out_view(k, chunk.cols // parts)
            view[...] = state["cur"][0][...].reshape(view.shape)
            if chunk.split:
                peer = self.place.core_peer() if summed else self.place.x_peer()
                state["copies"] = [self.ship(view, view, peer)]
        elif s == stages + 1 and chunk.split and not summed:
            view = self.out_view(k, chunk.cols // 2)
            state["copies"] = [self.ship(view, view, self.place.core_peer())]

    def finish(self):
        for copy in self.sent:
            copy.wait_send()


def run_back(reduce, chunks, work):
    ready, now = {}, 0.0
    for us, _, gives in work:
        now += us
        for k in gives:
            ready[k] = now
    events, free = [], 0.0
    for k, chunk in enumerate(chunks):
        begin = max(free, ready.get(k, 0.0))
        free = begin + (PACE_US if chunk.split else 0.0)
        lag = LAST_LAG_US if k >= len(chunks) - 3 else LAG_US
        events += [(begin + s * lag, k, s) for s in range(len(chunk.order) + 3)]
    made, now, work = {k for k in range(len(chunks)) if k not in ready}, 0.0, list(work)
    for time, k, s in sorted(events):
        while work and (now < time or k not in made):
            us, run, gives = work.pop(0)
            run()
            made |= set(gives)
            now += us
        now = max(now, time)
        reduce.advance(k, s)
    for _, run, _ in work:
        run()


def back_kernel(mesh, chunks, count, *refs):
    far, rest = refs[:3], refs[3:]
    inputs, rest = rest[:15], rest[15:]
    sums, rest = rest[:count], rest[count:]
    gt_out, gm_out, rest = rest[0], rest[1], rest[2:]
    loaded, rest = rest[:14], rest[14:]
    (dk_acc, dv_acc, dqkv, h1, da, do1, g_cross, g_out, g_qkv, vectors, seg_col) = rest[:11]
    rest = rest[11:]
    held, rest = rest[: sum(c.held for c in chunks)], rest[sum(c.held for c in chunks) :]
    received, (send, recv, own, load, store) = rest[:-5], rest[-5:]
    own_seg = inputs[14]
    place = Place(mesh)
    place.greet(True)
    grads = list(far) + [g_cross, g_out, vectors, g_qkv]
    reduce = Reduce(mesh, place, chunks, grads, held, received, sums, send, recv, own)
    loads = [pltpu.make_async_copy(src, dst, load.at[i]) for i, (src, dst) in enumerate(zip(inputs[:14], loaded))]
    waiting = list(range(14))
    (dr2, dq, w_cq, r1, par, vec_two, tok, w_out, o1, mem, dckv, qkv, w_ckv, w_qkv) = loaded
    length, width = tok.shape
    given = []
    vec = [jnp.zeros((1, width), F32) for _ in range(3)]

    def fetch(first, last):
        def run():
            for copy in loads[first:last]:
                copy.start()

        return run

    def need(upto):
        while waiting and waiting[0] <= upto:
            loads[waiting.pop(0)].wait()

    def give(at, ref, out):
        copy = pltpu.make_async_copy(ref, out, store.at[at])
        copy.start()
        given.append(copy)

    def hidden(t):
        def run():
            need(7)
            if t == 0:
                seg_col[...] = jnp.broadcast_to(own_seg[...].astype(F32), (8, length)).T
                dk_acc[...] = jnp.zeros_like(dk_acc)
                dv_acc[...] = jnp.zeros_like(dv_acc)
            rows = pl.ds(t * 256, 256)
            grad = dr2[rows, :] * par[7:8, :] + dot_nt(dq[rows, :], w_cq[...])
            normal, scale = norm_parts(r1[rows, :])
            h1[rows, :] = (normal * par[0:1, :] + par[3:4, :]).astype(BF)
            vec[0] += down_sum(grad * normal)
            vec[1] += down_sum(grad)
            back = norm_back(grad, normal, scale, par[0:1, :])
            vec[2] += down_sum(tok[rows, :].astype(F32) * back)
            dr2[rows, :] = back
            low = back.astype(BF)
            da[rows, :] = low
            do1[rows, :] = dot_nt(low, w_out[...]).astype(BF)
            if (t + 1) * 256 == length:
                every = jnp.concatenate(vec + [vec_two[3:6, :], vec_two[0:3, :], jnp.zeros((7, width), F32)], axis=0)
                wide = mesh.shape["wide"]
                each = width // wide
                for w in range(wide):
                    part = every[:, w * each : (w + 1) * each]
                    part = jnp.concatenate([part, jnp.zeros((16, 128 - each), F32)], axis=1)
                    spot, rest = [], w
                    for low_bit, size in place.parts:
                        spot.append((w >> low_bit) % size)
                    vectors[tuple(spot)] = part.astype(BF)

        return run

    def put(ref, at, cols, value):
        ref[..., pl.ds(at, cols)] = value.astype(BF).reshape(ref.shape[:-1] + (cols,))

    def grad_out():
        need(8)
        put(g_out, 0, width, dot_tn(o1[...], da[...]))

    def grad_cq():
        put(g_cross, 0, width, dot_tn(h1[...], dq[...]))

    def grad_ckv(t):
        def run():
            need(10)
            put(g_cross, (t + 1) * width, width, dot_tn(mem[...], dckv[:, pl.ds(t * width, width)]))

        return run

    def grad_mem(t):
        def run():
            need(12)
            rows = pl.ds(t * 256, 256)
            r1[rows, :] = dot_nt(dckv[rows, :], w_ckv[...])
            if (t + 1) * 256 == length:
                give(0, r1, gm_out)

        return run

    def attend(b, g):
        def run():
            need(11)
            limit = (b + 1) * DENSE
            mine = own_seg[:, b * DENSE : (b + 1) * DENSE].astype(F32)
            same = seg_col[pl.ds(0, limit), 0:1] == jnp.concatenate([mine] * SIDE, axis=1)
            key = lax.broadcasted_iota(jnp.int32, (limit, SIDE * DENSE), 0)
            query = lax.rem(lax.broadcasted_iota(jnp.int32, (limit, SIDE * DENSE), 1), DENSE) + b * DENSE
            shift = jnp.where(same & (key <= query), 0.0, NEGATIVE)
            dense_attend_bwd(qkv, do1, b * DENSE, limit, shift, dqkv, dk_acc, dv_acc, g)

        return run

    def grad_qkv(t):
        def run():
            if t == 1:
                dqkv[:, width : 2 * width] = dk_acc[...].astype(BF)
            if t == 2:
                dqkv[:, 2 * width :] = dv_acc[...].astype(BF)
            put(g_qkv, t * width, width, dot_tn(tok[...], dqkv[:, pl.ds(t * width, width)]))

        return run

    def grad_tok(t):
        def run():
            need(13)
            rows = pl.ds(t * 256, 256)
            dr2[rows, :] = dr2[rows, :] * par[6:7, :] + dot_nt(dqkv[rows, :], w_qkv[...])
            if (t + 1) * 256 == length:
                give(1, dr2, gt_out)

        return run

    def chunks_of(which, col=None):
        return [k for k, c in enumerate(chunks) if c.which == which and col in (None, c.col)]

    parts = length // 256
    work = [(0.1, fetch(0, 8), [])]
    work += [(1.2, hidden(t), chunks_of(5) if t + 1 == parts else []) for t in range(parts)]
    work[2:2] = [(0.1, fetch(8, 14), [])]
    work += [(0.9, grad_out, chunks_of(4)), (0.9, grad_cq, chunks_of(3, 0))]
    work += [(0.9, grad_ckv(t), chunks_of(3, (t + 1) * width)) for t in range(2)]
    work += [(0.25 + 0.25 * b, attend(b, g), []) for b in range(length // DENSE) for g in range(width // GROUP)]
    work += [(1.0, grad_qkv(t), chunks_of(6, t * width)) for t in range(3)]
    work += [(0.4, grad_mem(t), []) for t in range(parts)]
    work += [(0.6, grad_tok(t), []) for t in range(parts)]
    run_back(reduce, chunks, work)
    need(13)
    reduce.finish()
    for copy in given:
        copy.wait()


def dense_attend_bwd(qkv, do_ref, q0, limit, shift, dqkv, dk_acc, dv_acc, g):
    width = do_ref.shape[1]
    factor = HD**-0.5
    rows = lax.broadcasted_iota(jnp.int32, (SIDE * DENSE, GROUP), 0) // DENSE
    heads = lax.broadcasted_iota(jnp.int32, (SIDE * DENSE, GROUP), 1) // HD
    do_mask = jnp.where(rows == heads, 1.0, 0.0).astype(BF)
    q_mask = jnp.where(rows == heads, factor, 0.0).astype(BF)
    places = lax.broadcasted_iota(jnp.int32, (DENSE, GROUP), 1) // HD
    lanes = pl.ds(g * GROUP, GROUP)
    query = jnp.concatenate([qkv[pl.ds(q0, DENSE), lanes]] * SIDE, axis=0) * q_mask
    grad = jnp.concatenate([do_ref[pl.ds(q0, DENSE), lanes]] * SIDE, axis=0) * do_mask
    keys = qkv[pl.ds(0, limit), pl.ds(width + g * GROUP, GROUP)]
    values = qkv[pl.ds(0, limit), pl.ds(2 * width + g * GROUP, GROUP)]
    score = dot_nt(keys, query) + shift
    slopes = dot_nt(values, grad)
    raised = jnp.exp(score - jnp.max(score, axis=0, keepdims=True))
    probs = raised * (1.0 / down_sum(raised))
    delta = (probs * (slopes - down_sum(probs * slopes))).astype(BF)
    dv_acc[pl.ds(0, limit), lanes] += dot(probs.astype(BF), grad)
    dk_acc[pl.ds(0, limit), lanes] += dot(delta, query)
    stacked = dot_tn(delta, keys)
    dq = stacked[:DENSE]
    for h in range(1, SIDE):
        dq = jnp.where(places == h, stacked[h * DENSE : (h + 1) * DENSE], dq)
    dqkv[pl.ds(q0, DENSE), lanes] = (dq * factor).astype(BF)


def back(mesh, far, inputs, own_seg, rows, collective):
    kinds = reduce_orders(mesh)
    digits = tuple(size for _, size in wide_parts(mesh))
    wide = mesh.shape["wide"]
    length, width = inputs[0].shape
    each = width // wide
    views, chunks, sums = [], [], []

    def add(which, sub, high, cols, split, held):
        for j in range(sub or 1):
            unit = FAR_COLS if which == 0 else min(cols, 512)
            for c in range(cols // unit):
                order = kinds[PATTERN[len(chunks) % len(PATTERN)]]
                at = j if sub is not None else None
                chunks.append(Chunk(mesh, which, at, high, c * unit, unit, order, split, held))

    for which, grad in enumerate(far):
        high, cols = grad.shape[0] // wide, grad.shape[1]
        sub = FAR_PARTS if high * wide > width else 1
        views.append(grad.reshape(digits + (sub, high // sub, cols)))
        sums.append(shaped(high, cols))
        add(which, sub, high // sub, cols, True, True)
    for which, cols in ((3, 3 * width), (4, width), (5, 128), (6, 3 * width)):
        high, split = (16, False) if which == 5 else (each, True)
        sums.append(shaped(high, cols))
        add(which, None, high, cols, split, False)
    vm = pltpu.VMEM
    arrays = list(inputs)
    scratch = [vm(a.shape, a.dtype) for a in arrays]
    scratch += [vm((length, width), F32)] * 2 + [vm((length, 3 * width), BF)] + [vm((length, width), BF)] * 3
    scratch += [vm(digits + (each, cols), BF) for cols in (3 * width, width, 3 * width)]
    scratch += [vm(digits + (16, 128), BF), vm((length, 8), F32)]
    scratch += [vm(c.shape, BF) for c in chunks if c.held]
    scratch += [vm(shape, BF) for c in chunks for shapes in c.received for shape in shapes]
    copies = sum(c.copies for c in chunks)
    scratch += [pltpu.SemaphoreType.DMA((n,)) for n in (copies, copies, len(chunks), len(arrays), 2)]
    large = shaped(length, width, dtype=F32)
    return pl.pallas_call(
        functools.partial(back_kernel, mesh, chunks, len(sums)),
        out_shape=tuple(sums) + (large, large),
        in_specs=[pl.BlockSpec(memory_space=pl.ANY)] * (len(far) + len(arrays)) + [pl.BlockSpec(memory_space=vm)],
        out_specs=tuple(pl.BlockSpec(memory_space=vm) for _ in sums) + (pl.BlockSpec(memory_space=pl.ANY),) * 2,
        scratch_shapes=scratch,
        compiler_params=pltpu.CompilerParams(
            collective_id=collective, has_side_effects=True, vmem_limit_bytes=VMEM_BYTES
        ),
        name="back",
    )(*views, *arrays, own_seg.reshape(1, length))


def finish_kernel(count, rows, *refs):
    s_in, s_down, s_co, s_cross, s_out, s_vec, s_qkv = refs[:count]
    large, outs, held, sems = refs[count : count + 2], refs[count + 2 : -3], refs[-3:-1], refs[-1]
    moves = [pltpu.make_async_copy(large[i], held[i], sems.at[i]) for i in range(2)]
    for move in moves:
        move.start()
    width = s_out.shape[1]
    plain = (s_qkv[...], s_out[...], s_cross[:, :width], s_cross[:, width:], s_co[...], s_in[...], s_down[...])
    for value, out in zip(plain, outs[2:]):
        out[...] = value.astype(F32)
    for i in range(2):
        moves[i].wait()
        moves[i] = pltpu.make_async_copy(held[i], outs[i], sems.at[i])
        moves[i].start()
    vectors = s_vec[...].astype(F32)
    for at, out in enumerate(outs[2 + len(plain) :]):
        for j in range(3):
            out[j : j + 1, :] = vectors[3 * j + at : 3 * j + at + 1, :rows]
    for move in moves:
        move.wait()


def finish(sums, large, shapes, rows):
    vmem = pl.BlockSpec(memory_space=pltpu.VMEM)
    anywhere = pl.BlockSpec(memory_space=pl.ANY)
    outs = [shaped(*a.shape, dtype=F32) for a in large] + [shaped(*s, dtype=F32) for s in shapes]
    return pl.pallas_call(
        functools.partial(finish_kernel, len(sums), rows),
        out_shape=tuple(outs),
        in_specs=[vmem] * len(sums) + [anywhere] * 2,
        out_specs=(anywhere,) * 2 + (vmem,) * len(shapes),
        scratch_shapes=[pltpu.VMEM(a.shape, F32) for a in large] + [pltpu.SemaphoreType.DMA((2,))],
        compiler_params=pltpu.CompilerParams(vmem_limit_bytes=VMEM_BYTES),
        name="finish",
    )(*sums, *large)


def body(
    mesh,
    tokens,
    memory,
    target_segments,
    memory_segments,
    self_qkv,
    self_out,
    cross_q,
    cross_kv,
    cross_out,
    ffn_in,
    ffn_out,
    norm_gain,
    norm_bias,
    omega,
    cotangent,
):
    wide = mesh.shape["wide"]
    rows = self_qkv.shape[0]
    width = rows * wide
    small = jnp.concatenate([norm_gain, norm_bias, omega], axis=1).T
    small = jnp.pad(small, ((0, 7), (0, 128 - rows)))
    weights, made = front(
        mesh, (self_qkv, self_out, cross_q, cross_kv, cross_out, ffn_in, ffn_out, small),
        tokens, memory, target_segments, memory_segments, rows, 1,
    )
    output, (*sums, grad_tokens, grad_memory) = layer(
        mesh, tokens, memory, target_segments, cotangent, weights, made, rows
    )
    shapes = ((rows, 3 * width), (rows, width), (rows, width), (rows, 2 * width), (rows, width))
    shapes += (ffn_in.shape, ffn_out.shape, (3, rows), (3, rows), (3, rows))
    grad_tokens, grad_memory, *summed = finish(sums, (grad_tokens, grad_memory), shapes, rows)
    summed = tuple(summed[:7]) + tuple(vector.T for vector in summed[7:])
    return (output, grad_tokens, grad_memory) + summed


def solution(mesh):
    in_specs = (
        P(("narrow", "wide"), None),
        P(("narrow", "wide"), None),
        P(("narrow", "wide")),
        P(("narrow", "wide")),
        P("wide", None),
        P("wide", None),
        P("wide", None),
        P("wide", None),
        P("wide", None),
        P("wide", None),
        P("wide", None),
        P("wide", None),
        P("wide", None),
        P("wide", None),
        P(("narrow", "wide"), None),
    )
    out_specs = (
        P(("narrow", "wide"), None),
        P(("narrow", "wide"), None),
        P(("narrow", "wide"), None),
        P("wide", None),
        P("wide", None),
        P("wide", None),
        P("wide", None),
        P("wide", None),
        P("wide", None),
        P("wide", None),
        P("wide", None),
        P("wide", None),
        P("wide", None),
    )
    return jax.shard_map(functools.partial(body, mesh), mesh=mesh, in_specs=in_specs, out_specs=out_specs, check_vma=False)
```

```python
import functools
import itertools
import math

import jax
import jax.numpy as jnp
from jax import lax
from jax.experimental import pallas as pl
from jax.experimental.pallas import tpu as pltpu
from jax.sharding import PartitionSpec as P

HD = 64

EPSILON = 1e-05
NEGATIVE = -1000000000.0
SEGS = 32


def wide_parts(mesh):
    bits = mesh.shape["wide"].bit_length() - 1
    low = [(0, 1)] if bits % 2 else []
    low = low + [(at, 2) for at in range(bits % 2, bits, 2)]
    return [(at, 2**count) for at, count in low[::-1]]


class Place:
    def __init__(self, mesh):
        self.parts = wide_parts(mesh)
        self.n = lax.axis_index("narrow")
        self.w = lax.axis_index("wide")
        self.core = lax.rem(self.n, 2)
        self.x = lax.div(self.n, 2)
        self.digits = [lax.rem(lax.div(self.w, 2**low), size) for low, size in self.parts]

    def flip(self, value, d, size):
        out = 0
        bit = 1
        while bit < size:
            digit = lax.rem(lax.div(value, bit), 2)
            out = out + bit * (1 - digit if d & bit else digit)
            bit *= 2
        return out

    def digit_peer(self, j, d):
        low, size = self.parts[j]
        other = self.flip(self.digits[j], d, size)
        return (self.n, self.w + (other - self.digits[j]) * 2**low)

    def x_peer(self):
        return ((1 - self.x) * 2 + self.core, self.w)

    def core_peer(self):
        return (self.x * 2 + 1 - self.core, self.w)

    def peers(self, stage):
        if stage == "x":
            return [self.x_peer()]
        if stage == "core":
            return [self.core_peer()]
        return [self.digit_peer(stage, d) for d in range(1, self.parts[stage][1])]

    def wide_peer(self, offsets):
        w = 0
        for (low, size), digit, d in zip(self.parts, self.digits, offsets):
            w = w + self.flip(digit, d, size) * 2**low
        return (self.n, w)

    def greet(self, whole=False):
        others = [self.x_peer(), self.core_peer()]
        if whole:
            choices = itertools.product(*[range(size) for _, size in self.parts])
            others += [self.wide_peer(d) for d in choices if any(d)]
        else:
            others += [p for j in range(len(self.parts)) for p in self.peers(j)]
        barrier = pltpu.get_barrier_semaphore()
        for peer in others:
            pl.semaphore_signal(barrier, inc=1, device_id=peer, device_id_type=pl.DeviceIdType.MESH)
        pl.semaphore_wait(barrier, len(others))


def stage_orders(mesh):
    count = len(wide_parts(mesh))
    early = list(range(count - 1)) + ["x", count - 1, "core"]
    late = list(range(count))[::-1] + ["x", "core"]
    return early, late


def stage_copies(mesh, order):
    parts = wide_parts(mesh)
    return sum(1 if isinstance(s, str) else parts[s][1] - 1 for s in order)


BF = jnp.bfloat16
F32 = jnp.float32
def dot(left, right):
    return lax.dot_general(left, right, (((1,), (0,)), ((), ())), preferred_element_type=F32)


def dot_nt(left, right):
    return lax.dot_general(left, right, (((1,), (1,)), ((), ())), preferred_element_type=F32)


def dot_tn(left, right):
    return lax.dot_general(left, right, (((0,), (0,)), ((), ())), preferred_element_type=F32)


def norm_parts(resid):
    middle = jnp.mean(resid, axis=-1, keepdims=True)
    centred = resid - middle
    spread = jnp.mean(centred * centred, axis=-1, keepdims=True)
    scale = lax.rsqrt(spread + EPSILON)
    return centred * scale, scale


def norm_back(grad, normal, scale, gain):
    scaled = grad * gain
    middle = jnp.mean(scaled, axis=-1, keepdims=True)
    along = jnp.mean(scaled * normal, axis=-1, keepdims=True)
    return (scaled - middle - normal * along) * scale


def down_sum(value):
    return jnp.sum(value, axis=0, keepdims=True)


QB = 64
WIN = 256
WIDER = 512
GROUP = 256
SIDE = GROUP // HD
VMEM_BYTES = 56 * 2**20


def head_masks(scale):
    rows = lax.broadcasted_iota(jnp.int32, (SIDE * QB, GROUP), 0) // QB
    lanes = lax.broadcasted_iota(jnp.int32, (SIDE * QB, GROUP), 1) // HD
    return jnp.where(rows == lanes, scale, 0.0).astype(BF)


def pick_heads(stacked):
    lanes = lax.broadcasted_iota(jnp.int32, (QB, GROUP), 1) // HD
    out = stacked[:QB]
    for h in range(1, SIDE):
        out = jnp.where(lanes == h, stacked[h * QB : (h + 1) * QB], out)
    return out


def stack_heads(block, mask):
    return jnp.concatenate([block] * SIDE, axis=0) * mask


class Block:
    def __init__(self, b, ranges_s, length):
        self.b = b
        self.q0 = pl.multiple_of(b * QB, QB)
        self.first = (ranges_s[1, self.q0] // 16) * 16
        self.last = ranges_s[2, self.q0 + QB - 1]
        self.span = self.last - self.first
        self.length = length

    def window(self, step, size):
        begin = self.first + step * size
        return begin, pl.multiple_of(jnp.minimum(begin, self.length - size), 16)


def for_blocks(count, at_a_time, make, together, steps):
    def one(t, carry):
        blocks = [make(t * at_a_time + i) for i in range(at_a_time)]
        span = blocks[0].span
        for block in blocks[1:]:
            span = jnp.maximum(span, block.span)

        @pl.when(span < WIN)
        def _():
            together(blocks, WIN)

        @pl.when((span >= WIN) & (span < WIDER))
        def _():
            together(blocks, WIDER)

        @pl.when(span >= WIDER)
        def _():
            for block in blocks:
                steps(block)

        return carry

    lax.fori_loop(0, count // at_a_time, one, 0)


def attend_fwd(q_ref, q_at, k_ref, k_at, v_at, ranges_s, cols_ref, o_ref):
    length = k_ref.shape[0]
    mask = head_masks(HD**-0.5)
    groups = range(o_ref.shape[1] // GROUP)

    def allowed(block, begin, start, size):
        low = cols_ref[pl.ds(block.q0, QB), 1:2]
        high = cols_ref[pl.ds(block.q0, QB), 2:3]
        places = start + lax.broadcasted_iota(jnp.int32, (QB, size), 1)
        ok = (places >= jnp.maximum(low, begin)) & (places <= high)
        return jnp.concatenate([ok] * SIDE, axis=0)

    def scores(block, g, start, size, ok):
        query = stack_heads(q_ref[pl.ds(block.q0, QB), pl.ds(q_at + g * GROUP, GROUP)], mask)
        keys = k_ref[pl.ds(start, size), pl.ds(k_at + g * GROUP, GROUP)]
        return jnp.where(ok, dot_nt(query, keys), NEGATIVE)

    def values(g, start, size):
        return k_ref[pl.ds(start, size), pl.ds(v_at + g * GROUP, GROUP)]

    def store(block, g, stacked):
        o_ref[pl.ds(block.q0, QB), pl.ds(g * GROUP, GROUP)] = pick_heads(stacked).astype(BF)

    def at_once(blocks, size):
        todo = []
        for block in blocks:
            begin, start = block.window(0, size)
            ok = allowed(block, begin, start, size)
            todo += [(block, g, start, scores(block, g, start, size, ok)) for g in groups]
        tops = [jnp.max(score, axis=-1, keepdims=True) for _, _, _, score in todo]
        raised = [jnp.exp(score - top) for (_, _, _, score), top in zip(todo, tops)]
        totals = [jnp.sum(r, axis=-1, keepdims=True) for r in raised]
        weights = [(r * (1.0 / total)).astype(BF) for r, total in zip(raised, totals)]
        mixed = [dot(w, values(g, start, size)) for w, (_, g, start, _) in zip(weights, todo)]
        for m, (block, g, _, _) in zip(mixed, todo):
            store(block, g, m)

    def steps(block):
        count = block.span // WIN + 1
        for g in groups:

            def score_at(k):
                begin, start = block.window(k, WIN)
                return start, scores(block, g, start, WIN, allowed(block, begin, start, WIN))

            def stats(k, state):
                top, total = state
                _, score = score_at(k)
                higher = jnp.maximum(top, jnp.max(score, axis=-1, keepdims=True))
                raised = jnp.sum(jnp.exp(score - higher), axis=-1, keepdims=True)
                return higher, total * jnp.exp(top - higher) + raised

            start_top = jnp.full((SIDE * QB, 1), 2 * NEGATIVE, F32)
            top, total = lax.fori_loop(0, count, stats, (start_top, jnp.zeros((SIDE * QB, 1), F32)))

            def mix(k, out):
                start, score = score_at(k)
                weights = jnp.exp(score - top) * (1.0 / total)
                return out + dot(weights.astype(BF), values(g, start, WIN))

            store(block, g, lax.fori_loop(0, count, mix, jnp.zeros((SIDE * QB, GROUP), F32)))

    for_blocks(
        q_ref.shape[0] // QB,
        4,
        lambda b: Block(b, ranges_s, length),
        at_once,
        steps,
    )


def attend_bwd(q_ref, q_at, k_ref, k_at, v_at, do_ref, ranges_s, lo_rows, hi_rows, dq_ref, dq_at, dk_acc, dv_acc):
    length = k_ref.shape[0]
    factor = HD**-0.5
    q_mask = head_masks(factor)
    do_mask = head_masks(1.0)
    groups = range(do_ref.shape[1] // GROUP)
    dk_acc[...] = jnp.zeros(dk_acc.shape, F32)
    dv_acc[...] = jnp.zeros(dv_acc.shape, F32)

    def keys(g, start, size):
        return k_ref[pl.ds(start, size), pl.ds(k_at + g * GROUP, GROUP)]

    def values(g, start, size):
        return k_ref[pl.ds(start, size), pl.ds(v_at + g * GROUP, GROUP)]

    def query(block, g):
        return stack_heads(q_ref[pl.ds(block.q0, QB), pl.ds(q_at + g * GROUP, GROUP)], q_mask)

    def grad(block, g):
        return stack_heads(do_ref[pl.ds(block.q0, QB), pl.ds(g * GROUP, GROUP)], do_mask)

    def allowed(block, begin, start, size):
        low = lo_rows[pl.ds(block.b, 1), :]
        high = hi_rows[pl.ds(block.b, 1), :]
        places = start + lax.broadcasted_iota(jnp.int32, (size, SIDE * QB), 0)
        return (places >= jnp.maximum(low, begin)) & (places <= high)

    def scores(block, g, start, size, ok):
        return jnp.where(ok, dot_nt(keys(g, start, size), query(block, g)), NEGATIVE)

    def accumulate(g, start, size, dv, dk):
        rows = pl.ds(start, size)
        lanes = pl.ds(g * GROUP, GROUP)
        dv_acc[rows, lanes] += dv
        dk_acc[rows, lanes] += dk

    def store(block, g, stacked):
        dq = pick_heads(stacked) * factor
        dq_ref[pl.ds(block.q0, QB), pl.ds(dq_at + g * GROUP, GROUP)] = dq.astype(BF)

    def at_once(blocks, size):
        todo, score, slopes = [], [], []
        for block in blocks:
            begin, start = block.window(0, size)
            ok = allowed(block, begin, start, size)
            for g in groups:
                todo.append((block, g, start))
                score.append(scores(block, g, start, size, ok))
                slopes.append(dot_nt(values(g, start, size), grad(block, g)))
        raised = [jnp.exp(s - jnp.max(s, axis=0, keepdims=True)) for s in score]
        probs = [r * (1.0 / down_sum(r)) for r in raised]
        delta = [(p * (s - down_sum(p * s))).astype(BF) for p, s in zip(probs, slopes)]
        dv = [dot(p.astype(BF), grad(block, g)) for p, (block, g, _) in zip(probs, todo)]
        dk = [dot(d, query(block, g)) for d, (block, g, _) in zip(delta, todo)]
        dq = [dot_tn(d, keys(g, start, size)) for d, (_, g, start) in zip(delta, todo)]
        for i, (block, g, start) in enumerate(todo):
            store(block, g, dq[i])
            accumulate(g, start, size, dv[i], dk[i])

    def steps(block):
        count = block.span // WIN + 1
        for g in groups:

            def score_at(k):
                begin, start = block.window(k, WIN)
                return start, scores(block, g, start, WIN, allowed(block, begin, start, WIN))

            def stats(k, state):
                top, total = state
                _, score = score_at(k)
                higher = jnp.maximum(top, jnp.max(score, axis=0, keepdims=True))
                return higher, total * jnp.exp(top - higher) + down_sum(jnp.exp(score - higher))

            start_top = jnp.full((1, SIDE * QB), 2 * NEGATIVE, F32)
            top, total = lax.fori_loop(0, count, stats, (start_top, jnp.zeros((1, SIDE * QB), F32)))

            def probs_of(k):
                start, score = score_at(k)
                return start, jnp.exp(score - top) * (1.0 / total), dot_nt(values(g, start, WIN), grad(block, g))

            def centre(k, middle):
                _, probs, slopes = probs_of(k)
                return middle + down_sum(probs * slopes)

            middle = lax.fori_loop(0, count, centre, jnp.zeros((1, SIDE * QB), F32))

            def last_pass(k, out):
                start, probs, slopes = probs_of(k)
                delta = (probs * (slopes - middle)).astype(BF)
                accumulate(g, start, WIN, dot(probs.astype(BF), grad(block, g)), dot(delta, query(block, g)))
                return out + dot_tn(delta, keys(g, start, WIN))

            store(block, g, lax.fori_loop(0, count, last_pass, jnp.zeros((SIDE * QB, GROUP), F32)))

    for_blocks(
        q_ref.shape[0] // QB,
        2,
        lambda b: Block(b, ranges_s, length),
        at_once,
        steps,
    )


def over_tiles(count, size, step):
    for t in range(count):
        step(t * size)


def gelu_parts(value):
    area = 0.5 * (1.0 + lax.erf(value * (0.5**0.5)))
    bell = jnp.exp(-0.5 * value * value) * 0.3989422804014327
    return value * area, area + value * bell


def middle_kernel(ranges_s, *refs):
    inputs, refs = refs[:10], refs[10:]
    outs, refs = refs[:8], refs[8:]
    loaded, refs = refs[:10], refs[10:]
    (out_ref, dr2_ref, dckv, g_in, g_down, g_co, vec_ref), refs = refs[:7], refs[7:]
    (o2_ref, do2_ref, r2_ref, h2_ref, z_ref, gp_ref, du_ref, dr3_ref, df_ref, da_ref), refs = refs[:10], refs[10:]
    lo_rows, hi_rows, load, store = refs
    loads = [pltpu.make_async_copy(src, dst, load.at[i]) for i, (src, dst) in enumerate(zip(inputs, loaded))]
    for copy in loads:
        copy.start()
    waiting, given = list(range(len(loads))), []
    (cq, ckv, cols, ranges, par, r1_ref, w_co, w_in, w_down, cot_ref) = loaded

    def need(upto):
        while waiting and waiting[0] <= upto:
            loads[waiting.pop(0)].wait()

    def give(at, ref):
        copy = pltpu.make_async_copy(ref, outs[at], store.at[at])
        copy.start()
        given.append(copy)

    tokens, width = r1_ref.shape
    wide = w_in.shape[1]
    need(3)
    attend_fwd(cq, 0, ckv, 0, width, ranges_s, cols, o2_ref)
    need(6)

    def resid_two(t):
        rows = pl.ds(t * 256, 256)
        hidden = norm_parts(r1_ref[rows, :])[0] * par[0:1, :] + par[3:4, :]
        resid = hidden * par[7:8, :] + dot(o2_ref[rows, :], w_co[...])
        r2_ref[rows, :] = resid
        h2_ref[rows, :] = (norm_parts(resid)[0] * par[1:2, :] + par[4:5, :]).astype(BF)

    for t in range(tokens // 256):
        resid_two(t)

    def up(at):
        lanes = pl.ds(at, 256)
        active, slope = gelu_parts(dot(h2_ref[...], w_in[:, lanes]))
        z_ref[:, lanes] = active.astype(BF)
        gp_ref[:, lanes] = slope

    need(7)
    over_tiles(wide // 256, 256, up)
    need(9)
    vec = [jnp.zeros((1, width), F32) for _ in range(6)]
    for t in range(tokens // 256):
        rows = pl.ds(t * 256, 256)
        hidden = norm_parts(r2_ref[rows, :])[0] * par[1:2, :] + par[4:5, :]
        resid = hidden * par[8:9, :] + dot(z_ref[rows, :], w_down[...])
        normal, scale = norm_parts(resid)
        out_ref[rows, :] = (normal * par[2:3, :] + par[5:6, :]).astype(BF)
        grad = cot_ref[rows, :].astype(F32)
        vec[0] += down_sum(grad * normal)
        vec[1] += down_sum(grad)
        back = norm_back(grad, normal, scale, par[2:3, :])
        vec[2] += down_sum(hidden * back)
        dr3_ref[rows, :] = back
        df_ref[rows, :] = back.astype(BF)

    give(0, out_ref)

    def grad_down(at):
        g_down[pl.ds(at, 256), :] = dot_tn(z_ref[:, pl.ds(at, 256)], df_ref[...]).astype(BF)

    over_tiles(wide // 256, 256, grad_down)
    give(5, g_down)

    def down(at):
        lanes = pl.ds(at, 256)
        grad = dot_nt(df_ref[...], w_down[pl.ds(at, 256), :])
        du_ref[:, lanes] = (grad * gp_ref[:, lanes]).astype(BF)

    over_tiles(wide // 256, 256, down)
    for t in range(tokens // 256):
        rows = pl.ds(t * 256, 256)
        grad = dr3_ref[rows, :] * par[8:9, :] + dot_nt(du_ref[rows, :], w_in[...])
        normal, scale = norm_parts(r2_ref[rows, :])
        vec[3] += down_sum(grad * normal)
        vec[4] += down_sum(grad)
        back = norm_back(grad, normal, scale, par[1:2, :])
        hidden = norm_parts(r1_ref[rows, :])[0] * par[0:1, :] + par[3:4, :]
        vec[5] += down_sum(hidden * back)
        dr2_ref[rows, :] = back
        low = back.astype(BF)
        da_ref[rows, :] = low
        do2_ref[rows, :] = dot_nt(low, w_co[...]).astype(BF)
    for k in range(6):
        vec_ref[k : k + 1, :] = vec[k]
    give(7, vec_ref)
    give(1, dr2_ref)

    def grad_up(at):
        lanes = pl.ds(at, 256)
        g_in[:, lanes] = dot_tn(h2_ref[...], du_ref[:, lanes]).astype(BF)

    over_tiles(wide // 256, 256, grad_up)
    give(4, g_in)

    def grad_co(at):
        lanes = pl.ds(at, 256)
        g_co[:, lanes] = dot_tn(o2_ref[...], da_ref[:, lanes]).astype(BF)

    over_tiles(width // 256, 256, grad_co)
    give(6, g_co)
    for b in range(tokens // QB):
        for at, ref in ((1, lo_rows), (2, hi_rows)):
            row = ranges[at : at + 1, b * QB : (b + 1) * QB]
            ref[b : b + 1, :] = jnp.concatenate([row] * SIDE, axis=1)
    dk_acc, dv_acc = gp_ref.at[:, pl.ds(0, width)], gp_ref.at[:, pl.ds(width, width)]
    attend_bwd(cq, 0, ckv, 0, width, do2_ref, ranges_s, lo_rows, hi_rows, df_ref, 0, dk_acc, dv_acc)
    give(2, df_ref)
    dckv[:, :width] = dk_acc[...].astype(BF)
    dckv[:, width:] = dv_acc[...].astype(BF)
    give(3, dckv)
    for copy in given:
        copy.wait()


def middle(ranges, arrays):
    cq, ckv, w_in = arrays[0], arrays[1], arrays[7]
    length, width = cq.shape
    ff = w_in.shape[1]
    vm, anywhere = pltpu.VMEM, pl.BlockSpec(memory_space=pl.ANY)
    outs = (
        shaped(length, width), shaped(length, width, dtype=F32), shaped(length, width), shaped(length, 2 * width),
        shaped(width, ff), shaped(ff, width), shaped(width, width), shaped(8, width, dtype=F32),
    )
    scratch = [vm(a.shape, a.dtype) for a in arrays]
    scratch += [vm(o.shape, o.dtype) for i, o in enumerate(outs) if i != 2]
    scratch += [vm((length, width), BF)] * 2 + [vm((length, width), F32), vm((length, width), BF), vm((length, ff), BF)]
    scratch += [vm((length, ff), F32), vm((length, ff), BF), vm((length, width), F32)] + [vm((length, width), BF)] * 2
    scratch += [vm((length // QB, SIDE * QB), jnp.int32)] * 2
    scratch += [pltpu.SemaphoreType.DMA((len(arrays),)), pltpu.SemaphoreType.DMA((len(outs),))]
    return pl.pallas_call(
        middle_kernel,
        out_shape=outs,
        in_specs=[pl.BlockSpec(memory_space=pltpu.SMEM)] + [anywhere] * len(arrays),
        out_specs=(anywhere,) * len(outs),
        scratch_shapes=scratch,
        compiler_params=pltpu.CompilerParams(vmem_limit_bytes=VMEM_BYTES),
        name="middle",
    )(ranges, *arrays)


def shaped(*dims, dtype=BF):
    return jax.ShapeDtypeStruct(dims, dtype)


STEP_US = 1.35
FIRST_CHUNKS, FIRST_LAG, LATER_LAG = 8, 4, 4


def run_plan(events, advance, work):
    now, whole, work = 0.0, set(), list(work)

    def do_work(until):
        nonlocal now
        while work and set(work[0][0]) <= whole and now < until:
            _, us, run = work.pop(0)
            run()
            now += us

    for time, k, s in events:
        do_work(time)
        now = max(now, time)
        if advance(k, s):
            whole.add(k)
    do_work(float("inf"))
    assert not work


DENSE = 128


class Gather:
    def __init__(self, place, chunks, shards, fulls, send, recv, own):
        self.place, self.chunks, self.shards, self.fulls = place, chunks, shards, fulls
        self.send, self.recv, self.used, self.sent = send, recv, 0, []
        self.states = []
        for k, chunk in enumerate(chunks):
            src, target = self.views(chunk, [])
            mine = pltpu.make_async_copy(src, target, own.at[k])
            mine.start()
            self.states.append({"done": [], "copies": [], "order": chunk[6], "mine": mine})

    def views(self, chunk, done):
        which, row, rows, col, cols, split, _ = chunk
        place = self.place
        quarter, half = cols // 4, cols // 2
        lanes = pl.ds(col, cols)
        if split:
            lanes = pl.ds(pl.multiple_of(col + place.core * half, 128), half)
            if "x" not in done:
                lanes = pl.ds(pl.multiple_of(col + place.core * half + place.x * quarter, 128), quarter)
        spot = tuple(slice(None) if j in done else place.digits[j] for j in range(len(place.parts)))
        target = self.fulls[which].at[spot + (pl.ds(row, rows), lanes)]
        if done:
            return target, target
        return self.shards[which].at[pl.ds(row, rows), lanes], target

    def advance(self, k, s):
        state = self.states[k]
        stages = len(state["order"])
        if s > stages:
            return False
        if s == 1:
            state["mine"].wait()
        for copy in state["copies"]:
            copy.wait_recv()
        state["copies"] = []
        if s == stages:
            return True
        stage = state["order"][s]
        src, target = self.views(self.chunks[k], state["done"])
        for peer in self.place.peers(stage):
            at = self.used
            self.used += 1
            copy = pltpu.make_async_remote_copy(
                src_ref=src, dst_ref=target, send_sem=self.send.at[at], recv_sem=self.recv.at[at],
                device_id=peer, device_id_type=pl.DeviceIdType.MESH,
            )
            copy.start()
            state["copies"].append(copy)
            self.sent.append(copy)
        state["done"] = state["done"] + [stage]
        return False

    def events(self):
        events = []
        for k, chunk in enumerate(self.chunks):
            lag = FIRST_LAG if k < FIRST_CHUNKS else LATER_LAG
            events += [(STEP_US * (k + s * lag), k, s) for s in range(len(chunk[6]) + 1)]
        return sorted(events, key=lambda e: (e[0], e[1]))

    def finish(self):
        for copy in self.sent:
            copy.wait_send()


def segment_ranges(own, far, out):
    width = own.shape[1]
    numbers = lax.broadcasted_iota(jnp.int32, (SEGS, width), 0).astype(F32)
    mine = (own == numbers).astype(F32)

    def counted(hit):
        return jnp.sum(mine * jnp.sum(hit.astype(F32), axis=1, keepdims=True), axis=0, keepdims=True)

    out[0:1, :] = counted(own < numbers).astype(jnp.int32)
    out[1:2, :] = counted(far < numbers).astype(jnp.int32)
    out[2:3, :] = (counted(far <= numbers) - 1.0).astype(jnp.int32)
    out[3:8, :] = jnp.zeros((5, width), jnp.int32)


def dense_attend(q_ref, q_at, q0, k_ref, k_at, v_at, limit, allowed, o_ref):
    rows = lax.broadcasted_iota(jnp.int32, (SIDE * DENSE, GROUP), 0) // DENSE
    lanes = lax.broadcasted_iota(jnp.int32, (SIDE * DENSE, GROUP), 1) // HD
    mask = jnp.where(rows == lanes, HD**-0.5, 0.0).astype(BF)
    shift = jnp.where(allowed, 0.0, NEGATIVE)
    shift = jnp.concatenate([shift] * SIDE, axis=0)
    places = lax.broadcasted_iota(jnp.int32, (DENSE, GROUP), 1) // HD
    for g in range(o_ref.shape[1] // GROUP):
        block = q_ref[pl.ds(q0, DENSE), pl.ds(q_at + g * GROUP, GROUP)]
        query = jnp.concatenate([block] * SIDE, axis=0) * mask
        score = dot_nt(query, k_ref[pl.ds(0, limit), pl.ds(k_at + g * GROUP, GROUP)]) + shift
        raised = jnp.exp(score - jnp.max(score, axis=-1, keepdims=True))
        total = jnp.sum(raised, axis=-1, keepdims=True)
        mixed = dot(raised.astype(BF), k_ref[pl.ds(0, limit), pl.ds(v_at + g * GROUP, GROUP)]) * (1.0 / total)
        out = mixed[:DENSE]
        for h in range(1, SIDE):
            out = jnp.where(places == h, mixed[h * DENSE : (h + 1) * DENSE], out)
        o_ref[pl.ds(q0, DENSE), pl.ds(g * GROUP, GROUP)] = out.astype(BF)


def front_kernel(mesh, chunks, count, sizes, *refs):
    shards, rest = refs[:count], refs[count:]
    tok_in, mem_in, own_seg, far_seg = rest[:4]
    rest = rest[4:]
    fulls, rest = rest[:count], rest[count:]
    outs, rest = rest[:8], rest[8:]
    (qkv, o1, r1, cq, ckv, cols, ranges, par, tok, mem, w_qkv, w_out, w_cq, w_ckv, small, seg_col) = rest[:16]
    send, recv, own, load, load_in, store = rest[16:]
    place = Place(mesh)
    place.greet()
    gather = Gather(place, chunks, shards, fulls, send, recv, own)
    taken = [
        pltpu.make_async_copy(tok_in, tok, load_in.at[0]),
        pltpu.make_async_copy(mem_in, mem, load_in.at[1]),
    ]
    length, width = tok.shape
    held = {0: w_qkv, 1: w_out, 2: w_cq, 3: w_ckv, count - 1: small}
    loads = {}

    def fetch(k):
        which, row, rows, col, cols, split, _ = chunks[k]
        if which not in held:
            return
        loads[k] = pltpu.make_async_copy(
            fulls[which].at[..., pl.ds(col, cols)], held[which].at[..., pl.ds(col, cols)], load.at[k]
        )
        loads[k].start()

    def chunk_of(which, col):
        return [k for k, c in enumerate(chunks) if c[0] == which and c[3] == col][0]

    def weight(ref, col, cols):
        flat = ref.shape[:-2]
        return ref[..., pl.ds(col, cols)].reshape(math.prod(flat) * ref.shape[-2], cols)

    def give(at, ref):
        copy = pltpu.make_async_copy(ref, outs[at], store.at[at])
        copy.start()
        given.append(copy)

    given = []

    def project(t):
        def run():
            loads[chunk_of(0, t * 512)].wait()
            if t == 0:
                taken[0].wait()
            qkv[:, pl.ds(t * 512, 512)] = dot(tok[...], weight(w_qkv, t * 512, 512)).astype(BF)
            if t == 2:
                give(0, qkv)

        return run

    def columns():
        own_row = own_seg[...].astype(F32)
        segment_ranges(own_row, far_seg[...].astype(F32), ranges)
        cols[...] = ranges[...].astype(F32).T.astype(jnp.int32)
        give(6, ranges)
        give(5, cols)
        seg_col[...] = jnp.broadcast_to(own_row, (8, length)).T

    def attend_self(b):
        def run():
            q0, limit = b * DENSE, (b + 1) * DENSE
            same = seg_col[pl.ds(q0, DENSE), 0:1] == own_seg[:, pl.ds(0, limit)].astype(F32)
            key = lax.broadcasted_iota(jnp.int32, (DENSE, limit), 1)
            query = q0 + lax.broadcasted_iota(jnp.int32, (DENSE, limit), 0)
            dense_attend(qkv, 0, q0, qkv, width, 2 * width, limit, same & (key <= query), o1)
            if limit == length:
                give(1, o1)

        return run

    def pairs(t):
        def run():
            loads[chunk_of(3, t * 512)].wait()
            if t == 0:
                taken[1].wait()
            ckv[:, pl.ds(t * 512, 512)] = dot(mem[...], weight(w_ckv, t * 512, 512)).astype(BF)
            if t == 1:
                give(4, ckv)

        return run

    def params():
        loads[chunk_of(count - 1, 0)].wait()
        each = sizes[count - 1]
        flat = small[...].reshape(math.prod(small.shape[:-2]), small.shape[-2], small.shape[-1])
        par[...] = jnp.concatenate([flat[w, :, :each].astype(F32) for w in range(flat.shape[0])], axis=1)
        give(7, par)

    def hidden(t):
        def run():
            if t == 0:
                loads[chunk_of(1, 0)].wait()
                loads[chunk_of(2, 0)].wait()
            rows = pl.ds(t * 256, 256)
            resid = tok[rows, :].astype(F32) * par[6:7, :] + dot(o1[rows, :], weight(w_out, 0, width))
            r1[rows, :] = resid
            normal, _ = norm_parts(resid)
            low = (normal * par[0:1, :] + par[3:4, :]).astype(BF)
            cq[rows, :] = dot(low, weight(w_cq, 0, width)).astype(BF)
            if (t + 1) * 256 == length:
                give(2, r1)
                give(3, cq)

        return run

    def take():
        for copy in taken:
            copy.start()

    work = [((), 0.1, take), ((), 0.5, columns)]
    work += [((chunk_of(0, t * 512),), 0.8, project(t)) for t in range(3)]
    work += [((), 0.2 + 0.15 * b, attend_self(b)) for b in range(length // DENSE)]
    work += [((chunk_of(count - 1, 0),), 0.2, params)]
    work += [((chunk_of(1, 0), chunk_of(2, 0)), 0.9, hidden(t)) for t in range(length // 256)]
    work += [((chunk_of(3, t * 512),), 0.8, pairs(t)) for t in range(2)]

    def advance(k, s):
        whole = gather.advance(k, s)
        if whole:
            fetch(k)
        return whole

    run_plan(gather.events(), advance, work)
    gather.finish()
    for copy in given:
        copy.wait()


def front(mesh, shards, tokens, memory, own_seg, far_seg, rows, collective):
    early, late = stage_orders(mesh)
    digits = tuple(size for _, size in wide_parts(mesh))
    small_order = [s for s in early if not isinstance(s, str)]
    count = len(shards)
    length, width = tokens.shape
    chunks = []
    for which in [0, count - 1] + list(range(1, count - 1)):
        high, cols = shards[which].shape
        if cols < 512:
            chunks.append((which, 0, high, 0, cols, False, small_order))
            continue
        cut = max(1, high // 64)
        for r in range(cut):
            for c in range(cols // 512):
                order = late if len(chunks) % 8 in LATE_CHUNKS else early
                chunks.append((which, r * (high // cut), high // cut, c * 512, 512, True, order))
    copies = sum(stage_copies(mesh, c[6]) for c in chunks)
    fulls = tuple(jax.ShapeDtypeStruct(digits + s.shape, s.dtype) for s in shards)
    made = (
        shaped(length, 3 * width), shaped(length, width), shaped(length, width, dtype=F32), shaped(length, width),
        shaped(length, 2 * width), shaped(length, 8, dtype=jnp.int32), shaped(8, length, dtype=jnp.int32),
        shaped(16, width, dtype=F32),
    )
    vm = pltpu.VMEM
    kept = [0, 1, 2, 3, count - 1]
    results = pl.pallas_call(
        functools.partial(front_kernel, mesh, chunks, count, [s.shape[0] for s in shards[:-1]] + [rows]),
        out_shape=fulls + made,
        in_specs=[pl.BlockSpec(memory_space=pl.ANY)] * (count + 2) + [pl.BlockSpec(memory_space=vm)] * 2,
        out_specs=tuple(pl.BlockSpec(memory_space=pl.ANY) for _ in fulls + made),
        scratch_shapes=[vm(m.shape, m.dtype) for m in made]
        + [vm(tokens.shape, BF), vm(memory.shape, BF)]
        + [vm(fulls[k].shape, BF) for k in kept]
        + [
            vm((length, 8), F32),
            pltpu.SemaphoreType.DMA((copies,)),
            pltpu.SemaphoreType.DMA((copies,)),
            pltpu.SemaphoreType.DMA((len(chunks),)),
            pltpu.SemaphoreType.DMA((len(chunks),)),
            pltpu.SemaphoreType.DMA((2,)),
            pltpu.SemaphoreType.DMA((len(made),)),
        ],
        compiler_params=pltpu.CompilerParams(
            collective_id=collective, has_side_effects=True, vmem_limit_bytes=VMEM_BYTES
        ),
        name="front",
    )(*shards, tokens, memory, own_seg.reshape(1, length), far_seg.reshape(1, length))
    return [full.reshape((-1, full.shape[-1])) for full in results[:count]], results[count:]


LATE_CHUNKS = (1, 4, 6)


def layer(mesh, tokens, memory, segments, cotangent, weights, made, rows):
    w_qkv, w_out, w_cq, w_ckv, w_co, w_in, w_down, _ = weights
    qkv, o1, r1, cq, ckv, cols, ranges, par = made
    arrays = (cq, ckv, cols, ranges, par, r1, w_co, w_in, w_down, cotangent)
    out, dr2, dcq, dckv, g_in, g_down, g_co, vec_two = middle(ranges, arrays)
    inputs = (dr2, dcq, w_cq, r1, par, vec_two, tokens, w_out, o1, memory, dckv, qkv, w_ckv, w_qkv)
    return out, back(mesh, (g_in, g_down, g_co), inputs, segments, rows, 2)


PACE_US, LAG_US, LAST_LAG_US = 1.3, 6.0, 3.0
PATTERN = "yxyxyxyxyxyxyxyxy"
FAR_COLS, FAR_PARTS = 512, 4


def reduce_orders(mesh):
    digits = list(range(len(wide_parts(mesh))))[::-1]
    return {
        "x": ["core", "x"] + digits,
        "y": ["core", digits[0], "x"] + digits[1:],
        "z": ["core"] + digits[::-1] + ["x"],
        "n": ["core"] + digits + ["sum x"],
    }


def stage_peers(mesh, stage):
    sizes = [size for _, size in wide_parts(mesh)]
    if stage == "all":
        return [d for d in itertools.product(*[range(size) for size in sizes]) if any(d)]
    return [tuple(d if j == stage else 0 for j in range(len(sizes))) for d in range(1, sizes[stage])]


class Chunk:
    def __init__(self, mesh, which, sub, rows, col, cols, order, split, held):
        self.which, self.sub, self.rows, self.col, self.cols = which, sub, rows, col, cols
        self.order, self.split, self.held = order, split, held
        sizes = [size for _, size in wide_parts(mesh)]
        self.received = []
        self.copies = 2 if split else 0
        lanes = cols // 2 if split else cols
        self.shape = tuple(sizes) + (rows, lanes)
        for stage in order:
            if isinstance(stage, str) and stage != "all":
                lanes = lanes // 2 if stage == "x" and split else lanes
                count = 1
            else:
                sizes = [1 if stage in ("all", j) else size for j, size in enumerate(sizes)]
                count = len(stage_peers(mesh, stage))
            self.received.append([tuple(sizes) + (rows, lanes)] * count)
            self.copies += count


class Reduce:
    def __init__(self, mesh, place, chunks, grads, held, received, sums, send, recv, own):
        self.mesh, self.place, self.chunks, self.grads, self.sums = mesh, place, chunks, grads, sums
        self.send, self.recv, self.used, self.sent = send, recv, 0, []
        held, received = list(held), list(received)
        self.states = []
        for k, chunk in enumerate(chunks):
            half = chunk.cols // 2 if chunk.split else chunk.cols
            source = grads[chunk.which]
            near = chunk.col + place.core * half if chunk.split else chunk.col
            far = chunk.col + (1 - place.core) * half if chunk.split else chunk.col
            state = {"copies": [], "bufs": [], "mine": None}
            if chunk.held:
                cur = (held.pop(0), 0, half, None)
                mine = pltpu.make_async_copy(self.view((source, near, half, chunk.sub)), cur[0], own.at[k])
                mine.start()
                state["mine"] = mine
            else:
                cur = (source, near, half, chunk.sub)
            state["cur"], state["other"] = cur, (source, far, half, chunk.sub)
            state["pool"] = [[received.pop(0) for _ in shapes] for shapes in chunk.received]
            self.states.append(state)

    def view(self, cur, digits=None, lane=None, size=None):
        ref, off, lanes, sub = cur
        spot = [slice(None)] * len(self.place.parts)
        for j, index in (digits or {}).items():
            spot[j] = pl.ds(index, 1)
        if sub is not None:
            spot.append(sub)
        start = off if lane is None else off + lane
        if not isinstance(start, int):
            start = pl.multiple_of(start, 128)
        return ref.at[tuple(spot) + (slice(None), pl.ds(start, size or lanes))]

    def ship(self, src, target, peer):
        at = self.used
        self.used += 1
        copy = pltpu.make_async_remote_copy(
            src_ref=src, dst_ref=target, send_sem=self.send.at[at], recv_sem=self.recv.at[at],
            device_id=peer, device_id_type=pl.DeviceIdType.MESH,
        )
        copy.start()
        self.sent.append(copy)
        return copy

    def spots(self, stage, offsets):
        return {
            j: self.place.flip(self.place.digits[j], d, self.place.parts[j][1])
            for j, d in enumerate(offsets)
            if stage in ("all", j)
        }

    def begin(self, k, s):
        chunk, state, place = self.chunks[k], self.states[k], self.place
        stage, cur = chunk.order[s], state["cur"]
        bufs = state["pool"][s]
        if stage == "core":
            state["copies"] = [self.ship(self.view(state["other"]), bufs[0], place.core_peer())]
        elif stage == "sum x":
            state["copies"] = [self.ship(self.view(cur), bufs[0], place.x_peer())]
        elif stage == "x":
            src = self.view(cur)
            if chunk.split:
                half = cur[2] // 2
                src = self.view(cur, lane=(1 - place.x) * half, size=half)
            state["copies"] = [self.ship(src, bufs[0], place.x_peer())]
        else:
            for buf, offsets in zip(bufs, stage_peers(self.mesh, stage)):
                src = self.view(cur, self.spots(stage, offsets))
                state["copies"].append(self.ship(src, buf, place.wide_peer(offsets)))

    def end(self, k, s):
        chunk, state, place = self.chunks[k], self.states[k], self.place
        stage, cur, bufs = chunk.order[s], state["cur"], state["pool"][s]
        for copy in state["copies"]:
            copy.wait_recv()
        state["copies"] = []
        if stage == "core":
            if state["mine"] is not None:
                state["mine"].wait()
            mine = self.view(cur)
        elif stage == "sum x":
            mine = self.view(cur)
        elif stage == "x":
            half = cur[2] // 2 if chunk.split else cur[2]
            mine = self.view(cur, lane=place.x * half, size=half) if chunk.split else self.view(cur)
        else:
            mine = self.view(cur, self.spots(stage, (0,) * len(place.parts)))
        if len(bufs) == 1:
            bufs[0][...] = mine[...] + bufs[0][...]
        else:
            value = mine[...].astype(F32)
            for buf in bufs:
                value = value + buf[...].astype(F32)
            bufs[0][...] = value.astype(BF)
        state["cur"] = (bufs[0], 0, bufs[0].shape[-1], None)

    def out_view(self, k, size):
        chunk, start = self.chunks[k], self.chunks[k].col
        if size < chunk.cols:
            start = start + self.place.core * (chunk.cols // 2)
        if size < chunk.cols // 2:
            start = start + self.place.x * (chunk.cols // 4)
        if not isinstance(start, int):
            start = pl.multiple_of(start, 128)
        return self.sums[chunk.which].at[pl.ds((chunk.sub or 0) * chunk.rows, chunk.rows), pl.ds(start, size)]

    def advance(self, k, s):
        chunk, state = self.chunks[k], self.states[k]
        stages = len(chunk.order)
        if 0 < s <= stages:
            self.end(k, s - 1)
        if s < stages:
            self.begin(k, s)
            return
        if s > stages:
            for copy in state["copies"]:
                copy.wait_recv()
            state["copies"] = []
        summed = "sum x" in chunk.order
        if s == stages:
            parts = 1 if not chunk.split else 2 if summed else 4
            view = self.out_view(k, chunk.cols // parts)
            view[...] = state["cur"][0][...].reshape(view.shape)
            if chunk.split:
                peer = self.place.core_peer() if summed else self.place.x_peer()
                state["copies"] = [self.ship(view, view, peer)]
        elif s == stages + 1 and chunk.split and not summed:
            view = self.out_view(k, chunk.cols // 2)
            state["copies"] = [self.ship(view, view, self.place.core_peer())]

    def finish(self):
        for copy in self.sent:
            copy.wait_send()


def run_back(reduce, chunks, work):
    ready, now = {}, 0.0
    for us, _, gives in work:
        now += us
        for k in gives:
            ready[k] = now
    events, free = [], 0.0
    for k, chunk in enumerate(chunks):
        begin = max(free, ready.get(k, 0.0))
        free = begin + (PACE_US if chunk.split else 0.0)
        lag = LAST_LAG_US if k >= len(chunks) - 3 else LAG_US
        events += [(begin + s * lag, k, s) for s in range(len(chunk.order) + 3)]
    made, now, work = {k for k in range(len(chunks)) if k not in ready}, 0.0, list(work)
    for time, k, s in sorted(events):
        while work and (now < time or k not in made):
            us, run, gives = work.pop(0)
            run()
            made |= set(gives)
            now += us
        now = max(now, time)
        reduce.advance(k, s)
    for _, run, _ in work:
        run()


def back_kernel(mesh, chunks, count, *refs):
    far, rest = refs[:3], refs[3:]
    inputs, rest = rest[:15], rest[15:]
    sums, rest = rest[:count], rest[count:]
    gt_out, gm_out, rest = rest[0], rest[1], rest[2:]
    loaded, rest = rest[:14], rest[14:]
    (dk_acc, dv_acc, dqkv, h1, da, do1, g_cross, g_out, g_qkv, vectors, seg_col) = rest[:11]
    rest = rest[11:]
    held, rest = rest[: sum(c.held for c in chunks)], rest[sum(c.held for c in chunks) :]
    received, (send, recv, own, load, store) = rest[:-5], rest[-5:]
    own_seg = inputs[14]
    place = Place(mesh)
    place.greet(True)
    grads = list(far) + [g_cross, g_out, vectors, g_qkv]
    reduce = Reduce(mesh, place, chunks, grads, held, received, sums, send, recv, own)
    loads = [pltpu.make_async_copy(src, dst, load.at[i]) for i, (src, dst) in enumerate(zip(inputs[:14], loaded))]
    waiting = list(range(14))
    (dr2, dq, w_cq, r1, par, vec_two, tok, w_out, o1, mem, dckv, qkv, w_ckv, w_qkv) = loaded
    length, width = tok.shape
    given = []
    vec = [jnp.zeros((1, width), F32) for _ in range(3)]

    def fetch(first, last):
        def run():
            for copy in loads[first:last]:
                copy.start()

        return run

    def need(upto):
        while waiting and waiting[0] <= upto:
            loads[waiting.pop(0)].wait()

    def give(at, ref, out):
        copy = pltpu.make_async_copy(ref, out, store.at[at])
        copy.start()
        given.append(copy)

    def hidden(t):
        def run():
            need(7)
            if t == 0:
                seg_col[...] = jnp.broadcast_to(own_seg[...].astype(F32), (8, length)).T
                dk_acc[...] = jnp.zeros_like(dk_acc)
                dv_acc[...] = jnp.zeros_like(dv_acc)
            rows = pl.ds(t * 256, 256)
            grad = dr2[rows, :] * par[7:8, :] + dot_nt(dq[rows, :], w_cq[...])
            normal, scale = norm_parts(r1[rows, :])
            h1[rows, :] = (normal * par[0:1, :] + par[3:4, :]).astype(BF)
            vec[0] += down_sum(grad * normal)
            vec[1] += down_sum(grad)
            back = norm_back(grad, normal, scale, par[0:1, :])
            vec[2] += down_sum(tok[rows, :].astype(F32) * back)
            dr2[rows, :] = back
            low = back.astype(BF)
            da[rows, :] = low
            do1[rows, :] = dot_nt(low, w_out[...]).astype(BF)
            if (t + 1) * 256 == length:
                every = jnp.concatenate(vec + [vec_two[3:6, :], vec_two[0:3, :], jnp.zeros((7, width), F32)], axis=0)
                wide = mesh.shape["wide"]
                each = width // wide
                for w in range(wide):
                    part = every[:, w * each : (w + 1) * each]
                    part = jnp.concatenate([part, jnp.zeros((16, 128 - each), F32)], axis=1)
                    spot, rest = [], w
                    for low_bit, size in place.parts:
                        spot.append((w >> low_bit) % size)
                    vectors[tuple(spot)] = part.astype(BF)

        return run

    def put(ref, at, cols, value):
        ref[..., pl.ds(at, cols)] = value.astype(BF).reshape(ref.shape[:-1] + (cols,))

    def grad_out():
        need(8)
        put(g_out, 0, width, dot_tn(o1[...], da[...]))

    def grad_cq():
        put(g_cross, 0, width, dot_tn(h1[...], dq[...]))

    def grad_ckv(t):
        def run():
            need(10)
            put(g_cross, (t + 1) * width, width, dot_tn(mem[...], dckv[:, pl.ds(t * width, width)]))

        return run

    def grad_mem(t):
        def run():
            need(12)
            rows = pl.ds(t * 256, 256)
            r1[rows, :] = dot_nt(dckv[rows, :], w_ckv[...])
            if (t + 1) * 256 == length:
                give(0, r1, gm_out)

        return run

    def attend(b, g):
        def run():
            need(11)
            limit = (b + 1) * DENSE
            mine = own_seg[:, b * DENSE : (b + 1) * DENSE].astype(F32)
            same = seg_col[pl.ds(0, limit), 0:1] == jnp.concatenate([mine] * SIDE, axis=1)
            key = lax.broadcasted_iota(jnp.int32, (limit, SIDE * DENSE), 0)
            query = lax.rem(lax.broadcasted_iota(jnp.int32, (limit, SIDE * DENSE), 1), DENSE) + b * DENSE
            shift = jnp.where(same & (key <= query), 0.0, NEGATIVE)
            dense_attend_bwd(qkv, do1, b * DENSE, limit, shift, dqkv, dk_acc, dv_acc, g)

        return run

    def grad_qkv(t):
        def run():
            if t == 1:
                dqkv[:, width : 2 * width] = dk_acc[...].astype(BF)
            if t == 2:
                dqkv[:, 2 * width :] = dv_acc[...].astype(BF)
            put(g_qkv, t * width, width, dot_tn(tok[...], dqkv[:, pl.ds(t * width, width)]))

        return run

    def grad_tok(t):
        def run():
            need(13)
            rows = pl.ds(t * 256, 256)
            dr2[rows, :] = dr2[rows, :] * par[6:7, :] + dot_nt(dqkv[rows, :], w_qkv[...])
            if (t + 1) * 256 == length:
                give(1, dr2, gt_out)

        return run

    def chunks_of(which, col=None):
        return [k for k, c in enumerate(chunks) if c.which == which and col in (None, c.col)]

    parts = length // 256
    work = [(0.1, fetch(0, 8), [])]
    work += [(1.2, hidden(t), chunks_of(5) if t + 1 == parts else []) for t in range(parts)]
    work[2:2] = [(0.1, fetch(8, 14), [])]
    work += [(0.9, grad_out, chunks_of(4)), (0.9, grad_cq, chunks_of(3, 0))]
    work += [(0.9, grad_ckv(t), chunks_of(3, (t + 1) * width)) for t in range(2)]
    work += [(0.25 + 0.25 * b, attend(b, g), []) for b in range(length // DENSE) for g in range(width // GROUP)]
    work += [(1.0, grad_qkv(t), chunks_of(6, t * width)) for t in range(3)]
    work += [(0.4, grad_mem(t), []) for t in range(parts)]
    work += [(0.6, grad_tok(t), []) for t in range(parts)]
    run_back(reduce, chunks, work)
    need(13)
    reduce.finish()
    for copy in given:
        copy.wait()


def dense_attend_bwd(qkv, do_ref, q0, limit, shift, dqkv, dk_acc, dv_acc, g):
    width = do_ref.shape[1]
    factor = HD**-0.5
    rows = lax.broadcasted_iota(jnp.int32, (SIDE * DENSE, GROUP), 0) // DENSE
    heads = lax.broadcasted_iota(jnp.int32, (SIDE * DENSE, GROUP), 1) // HD
    do_mask = jnp.where(rows == heads, 1.0, 0.0).astype(BF)
    q_mask = jnp.where(rows == heads, factor, 0.0).astype(BF)
    places = lax.broadcasted_iota(jnp.int32, (DENSE, GROUP), 1) // HD
    lanes = pl.ds(g * GROUP, GROUP)
    query = jnp.concatenate([qkv[pl.ds(q0, DENSE), lanes]] * SIDE, axis=0) * q_mask
    grad = jnp.concatenate([do_ref[pl.ds(q0, DENSE), lanes]] * SIDE, axis=0) * do_mask
    keys = qkv[pl.ds(0, limit), pl.ds(width + g * GROUP, GROUP)]
    values = qkv[pl.ds(0, limit), pl.ds(2 * width + g * GROUP, GROUP)]
    score = dot_nt(keys, query) + shift
    slopes = dot_nt(values, grad)
    raised = jnp.exp(score - jnp.max(score, axis=0, keepdims=True))
    probs = raised * (1.0 / down_sum(raised))
    delta = (probs * (slopes - down_sum(probs * slopes))).astype(BF)
    dv_acc[pl.ds(0, limit), lanes] += dot(probs.astype(BF), grad)
    dk_acc[pl.ds(0, limit), lanes] += dot(delta, query)
    stacked = dot_tn(delta, keys)
    dq = stacked[:DENSE]
    for h in range(1, SIDE):
        dq = jnp.where(places == h, stacked[h * DENSE : (h + 1) * DENSE], dq)
    dqkv[pl.ds(q0, DENSE), lanes] = (dq * factor).astype(BF)


def back(mesh, far, inputs, own_seg, rows, collective):
    kinds = reduce_orders(mesh)
    digits = tuple(size for _, size in wide_parts(mesh))
    wide = mesh.shape["wide"]
    length, width = inputs[0].shape
    each = width // wide
    views, chunks, sums = [], [], []

    def add(which, sub, high, cols, split, held):
        for j in range(sub or 1):
            unit = FAR_COLS if which == 0 else min(cols, 512)
            for c in range(cols // unit):
                order = kinds[PATTERN[len(chunks) % len(PATTERN)]]
                at = j if sub is not None else None
                chunks.append(Chunk(mesh, which, at, high, c * unit, unit, order, split, held))

    for which, grad in enumerate(far):
        high, cols = grad.shape[0] // wide, grad.shape[1]
        sub = FAR_PARTS if high * wide > width else 1
        views.append(grad.reshape(digits + (sub, high // sub, cols)))
        sums.append(shaped(high, cols))
        add(which, sub, high // sub, cols, True, True)
    for which, cols in ((3, 3 * width), (4, width), (5, 128), (6, 3 * width)):
        high, split = (16, False) if which == 5 else (each, True)
        sums.append(shaped(high, cols))
        add(which, None, high, cols, split, False)
    vm = pltpu.VMEM
    arrays = list(inputs)
    scratch = [vm(a.shape, a.dtype) for a in arrays]
    scratch += [vm((length, width), F32)] * 2 + [vm((length, 3 * width), BF)] + [vm((length, width), BF)] * 3
    scratch += [vm(digits + (each, cols), BF) for cols in (3 * width, width, 3 * width)]
    scratch += [vm(digits + (16, 128), BF), vm((length, 8), F32)]
    scratch += [vm(c.shape, BF) for c in chunks if c.held]
    scratch += [vm(shape, BF) for c in chunks for shapes in c.received for shape in shapes]
    copies = sum(c.copies for c in chunks)
    scratch += [pltpu.SemaphoreType.DMA((n,)) for n in (copies, copies, len(chunks), len(arrays), 2)]
    large = shaped(length, width, dtype=F32)
    return pl.pallas_call(
        functools.partial(back_kernel, mesh, chunks, len(sums)),
        out_shape=tuple(sums) + (large, large),
        in_specs=[pl.BlockSpec(memory_space=pl.ANY)] * (len(far) + len(arrays)) + [pl.BlockSpec(memory_space=vm)],
        out_specs=tuple(pl.BlockSpec(memory_space=vm) for _ in sums) + (pl.BlockSpec(memory_space=pl.ANY),) * 2,
        scratch_shapes=scratch,
        compiler_params=pltpu.CompilerParams(
            collective_id=collective, has_side_effects=True, vmem_limit_bytes=VMEM_BYTES
        ),
        name="back",
    )(*views, *arrays, own_seg.reshape(1, length))


def finish_kernel(count, rows, *refs):
    s_in, s_down, s_co, s_cross, s_out, s_vec, s_qkv = refs[:count]
    large, outs, held, sems = refs[count : count + 2], refs[count + 2 : -3], refs[-3:-1], refs[-1]
    moves = [pltpu.make_async_copy(large[i], held[i], sems.at[i]) for i in range(2)]
    for move in moves:
        move.start()
    for i in range(2):
        moves[i].wait()
        moves[i] = pltpu.make_async_copy(held[i], outs[i], sems.at[i])
        moves[i].start()
    width = s_out.shape[1]
    plain = (s_qkv[...], s_out[...], s_cross[:, :width], s_cross[:, width:], s_co[...], s_in[...], s_down[...])
    for value, out in zip(plain, outs[2:]):
        out[...] = value.astype(F32)
    vectors = s_vec[...].astype(F32)
    for at, out in enumerate(outs[2 + len(plain) :]):
        for j in range(3):
            out[j : j + 1, :] = vectors[3 * j + at : 3 * j + at + 1, :rows]
    for move in moves:
        move.wait()


def finish(sums, large, shapes, rows):
    vmem = pl.BlockSpec(memory_space=pltpu.VMEM)
    anywhere = pl.BlockSpec(memory_space=pl.ANY)
    outs = [shaped(*a.shape, dtype=F32) for a in large] + [shaped(*s, dtype=F32) for s in shapes]
    return pl.pallas_call(
        functools.partial(finish_kernel, len(sums), rows),
        out_shape=tuple(outs),
        in_specs=[vmem] * len(sums) + [anywhere] * 2,
        out_specs=(anywhere,) * 2 + (vmem,) * len(shapes),
        scratch_shapes=[pltpu.VMEM(a.shape, F32) for a in large] + [pltpu.SemaphoreType.DMA((2,))],
        compiler_params=pltpu.CompilerParams(vmem_limit_bytes=VMEM_BYTES),
        name="finish",
    )(*sums, *large)


def body(
    mesh,
    tokens,
    memory,
    target_segments,
    memory_segments,
    self_qkv,
    self_out,
    cross_q,
    cross_kv,
    cross_out,
    ffn_in,
    ffn_out,
    norm_gain,
    norm_bias,
    omega,
    cotangent,
):
    wide = mesh.shape["wide"]
    rows = self_qkv.shape[0]
    width = rows * wide
    small = jnp.concatenate([norm_gain, norm_bias, omega], axis=1).T
    small = jnp.pad(small, ((0, 7), (0, 128 - rows)))
    weights, made = front(
        mesh, (self_qkv, self_out, cross_q, cross_kv, cross_out, ffn_in, ffn_out, small),
        tokens, memory, target_segments, memory_segments, rows, 1,
    )
    output, (*sums, grad_tokens, grad_memory) = layer(
        mesh, tokens, memory, target_segments, cotangent, weights, made, rows
    )
    shapes = ((rows, 3 * width), (rows, width), (rows, width), (rows, 2 * width), (rows, width))
    shapes += (ffn_in.shape, ffn_out.shape, (3, rows), (3, rows), (3, rows))
    grad_tokens, grad_memory, *summed = finish(sums, (grad_tokens, grad_memory), shapes, rows)
    summed = tuple(summed[:7]) + tuple(vector.T for vector in summed[7:])
    return (output, grad_tokens, grad_memory) + summed


def solution(mesh):
    in_specs = (
        P(("narrow", "wide"), None),
        P(("narrow", "wide"), None),
        P(("narrow", "wide")),
        P(("narrow", "wide")),
        P("wide", None),
        P("wide", None),
        P("wide", None),
        P("wide", None),
        P("wide", None),
        P("wide", None),
        P("wide", None),
        P("wide", None),
        P("wide", None),
        P("wide", None),
        P(("narrow", "wide"), None),
    )
    out_specs = (
        P(("narrow", "wide"), None),
        P(("narrow", "wide"), None),
        P(("narrow", "wide"), None),
        P("wide", None),
        P("wide", None),
        P("wide", None),
        P("wide", None),
        P("wide", None),
        P("wide", None),
        P("wide", None),
        P("wide", None),
        P("wide", None),
        P("wide", None),
    )
    return jax.shard_map(functools.partial(body, mesh), mesh=mesh, in_specs=in_specs, out_specs=out_specs, check_vma=False)
```
